32 devices in a mesh: seq: 8 (over z, y), head: 4 (over x, core).
Axes of the slice: x: 2, y: 2, z: 4, core: 2. Of those that a mesh axis runs over, the one named last changes fastest.
Arguments:
- hidden_in: bfloat16 [6144, 2048], P('seq'), may hold values from -6 to 6
- lengths: int32 [3], replicated, may hold values from 1 to 6016, as said below
- attn_gain: float32 [2048], replicated, may hold values from 0.5 to 1.5
- w_query: bfloat16 [2048, 2048], P(None, 'head'), may hold values from -0.125 to 0.125
- w_key: bfloat16 [2048, 2048], P(None, 'head'), may hold values from -0.125 to 0.125
- w_value: bfloat16 [2048, 4096], P(None, 'head'), may hold values from -0.125 to 0.125
- w_gate: bfloat16 [2048, 4096], P(None, 'head'), may hold values from -0.125 to 0.125
- w_alpha: bfloat16 [2048, 16], P(None, 'head'), may hold values from -0.125 to 0.125
- w_beta: bfloat16 [2048, 16], P(None, 'head'), may hold values from -0.125 to 0.125
- conv_query: float32 [4, 2048], P(None, 'head'), may hold values from -3 to 3
- conv_key: float32 [4, 2048], P(None, 'head'), may hold values from -3 to 3
- conv_value: float32 [4, 4096], P(None, 'head'), may hold values from -3 to 3
- decay_log: float32 [16], replicated, may hold values from -3 to 2.7
- decay_bias: float32 [16], replicated, may hold values from -9 to -3
- out_gain: float32 [256], replicated, may hold values from 0.5 to 1.5
- w_out: bfloat16 [4096, 2048], P('head'), may hold values from -0.1875 to 0.1875
- ffn_gain: float32 [2048], replicated, may hold values from 0.5 to 1.5
- w_ffn_gate: bfloat16 [2048, 5504], P(None, 'head'), may hold values from -0.125 to 0.125
- w_ffn_up: bfloat16 [2048, 5504], P(None, 'head'), may hold values from -0.125 to 0.125
- w_ffn_down: bfloat16 [5504, 2048], P('head'), may hold values from -0.15625 to 0.15625
- grad_out: bfloat16 [6144, 2048], P('seq', 'head'), may hold values from -6 to 6
Outputs:
- hidden_out: bfloat16 [6144, 2048], P('seq', 'head')
- grad_in: float32 [6144, 2048], P('seq', 'head')
- grad_attn_gain: float32 [2048], P('seq')
- grad_w_query: float32 [2048, 2048], P('seq', 'head')
- grad_w_key: float32 [2048, 2048], P('seq', 'head')
- grad_w_value: float32 [2048, 4096], P('seq', 'head')
- grad_w_gate: float32 [2048, 4096], P('seq', 'head')
- grad_w_alpha: float32 [2048, 16], P('seq', 'head')
- grad_w_beta: float32 [2048, 16], P('seq', 'head')
- grad_conv_query: float32 [4, 2048], P(None, ('head', 'seq'))
- grad_conv_key: float32 [4, 2048], P(None, ('head', 'seq'))
- grad_conv_value: float32 [4, 4096], P(None, ('head', 'seq'))
- grad_decay_log: float32 [16], replicated
- grad_decay_bias: float32 [16], replicated
- grad_out_gain: float32 [256], replicated
- grad_w_out: float32 [4096, 2048], P('head', 'seq')
- grad_ffn_gain: float32 [2048], P('seq')
- grad_w_ffn_gate: float32 [2048, 5504], P('seq', 'head')
- grad_w_ffn_up: float32 [2048, 5504], P('seq', 'head')
- grad_w_ffn_down: float32 [5504, 2048], P('head', 'seq')
The draws below stay inside these ranges and needn't reach their ends.
Inputs may be any that keep to these rules, and one draw needn't show every extreme that they name: `lengths`: three sequences in order; each is padded to a multiple of 64 positions, the padded sequences fill all 6144 positions, and the first and the last padded sequence each take fewer than 768 positions.
All inputs are finite; a program needn't handle non-finite values.
Results may differ from the reference program's by a relative error of at most 0.025.
Values may be sent and summed in bfloat16 or wider, within the bound.
A program may use at most 320 MiB of HBM per device.

```python
import jax
import jax.numpy as jnp
from jax import lax

D = 2048
H = 16
DK = 128
DV = 256
FF = 5504
TOK_DEV = 768
GROUP = 64
CONV = 4
TOKENS = 6144


def draw_lengths(key, part):
    key = jax.random.fold_in(key, 7)
    first_key, final_key, trim_key = jax.random.split(key, 3)
    first = GROUP * jax.random.randint(first_key, (), 1, TOK_DEV // GROUP)
    final = GROUP * jax.random.randint(final_key, (), 1, TOK_DEV // GROUP)
    padded = jnp.stack([first, TOKENS - first - final, final])
    trims = jax.random.randint(trim_key, (3,), 0, GROUP)
    return (padded - trims).astype(jnp.int32)


def spiked(values, rng, source, target, shards_of, factor):
    owner, partner = [(jnp.arange(values.shape[dim]) // (values.shape[dim] // shards_of)).reshape([-1 if axis == dim else 1 for axis in range(values.ndim)]) for dim in (source, target)]
    chosen = jax.random.permutation(rng, shards_of)[partner]
    strong = (owner == chosen) | (owner == (partner + shards_of // 2) % shards_of)
    return jnp.where(strong, factor * values, values)


def level_of(stream_key, shape, cuts, low, high):
    gain = 1.0
    for dim, shards_of in cuts:
        steps = jax.random.uniform(jax.random.fold_in(jax.random.fold_in(stream_key, 6), dim), (shards_of,), jnp.float32, low / len(cuts), high / len(cuts))
        gain = gain * jnp.repeat(jnp.exp(steps), shape[dim] // shards_of).reshape((-1,) + (1,) * (len(shape) - 1 - dim))
    return gain


def normal_values(key, extent, spread, most, cuts=(), kind=jnp.bfloat16):
    entries = spread * jax.random.normal(key, extent, jnp.float32)
    if cuts:
        entries = entries * level_of(key, extent, cuts, -0.22, 0.18)
    return jnp.clip(entries, -most, most).astype(kind)


def bell_draw_with(key, shape, width, limit, cuts, heavy, held_as=jnp.bfloat16):
    drawn = width * jax.random.normal(key, shape, jnp.float32)
    if cuts:
        drawn = drawn * level_of(key, shape, cuts, -0.22, 0.18)
    return jnp.clip(spiked(drawn, jax.random.fold_in(key, 3), *heavy), -limit, limit).astype(held_as)


def setup_inputs(seed: int = 0) -> dict:
    keys = jax.random.split(jax.random.key(seed), 22)
    return {
        "hidden_in": bell_draw_with(keys[0], (TOKENS, D), 1.0, 6.0, ((0, 8),), (0, 1, 8, 2.0)),
        "lengths": draw_lengths(jax.random.fold_in(keys[21], 71), 0),
        "attn_gain": jnp.clip(1.0 + 0.1 * jax.random.normal(keys[2], (D,), jnp.float32), 0.5, 1.5),
        "w_query": normal_values(keys[3], (D, H * DK), D ** -0.5, 0.125, ((1, 4),)),
        "w_key": normal_values(keys[4], (D, H * DK), D ** -0.5, 0.125, ((1, 4),)),
        "w_value": normal_values(keys[5], (D, H * DV), D ** -0.5, 0.125, ((1, 4),)),
        "w_gate": normal_values(keys[6], (D, H * DV), D ** -0.5, 0.125, ((1, 4),)),
        "w_alpha": normal_values(keys[7], (D, H), D ** -0.5, 0.125, ((1, 4),)),
        "w_beta": normal_values(keys[8], (D, H), D ** -0.5, 0.125, ((1, 4),)),
        "conv_query": normal_values(keys[9], (CONV, H * DK), CONV ** -0.5, 3.0, ((1, 4),), jnp.float32),
        "conv_key": normal_values(keys[10], (CONV, H * DK), CONV ** -0.5, 3.0, ((1, 4),), jnp.float32),
        "conv_value": normal_values(keys[11], (CONV, H * DV), CONV ** -0.5, 3.0, ((1, 4),), jnp.float32),
        "decay_log": jnp.clip(jax.random.uniform(keys[12], (H,), jnp.float32, -3.0, 2.7), -3.0, 2.7),
        "decay_bias": jnp.clip(jax.random.uniform(keys[13], (H,), jnp.float32, -9.0, -3.0), -9.0, -3.0),
        "out_gain": jnp.clip(1.0 + 0.1 * jax.random.normal(keys[14], (DV,), jnp.float32), 0.5, 1.5),
        "w_out": normal_values(keys[15], (H * DV, D), (H * DV // 4) ** -0.5, 0.1875, ((0, 4),)),
        "ffn_gain": jnp.clip(1.0 + 0.1 * jax.random.normal(keys[16], (D,), jnp.float32), 0.5, 1.5),
        "w_ffn_gate": normal_values(keys[17], (D, FF), D ** -0.5, 0.125, ((1, 4),)),
        "w_ffn_up": normal_values(keys[18], (D, FF), D ** -0.5, 0.125, ((1, 4),)),
        "w_ffn_down": normal_values(keys[19], (FF, D), (FF // 4) ** -0.5, 0.15625, ((0, 4),)),
        "grad_out": bell_draw_with(keys[20], (TOKENS, D), 1.0, 6.0, ((0, 8), (1, 4)), (0, 1, 8, 2.0)),
    }


highest = lax.Precision.HIGHEST
epsilon_norm = 1e-06
epsilon_gate = 1e-05

@jax.custom_vjp
def low(v):
    return lax.optimization_barrier(v.astype(jnp.bfloat16)).astype(jnp.float32)

@jax.custom_vjp
def low_back(v):
    return v

def low_keep(v):
    return (low(v), None)

def low_pass(kept, grad):
    return (grad,)

def back_keep(v):
    return (v, None)

def back_low(kept, grad):
    return (low(grad),)
low.defvjp(low_keep, low_pass)
low_back.defvjp(back_keep, back_low)

def full_dot(left, right):
    return jnp.dot(left, right, precision=highest, preferred_element_type=jnp.float32)

def batch_dot(spec, left, right):
    return jnp.einsum(spec, left, right, precision=highest, preferred_element_type=jnp.float32)

def layout(lengths, positions):
    padded = (lengths + (GROUP - 1)) // GROUP * GROUP
    seq_ends = jnp.cumsum(padded)
    begins = seq_ends - padded
    offset = positions[:, None] - begins[None, :]
    inside = (offset >= 0) & (positions[:, None] < seq_ends[None, :])
    valid_mask = jnp.any(inside & (offset < lengths[None, :]), axis=1).astype(jnp.float32)
    starts = jnp.any(offset == 0, axis=1).astype(jnp.float32)
    return (valid_mask, starts)

def delayed(values, shift_by):
    if shift_by == 0:
        return values
    return jnp.concatenate([jnp.zeros((shift_by,), values.dtype), values[:-shift_by]])

def convolve(extended, weight, starts):
    token_rows = starts.shape[0]
    running = extended[CONV - 1:] * weight[0]
    alive = jnp.ones_like(starts)
    for tap_index in range(1, CONV):
        alive = alive * (1.0 - delayed(starts, tap_index - 1))
        begin_row = CONV - 1 - tap_index
        running = running + extended[begin_row:begin_row + token_rows] * weight[tap_index] * alive[:, None]
    return jax.nn.silu(running)

def unit_rows(values):
    return values * lax.rsqrt(lax.optimization_barrier(jnp.sum(values * values, axis=-1, keepdims=True)) + epsilon_norm)

def make_features(starts, valid_mask, head_count):

    def features(ext_query, ext_key, ext_value, conv_query, conv_key, conv_value, alpha_pre, beta_pre, decay_log, decay_bias):
        token_rows = starts.shape[0]
        query_act = convolve(ext_query, conv_query, starts).reshape(token_rows, head_count, DK)
        key_act = convolve(ext_key, conv_key, starts).reshape(token_rows, head_count, DK)
        value_act = convolve(ext_value, conv_value, starts).reshape(token_rows, head_count, DV)
        query = unit_rows(query_act) * DK ** (-0.5)
        key_rows = unit_rows(key_act) * valid_mask[:, None, None]
        value = value_act * valid_mask[:, None, None]
        decay = -jnp.exp(decay_log) * jax.nn.softplus(alpha_pre + decay_bias) * valid_mask[:, None]
        beta = jax.nn.sigmoid(beta_pre)
        return (query, key_rows, value, decay, beta)
    return features

def unit_inverse(strict):
    group_len = strict.shape[-1]
    identity_c = jnp.eye(group_len, dtype=jnp.float32)
    result = identity_c - strict
    power_term = batch_dot('...ij,...jk->...ik', strict, strict)
    degree = 2
    while degree < group_len:
        result = batch_dot('...ij,...jk->...ik', result, identity_c + power_term)
        power_term = batch_dot('...ij,...jk->...ik', power_term, power_term)
        degree = degree * 2
    return result

def prepare(query, key_rows, value, decay, beta):
    group_len = query.shape[-2]
    cumulative = jnp.cumsum(decay, axis=-1)
    lower_mask = jnp.tril(jnp.ones((group_len, group_len), dtype=bool))
    strict_mask = jnp.tril(jnp.ones((group_len, group_len), dtype=bool), -1)
    log_gap = cumulative[..., :, None] - cumulative[..., None, :]
    decay_ratio = jnp.where(lower_mask, jnp.exp(jnp.where(lower_mask, log_gap, 0.0)), 0.0)
    similar = batch_dot('...ik,...jk->...ij', key_rows, key_rows)
    coupling = jnp.where(strict_mask, beta[..., :, None] * decay_ratio * similar, 0.0)
    inverse = unit_inverse(coupling)
    growth = jnp.exp(cumulative)[..., None]
    weights_w = batch_dot('...ij,...jk->...ik', inverse, beta[..., None] * growth * key_rows)
    values_u = batch_dot('...ij,...jk->...ik', inverse, beta[..., None] * value)
    mixing = decay_ratio * batch_dot('...ik,...jk->...ij', query, key_rows)
    closing = cumulative[..., -1:]
    key_decayed = jnp.exp(closing - cumulative)[..., None] * key_rows
    return (growth * query, mixing, weights_w, values_u, key_decayed, jnp.exp(closing[..., 0]))

def group_output(state, parts):
    query_d, mixing, weights_w, values_u, key_decayed, fading = parts
    fresh = values_u - batch_dot('...ck,...kv->...cv', weights_w, state)
    block_out = batch_dot('...ck,...kv->...cv', query_d, state) + batch_dot('...cd,...dv->...cv', mixing, fresh)
    after = fading[..., None, None] * state + batch_dot('...ck,...cv->...kv', key_decayed, fresh)
    return (block_out, after)

def to_blocks(values, group_count):
    shaped = values.reshape((group_count, values.shape[0] // group_count) + values.shape[1:])
    return jnp.swapaxes(shaped, 1, 2)

def from_blocks(blocks):
    merged = jnp.swapaxes(blocks, 1, 2)
    return merged.reshape((merged.shape[0] * merged.shape[1],) + merged.shape[2:])

def delta_rule(query, key_rows, value, decay, beta, keep_flags):
    group_count = query.shape[0] // GROUP

    def advance(state, block):
        query_b, key_b, value_b, decay_b, beta_b, keep_flag = block
        used = keep_flag * state
        block_out, after = group_output(used, prepare(query_b, key_b, value_b, decay_b, beta_b))
        return (after, block_out)
    blocks = (to_blocks(query, group_count), to_blocks(key_rows, group_count), to_blocks(value, group_count), to_blocks(decay, group_count), to_blocks(beta, group_count), keep_flags)
    start_state = jnp.zeros((H, DK, DV), jnp.float32)
    _, outputs = lax.scan(jax.checkpoint(advance), start_state, blocks)
    return from_blocks(outputs)

def gated_norm(delta_out, gate_heads, out_gain):
    scale_row = lax.rsqrt(lax.optimization_barrier(jnp.mean(delta_out * delta_out, axis=-1, keepdims=True)) + epsilon_gate)
    return delta_out * scale_row * out_gain * jax.nn.silu(gate_heads)

def norm_rows(values):
    return values * lax.rsqrt(lax.optimization_barrier(jnp.mean(values * values, axis=-1, keepdims=True)) + epsilon_norm)

def reference(hidden_in, lengths, attn_gain, w_query, w_key, w_value, w_gate, w_alpha, w_beta, conv_query, conv_key, conv_value, decay_log, decay_bias, out_gain, w_out, ffn_gain, w_ffn_gate, w_ffn_up, w_ffn_down, grad_out):
    positions = jnp.arange(TOKENS, dtype=jnp.int32)
    valid_mask, starts = layout(lengths, positions)
    keep_flags = 1.0 - starts[::GROUP]
    features = make_features(starts, valid_mask, H)
    rim_zeros = jnp.zeros((CONV - 1, 1), jnp.float32)

    def forward(inputs, attn_gain, w_query, w_key, w_value, w_gate, w_alpha, w_beta, conv_query, conv_key, conv_value, decay_log, decay_bias, out_gain, w_out, ffn_gain, w_ffn_gate, w_ffn_up, w_ffn_down):
        normed = low(norm_rows(inputs) * attn_gain)
        query_pre = low(low_back(full_dot(normed, w_query)))
        key_pre = low(low_back(full_dot(normed, w_key)))
        value_pre = low(low_back(full_dot(normed, w_value)))
        gate_pre = low_back(full_dot(normed, w_gate))
        alpha_pre = low_back(full_dot(normed, w_alpha))
        beta_pre = low_back(full_dot(normed, w_beta))
        ext_query = jnp.concatenate([rim_zeros * query_pre[:CONV - 1], query_pre])
        ext_key = jnp.concatenate([rim_zeros * key_pre[:CONV - 1], key_pre])
        ext_value = jnp.concatenate([rim_zeros * value_pre[:CONV - 1], value_pre])
        query_f, key_f, value_f, decay, beta = features(ext_query, ext_key, ext_value, conv_query, conv_key, conv_value, alpha_pre, beta_pre, decay_log, decay_bias)
        delta_out = delta_rule(low(query_f), low(key_f), low(value_f), decay, beta, keep_flags)
        delta_out = delta_out * valid_mask[:, None, None]
        gated = low(gated_norm(delta_out, gate_pre.reshape(TOKENS, H, DV), out_gain)).reshape(TOKENS, H * DV)
        middle = inputs + low_back(full_dot(gated, w_out))
        sent = low(middle)
        normed_ffn = low(norm_rows(sent) * ffn_gain)
        ffn_gate_pre = low_back(full_dot(normed_ffn, w_ffn_gate))
        ffn_up_pre = low_back(full_dot(normed_ffn, w_ffn_up))
        inner_act = low(jax.nn.silu(ffn_gate_pre) * ffn_up_pre)
        return middle + low_back(full_dot(inner_act, w_ffn_down))
    result, pullback = jax.vjp(forward, hidden_in.astype(jnp.float32), attn_gain, w_query.astype(jnp.float32), w_key.astype(jnp.float32), w_value.astype(jnp.float32), w_gate.astype(jnp.float32), w_alpha.astype(jnp.float32), w_beta.astype(jnp.float32), conv_query, conv_key, conv_value, decay_log, decay_bias, out_gain, w_out.astype(jnp.float32), ffn_gain, w_ffn_gate.astype(jnp.float32), w_ffn_up.astype(jnp.float32), w_ffn_down.astype(jnp.float32))
    grad_in, grad_attn_gain, grad_w_query, grad_w_key, grad_w_value, grad_w_gate, grad_w_alpha, grad_w_beta, grad_conv_query, grad_conv_key, grad_conv_value, grad_decay_log, grad_decay_bias, grad_out_gain, grad_w_out, grad_ffn_gain, grad_w_ffn_gate, grad_w_ffn_up, grad_w_ffn_down = pullback(grad_out.astype(jnp.float32))
    return (result.astype(jnp.bfloat16), grad_in, grad_attn_gain, grad_w_query, grad_w_key, grad_w_value, grad_w_gate, grad_w_alpha, grad_w_beta, grad_conv_query, grad_conv_key, grad_conv_value, grad_decay_log, grad_decay_bias, grad_out_gain, grad_w_out, grad_ffn_gain, grad_w_ffn_gate, grad_w_ffn_up, grad_w_ffn_down)
```

```python
import jax
import jax.numpy as jnp
from jax import lax
from jax.sharding import PartitionSpec as P

DK = 128
DV = 256
GROUP = 64
CONV = 4


highest = lax.Precision.HIGHEST
epsilon_norm = 1e-06
epsilon_gate = 1e-05


def shifted(block, axis, distance):
    devices = range(lax.axis_size(axis))
    route = [(i - distance, i) for i in devices if i - distance in devices]
    return lax.ppermute(block, axis, route)


def exchanged(block, axis, bit):
    route = [(i, i ^ bit) for i in range(lax.axis_size(axis))]
    return lax.ppermute(block, axis, route)


def half(block, axis, at, count):
    width = block.shape[axis] // count
    return lax.dynamic_slice_in_dim(block, at * width, width, axis)


def head_scattered(partial):
    place = lax.axis_index("head")
    core, chip = (place % 2, place // 2)
    rows, cols = partial.shape
    parts = partial.reshape(rows, 2, 2, cols // 4)
    low = jnp.concatenate([parts[:, 0, 0], parts[:, 1, 0]], axis=1)
    high = jnp.concatenate([parts[:, 0, 1], parts[:, 1, 1]], axis=1)
    mine = jnp.where(core == 0, low, high)
    other = jnp.where(core == 0, high, low).astype(jnp.bfloat16)
    mine = mine.astype(jnp.float32) + exchanged(other, "head", 1).astype(jnp.float32)
    kept = half(mine, 1, chip, 2)
    sent = half(mine, 1, 1 - chip, 2).astype(jnp.bfloat16)
    return kept + exchanged(sent, "head", 2).astype(jnp.float32)


def head_gathered(block):
    place = lax.axis_index("head")
    core, chip = (place % 2, place // 2)
    across = exchanged(block, "head", 2)
    beside = exchanged(block, "head", 1)
    corner = exchanged(across, "head", 1)
    low = jnp.where(core == 0, block, beside)
    high = jnp.where(core == 0, beside, block)
    far_low = jnp.where(core == 0, across, corner)
    far_high = jnp.where(core == 0, corner, across)
    near = jnp.concatenate([low, high], axis=1)
    far = jnp.concatenate([far_low, far_high], axis=1)
    return jnp.where(
        chip == 0,
        jnp.concatenate([near, far], axis=1),
        jnp.concatenate([far, near], axis=1),
    )


def head_summed(values):
    bit = 1
    while bit < lax.axis_size("head"):
        values = values + exchanged(values, "head", bit)
        bit = bit * 2
    return values


def all_summed(values):
    values = head_summed(values)
    bit = 1
    while bit < lax.axis_size("seq"):
        values = values + exchanged(values, "seq", bit)
        bit = bit * 2
    return values


def seq_scattered(partial):
    devices, place = (lax.axis_size("seq"), lax.axis_index("seq"))
    rows, cols = partial.shape
    parts = partial.astype(jnp.bfloat16).reshape(devices // 2, 2, rows // devices, cols)
    odd = place % 2
    mine = jnp.where(odd == 0, parts[:, 0], parts[:, 1])
    other = jnp.where(odd == 0, parts[:, 1], parts[:, 0])
    got = exchanged(other, "seq", 1)
    mine = (mine.astype(jnp.float32) + got.astype(jnp.float32)).astype(jnp.bfloat16)
    groups = [list(range(first, devices, 2)) for first in range(2)]
    return lax.psum_scatter(
        mine.reshape(rows // 2, cols),
        "seq",
        scatter_dimension=0,
        axis_index_groups=groups,
        tiled=True,
    ).astype(jnp.float32)


def prefix(linear, offset, direction):
    linear, offset = shifted(
        (linear.astype(jnp.bfloat16), offset.astype(jnp.bfloat16)), "seq", direction
    )
    offset = offset.astype(jnp.float32)
    distance = 1
    while True:
        last = distance * 2 >= lax.axis_size("seq") - 1
        sent = (linear, offset.astype(jnp.bfloat16))
        before_linear, before_offset = shifted(sent, "seq", direction * distance)
        offset = offset + jnp.einsum(
            "hij,hjk->hik", linear, before_offset, preferred_element_type=jnp.float32
        )
        if last:
            return offset
        linear = jnp.einsum(
            "hij,hjk->hik", linear, before_linear, preferred_element_type=jnp.float32
        ).astype(jnp.bfloat16)
        distance = distance * 2


def batch_dot(spec, left, right):
    return jnp.einsum(spec, left, right, precision=highest, preferred_element_type=jnp.float32)


def rounded(values):
    return lax.optimization_barrier(values.astype(jnp.bfloat16)).astype(jnp.float32)


def layout(lengths, positions):
    padded = (lengths + (GROUP - 1)) // GROUP * GROUP
    seq_ends = jnp.cumsum(padded)
    begins = seq_ends - padded
    offset = positions[:, None] - begins[None, :]
    inside = (offset >= 0) & (positions[:, None] < seq_ends[None, :])
    valid_mask = jnp.any(inside & (offset < lengths[None, :]), axis=1).astype(jnp.float32)
    starts = jnp.any(offset == 0, axis=1).astype(jnp.float32)
    return (valid_mask, starts)


def delayed(values, shift_by):
    if shift_by == 0:
        return values
    return jnp.concatenate([jnp.zeros((shift_by,), values.dtype), values[:-shift_by]])


def convolve(extended, weight, starts):
    token_rows = starts.shape[0]
    running = extended[CONV - 1 :] * weight[0]
    alive = jnp.ones_like(starts)
    for tap_index in range(1, CONV):
        alive = alive * (1.0 - delayed(starts, tap_index - 1))
        begin_row = CONV - 1 - tap_index
        running = (
            running
            + extended[begin_row : begin_row + token_rows] * weight[tap_index] * alive[:, None]
        )
    return jax.nn.silu(running)


def unit_rows(values):
    return values * lax.rsqrt(jnp.sum(values * values, axis=-1, keepdims=True) + epsilon_norm)


def make_features(starts, valid_mask, head_count):

    def features(
        ext_query,
        ext_key,
        ext_value,
        conv_query,
        conv_key,
        conv_value,
        alpha_pre,
        beta_pre,
        decay_log,
        decay_bias,
    ):
        token_rows = starts.shape[0]
        query_act = convolve(ext_query, conv_query, starts).reshape(token_rows, head_count, DK)
        key_act = convolve(ext_key, conv_key, starts).reshape(token_rows, head_count, DK)
        value_act = convolve(ext_value, conv_value, starts).reshape(token_rows, head_count, DV)
        query = unit_rows(query_act) * DK ** (-0.5)
        key_rows = unit_rows(key_act) * valid_mask[:, None, None]
        value = value_act * valid_mask[:, None, None]
        decay = -jnp.exp(decay_log) * jax.nn.softplus(alpha_pre + decay_bias) * valid_mask[:, None]
        beta = jax.nn.sigmoid(beta_pre)
        return (query, key_rows, value, decay, beta)

    return features


def unit_inverse(strict):
    group_len = strict.shape[-1]
    identity_c = jnp.eye(group_len, dtype=jnp.float32)
    result = identity_c - strict
    power_term = batch_dot("...ij,...jk->...ik", strict, strict)
    degree = 2
    while degree < group_len:
        result = batch_dot("...ij,...jk->...ik", result, identity_c + power_term)
        power_term = batch_dot("...ij,...jk->...ik", power_term, power_term)
        degree = degree * 2
    return result


def prepare(query, key_rows, value, decay, beta):
    group_len = query.shape[-2]
    cumulative = jnp.cumsum(decay, axis=-1)
    lower_mask = jnp.tril(jnp.ones((group_len, group_len), dtype=bool))
    strict_mask = jnp.tril(jnp.ones((group_len, group_len), dtype=bool), -1)
    log_gap = cumulative[..., :, None] - cumulative[..., None, :]
    decay_ratio = jnp.where(lower_mask, jnp.exp(jnp.where(lower_mask, log_gap, 0.0)), 0.0)
    similar = batch_dot("...ik,...jk->...ij", key_rows, key_rows)
    coupling = jnp.where(strict_mask, beta[..., :, None] * decay_ratio * similar, 0.0)
    inverse = unit_inverse(coupling)
    growth = jnp.exp(cumulative)[..., None]
    weights_w = batch_dot("...ij,...jk->...ik", inverse, beta[..., None] * growth * key_rows)
    values_u = batch_dot("...ij,...jk->...ik", inverse, beta[..., None] * value)
    mixing = decay_ratio * batch_dot("...ik,...jk->...ij", query, key_rows)
    closing = cumulative[..., -1:]
    key_decayed = jnp.exp(closing - cumulative)[..., None] * key_rows
    return (growth * query, mixing, weights_w, values_u, key_decayed, jnp.exp(closing[..., 0]))


def group_output(state, parts):
    query_d, mixing, weights_w, values_u, key_decayed, fading = parts
    fresh = values_u - batch_dot("...ck,...kv->...cv", weights_w, state)
    block_out = batch_dot("...ck,...kv->...cv", query_d, state) + batch_dot(
        "...cd,...dv->...cv", mixing, fresh
    )
    after = fading[..., None, None] * state + batch_dot("...ck,...cv->...kv", key_decayed, fresh)
    return (block_out, after)


def to_blocks(values, group_count):
    shaped = values.reshape((group_count, values.shape[0] // group_count) + values.shape[1:])
    return jnp.swapaxes(shaped, 1, 2)


def from_blocks(blocks):
    merged = jnp.swapaxes(blocks, 1, 2)
    return merged.reshape((merged.shape[0] * merged.shape[1],) + merged.shape[2:])


def gated_norm(delta_out, gate_heads, out_gain):
    scale_row = lax.rsqrt(jnp.mean(delta_out * delta_out, axis=-1, keepdims=True) + epsilon_gate)
    return delta_out * scale_row * out_gain * jax.nn.silu(gate_heads)


def with_rim(values, rim_rows):
    return jnp.concatenate(
        [values[: values.shape[0] - (CONV - 1)], values[values.shape[0] - (CONV - 1) :] + rim_rows]
    )


def dense(left, right):
    return jnp.dot(left, right, preferred_element_type=jnp.float32)


def shards(
    hidden_in,
    lengths,
    attn_gain,
    w_query,
    w_key,
    w_value,
    w_gate,
    w_alpha,
    w_beta,
    conv_query,
    conv_key,
    conv_value,
    decay_log,
    decay_bias,
    out_gain,
    w_out,
    ffn_gain,
    w_ffn_gate,
    w_ffn_up,
    w_ffn_down,
    grad_out,
):
    token_rows = hidden_in.shape[0]
    head_count = w_alpha.shape[1]
    col_width = grad_out.shape[1]
    group_count = token_rows // GROUP
    positions = lax.axis_index("seq") * token_rows + jnp.arange(token_rows, dtype=jnp.int32)
    valid_mask, starts = layout(lengths, positions)
    keep_flags = 1.0 - starts[::GROUP]
    head_first = lax.axis_index("head") * head_count
    col_first = lax.axis_index("head") * col_width
    local_log = lax.dynamic_slice_in_dim(decay_log, head_first, head_count)
    local_bias = lax.dynamic_slice_in_dim(decay_bias, head_first, head_count)
    inputs32 = hidden_in.astype(jnp.float32)
    attn_scale = lax.rsqrt(jnp.mean(inputs32 * inputs32, axis=-1, keepdims=True) + epsilon_norm)
    attn_hat = inputs32 * attn_scale
    normed = (attn_hat * attn_gain).astype(jnp.bfloat16)
    query_pre = dense(normed, w_query).astype(jnp.bfloat16)
    key_pre = dense(normed, w_key).astype(jnp.bfloat16)
    value_pre = dense(normed, w_value).astype(jnp.bfloat16)
    gate_pre = dense(normed, w_gate)
    alpha_pre = dense(normed, w_alpha)
    beta_pre = dense(normed, w_beta)
    tail_first = token_rows - (CONV - 1)
    key_first = query_pre.shape[1]
    value_first = key_first + key_pre.shape[1]
    rims = shifted(
        jnp.concatenate([query_pre[tail_first:], key_pre[tail_first:], value_pre[tail_first:]], 1),
        "seq",
        1,
    )
    rim_query = rims[:, :key_first]
    rim_key = rims[:, key_first:value_first]
    rim_value = rims[:, value_first:]
    ext_query = jnp.concatenate([rim_query, query_pre]).astype(jnp.float32)
    ext_key = jnp.concatenate([rim_key, key_pre]).astype(jnp.float32)
    ext_value = jnp.concatenate([rim_value, value_pre]).astype(jnp.float32)
    features = make_features(starts, valid_mask, head_count)
    made, feature_pull = jax.vjp(
        features,
        ext_query,
        ext_key,
        ext_value,
        conv_query,
        conv_key,
        conv_value,
        alpha_pre,
        beta_pre,
        local_log,
        local_bias,
    )
    query_f, key_f, value_f, decay, beta = made
    blocks_query = to_blocks(rounded(query_f), group_count)
    blocks_key = to_blocks(rounded(key_f), group_count)
    blocks_value = to_blocks(rounded(value_f), group_count)
    blocks_decay = to_blocks(decay, group_count)
    blocks_beta = to_blocks(beta, group_count)
    query_d, mixing, weights_w, values_u, key_decayed, fading = prepare(
        blocks_query, blocks_key, blocks_value, blocks_decay, blocks_beta
    )
    identity_k = jnp.eye(DK, dtype=jnp.float32)
    group_linear = fading[..., None, None] * identity_k - batch_dot(
        "...ck,...cj->...kj", key_decayed, weights_w
    )
    group_offset = batch_dot("...ck,...cv->...kv", key_decayed, values_u)
    start_linear = jnp.broadcast_to(identity_k, (head_count, DK, DK))
    start_offset = jnp.zeros((head_count, DK, DV), jnp.float32)

    def compose(carry, block):
        linear_part, offset_part = carry
        block_linear, block_offset, keep_flag = block
        linear_part = batch_dot("hij,hjk->hik", block_linear, keep_flag * linear_part)
        offset_part = (
            batch_dot("hij,hjk->hik", block_linear, keep_flag * offset_part) + block_offset
        )
        return ((linear_part, offset_part), None)

    (device_linear, device_offset), _ = lax.scan(
        compose, (start_linear, start_offset), (group_linear, group_offset, keep_flags)
    )
    entry_state = prefix(device_linear, device_offset, 1)

    def advance(state, block):
        block_linear, block_offset, keep_flag = block
        used = keep_flag * state
        return (batch_dot("hij,hjk->hik", block_linear, used) + block_offset, used)

    _, used_states = lax.scan(advance, entry_state, (group_linear, group_offset, keep_flags))
    fresh = values_u - batch_dot("nhck,nhkv->nhcv", weights_w, used_states)
    block_out = batch_dot("nhck,nhkv->nhcv", query_d, used_states) + batch_dot(
        "nhcd,nhdv->nhcv", mixing, fresh
    )
    delta_out = from_blocks(block_out) * valid_mask[:, None, None]
    gate_heads = gate_pre.reshape(token_rows, head_count, DV)
    gated_f, gated_pull = jax.vjp(gated_norm, delta_out, gate_heads, out_gain)
    gated = gated_f.astype(jnp.bfloat16).reshape(token_rows, head_count * DV)
    mixed = head_scattered(dense(gated, w_out))
    middle = lax.dynamic_slice_in_dim(inputs32, col_first, col_width, 1) + mixed
    sent = head_gathered(middle.astype(jnp.bfloat16)).astype(jnp.float32)
    ffn_scale = lax.rsqrt(jnp.mean(sent * sent, axis=-1, keepdims=True) + epsilon_norm)
    ffn_hat = sent * ffn_scale
    normed_ffn = (ffn_hat * ffn_gain).astype(jnp.bfloat16)
    ffn_gate_pre = dense(normed_ffn, w_ffn_gate)
    ffn_up_pre = dense(normed_ffn, w_ffn_up)
    sigmoid_gate = jax.nn.sigmoid(ffn_gate_pre)
    silu_gate = ffn_gate_pre * sigmoid_gate
    inner_act = (silu_gate * ffn_up_pre).astype(jnp.bfloat16)
    ffn_out = head_scattered(dense(inner_act, w_ffn_down))
    hidden_out = (middle + ffn_out).astype(jnp.bfloat16)
    grad_rows = head_gathered(grad_out)
    d_inner = dense(grad_rows, w_ffn_down.T)
    grad_w_ffn_down = seq_scattered(dense(grad_rows.T, inner_act))
    d_ffn_gate = (
        d_inner * ffn_up_pre * sigmoid_gate * (1.0 + ffn_gate_pre * (1.0 - sigmoid_gate))
    ).astype(jnp.bfloat16)
    d_ffn_up = (d_inner * silu_gate).astype(jnp.bfloat16)
    grad_w_ffn_gate = seq_scattered(dense(normed_ffn.T, d_ffn_gate))
    grad_w_ffn_up = seq_scattered(dense(normed_ffn.T, d_ffn_up))
    d_normed_ffn = dense(d_ffn_gate, w_ffn_gate.T) + dense(d_ffn_up, w_ffn_up.T)
    weighted_ffn = d_normed_ffn * ffn_hat
    grad_ffn_gain = jnp.sum(weighted_ffn, axis=0)
    ffn_dots = head_summed(jnp.mean(weighted_ffn * ffn_gain, axis=-1))[:, None]
    cols = lambda rows: lax.dynamic_slice_in_dim(rows, col_first, col_width, rows.ndim - 1)
    d_sent_cols = ffn_scale * (
        cols(ffn_gain) * head_scattered(d_normed_ffn) - cols(ffn_hat) * ffn_dots
    )
    d_middle = grad_out.astype(jnp.float32) + d_sent_cols
    d_mixed = head_gathered(d_middle.astype(jnp.bfloat16))
    grad_w_out = seq_scattered(dense(d_mixed.T, gated))
    d_gated = dense(d_mixed, w_out.T).reshape(token_rows, head_count, DV)
    d_delta, d_gate_heads, grad_gain_part = gated_pull(d_gated)
    d_delta = d_delta * valid_mask[:, None, None]
    d_gate_pre = d_gate_heads.reshape(token_rows, head_count * DV).astype(jnp.bfloat16)
    d_blocks = to_blocks(d_delta, group_count)
    local_grad = batch_dot("nhck,nhcv->nhkv", query_d, d_blocks) - batch_dot(
        "nhck,nhcv->nhkv", weights_w, batch_dot("nhcd,nhcv->nhdv", mixing, d_blocks)
    )

    def collect_back(carry, block):
        block_linear, block_grad, keep_flag = block
        return (keep_flag * (block_grad + batch_dot("hji,hjk->hik", block_linear, carry)), carry)

    entry_grad, _ = lax.scan(
        collect_back, start_offset, (group_linear, local_grad, keep_flags), reverse=True
    )
    exit_grad = prefix(jnp.swapaxes(device_linear, 1, 2), entry_grad, -1)
    _, after_grads = lax.scan(
        collect_back, exit_grad, (group_linear, local_grad, keep_flags), reverse=True
    )

    def group_fn(query_c, key_c, value_c, decay_c, beta_c):
        return group_output(used_states, prepare(query_c, key_c, value_c, decay_c, beta_c))

    _, pullback = jax.vjp(
        group_fn, blocks_query, blocks_key, blocks_value, blocks_decay, blocks_beta
    )
    block_grads = pullback((d_blocks, after_grads))
    d_query, d_key, d_value, d_decay, d_beta = [from_blocks(piece) for piece in block_grads]
    (
        d_ext_query,
        d_ext_key,
        d_ext_value,
        grad_conv_query,
        grad_conv_key,
        grad_conv_value,
        d_alpha,
        d_beta_pre,
        grad_log_local,
        grad_bias_local,
    ) = feature_pull((d_query, d_key, d_value, d_decay, d_beta))
    backs = shifted(
        jnp.concatenate(
            [d_ext_query[: CONV - 1], d_ext_key[: CONV - 1], d_ext_value[: CONV - 1]], 1
        ),
        "seq",
        -1,
    )
    back_query = backs[:, :key_first]
    back_key = backs[:, key_first:value_first]
    back_value = backs[:, value_first:]
    d_query_pre = with_rim(d_ext_query[CONV - 1 :], back_query).astype(jnp.bfloat16)
    d_key_pre = with_rim(d_ext_key[CONV - 1 :], back_key).astype(jnp.bfloat16)
    d_value_pre = with_rim(d_ext_value[CONV - 1 :], back_value).astype(jnp.bfloat16)
    d_alpha = d_alpha.astype(jnp.bfloat16)
    d_beta_pre = d_beta_pre.astype(jnp.bfloat16)
    grad_w_gate = seq_scattered(dense(normed.T, d_gate_pre))
    grad_w_query = seq_scattered(dense(normed.T, d_query_pre))
    grad_w_key = seq_scattered(dense(normed.T, d_key_pre))
    grad_w_value = seq_scattered(dense(normed.T, d_value_pre))
    grad_w_alpha = dense(normed.T, d_alpha)
    grad_w_beta = dense(normed.T, d_beta_pre)
    devices = lax.axis_size("seq")
    small = jnp.concatenate(
        [grad_w_alpha.reshape(devices, -1), grad_w_beta.reshape(devices, -1)]
        + [
            jnp.swapaxes(piece.reshape(CONV, devices, -1), 0, 1).reshape(devices, -1)
            for piece in (grad_conv_query, grad_conv_key, grad_conv_value)
        ],
        axis=1,
    )
    small_width = small.shape[1]
    small = seq_scattered(small.reshape(devices * small_width // 128, 128)).reshape(small_width)
    small_pieces = []
    for rows, width in [
        (normed.shape[1] // devices, head_count),
        (normed.shape[1] // devices, head_count),
        (CONV, grad_conv_query.shape[1] // devices),
        (CONV, grad_conv_key.shape[1] // devices),
        (CONV, grad_conv_value.shape[1] // devices),
    ]:
        small_pieces.append(small[: rows * width].reshape(rows, width))
        small = small[rows * width :]
    d_normed = (
        dense(d_query_pre, w_query.T)
        + dense(d_key_pre, w_key.T)
        + dense(d_value_pre, w_value.T)
        + dense(d_gate_pre, w_gate.T)
        + dense(d_alpha, w_alpha.T)
        + dense(d_beta_pre, w_beta.T)
    )
    weighted_attn = d_normed * attn_hat
    grad_attn_gain = jnp.sum(weighted_attn, axis=0)
    attn_dots = head_summed(jnp.mean(weighted_attn * attn_gain, axis=-1))[:, None]
    d_input_cols = attn_scale * (
        cols(attn_gain) * head_scattered(d_normed) - cols(attn_hat) * attn_dots
    )
    grad_in = d_middle + d_input_cols
    full_log = lax.dynamic_update_slice_in_dim(
        jnp.zeros(decay_log.shape, jnp.float32), grad_log_local, head_first, 0
    )
    full_bias = lax.dynamic_update_slice_in_dim(
        jnp.zeros(decay_bias.shape, jnp.float32), grad_bias_local, head_first, 0
    )
    sums = all_summed(
        jnp.concatenate([grad_gain_part, grad_ffn_gain, grad_attn_gain, full_log, full_bias])
    )
    gain_first = out_gain.shape[0]
    attn_first = gain_first + ffn_gain.shape[0]
    log_first = attn_first + attn_gain.shape[0]
    bias_first = log_first + decay_log.shape[0]
    rows_of = lambda whole: half(whole, 0, lax.axis_index("seq"), devices)
    return (
        hidden_out,
        grad_in,
        rows_of(sums[attn_first:log_first]),
        grad_w_query,
        grad_w_key,
        grad_w_value,
        grad_w_gate,
        *small_pieces,
        sums[log_first:bias_first],
        sums[bias_first:],
        sums[:gain_first],
        grad_w_out.T,
        rows_of(sums[gain_first:attn_first]),
        grad_w_ffn_gate,
        grad_w_ffn_up,
        grad_w_ffn_down.T,
    )


def solution(mesh):
    return jax.shard_map(
        shards,
        mesh=mesh,
        in_specs=(
            P("seq", None),
            P(),
            P(),
            P(None, "head"),
            P(None, "head"),
            P(None, "head"),
            P(None, "head"),
            P(None, "head"),
            P(None, "head"),
            P(None, "head"),
            P(None, "head"),
            P(None, "head"),
            P(),
            P(),
            P(),
            P("head", None),
            P(),
            P(None, "head"),
            P(None, "head"),
            P("head", None),
            P("seq", "head"),
        ),
        out_specs=(
            P("seq", "head"),
            P("seq", "head"),
            P("seq"),
            P("seq", "head"),
            P("seq", "head"),
            P("seq", "head"),
            P("seq", "head"),
            P("seq", "head"),
            P("seq", "head"),
            P(None, ("head", "seq")),
            P(None, ("head", "seq")),
            P(None, ("head", "seq")),
            P(),
            P(),
            P(),
            P("head", "seq"),
            P("seq"),
            P("seq", "head"),
            P("seq", "head"),
            P("head", "seq"),
        ),
        check_vma=False,
    )
```

```python
import functools

import jax
import jax.numpy as jnp
from jax import lax
from jax.experimental import pallas as pl
from jax.experimental.pallas import tpu as pltpu
from jax.sharding import PartitionSpec as P

DK = 128
DV = 256
GROUP = 64
CONV = 4
HALO = 16
WIDE = DK + DV

epsilon_norm = 1e-06
epsilon_gate = 1e-05

f32 = jnp.float32
bf16 = jnp.bfloat16


def contract(left, right, left_dim=1, right_dim=0):
    return lax.dot_general(
        left, right, (((left_dim,), (right_dim,)), ((), ())), preferred_element_type=f32
    )


def lane_heads(heads):
    return lax.broadcasted_iota(jnp.int32, (1, heads * GROUP), 1) // GROUP


def packed(full, heads):
    owner = lane_heads(heads)
    result = full[:GROUP]
    for head in range(1, heads):
        result = jnp.where(owner == head, full[head * GROUP : (head + 1) * GROUP], result)
    return result


def diagonal(values, heads):
    owner = lane_heads(heads)
    low = values.astype(bf16)
    return jnp.concatenate(
        [low * jnp.where(owner == head, 1.0, 0.0).astype(bf16) for head in range(heads)], axis=0
    )


def spread(columns, heads):
    owner = lane_heads(heads)
    result = jnp.broadcast_to(columns[0], (GROUP, heads * GROUP))
    for head in range(1, heads):
        result = jnp.where(owner == head, columns[head], result)
    return result


def halves(values):
    high = values.astype(bf16)
    return high, (values - high.astype(f32)).astype(bf16)


def product3(left, right, heads):
    left_high, left_low = halves(left)
    right_high, right_low = halves(right)
    rows = left.shape[0]
    first = contract(jnp.concatenate([left_high, left_low], axis=0), diagonal(right_high, heads))
    return first[:rows] + first[rows:] + contract(left_high, diagonal(right_low, heads))


def packed_inverse(coupling, heads):
    row = lax.broadcasted_iota(jnp.int32, coupling.shape, 0)
    lane = lax.broadcasted_iota(jnp.int32, coupling.shape, 1) % GROUP
    power = -coupling
    result = jnp.where(row == lane, 1.0, 0.0) + power
    power = product3(power, power, heads)
    degree = 2
    while degree * 2 < GROUP:
        both = product3(jnp.concatenate([result, power], axis=0), power, heads)
        result = result + both[:GROUP]
        power = both[GROUP:]
        degree = degree * 2
    return result + product3(result, power, heads)


def stacked(block, heads):
    width = block.shape[1] // heads
    return jnp.concatenate([block[:, h * width : (h + 1) * width] for h in range(heads)], axis=0)


def unstacked(block, heads):
    return jnp.concatenate([block[h * GROUP : (h + 1) * GROUP] for h in range(heads)], axis=1)


def fill(ext_ref, now_ref, before_ref, rim_ref, first, keep):
    before = jnp.where(first, rim_ref[...].astype(f32), before_ref[...].astype(f32))
    ext_ref[:HALO, :] = before * keep
    ext_ref[HALO:, :] = now_ref[...].astype(f32)


def tap_sum(ext_ref, conv_ref, low, width):
    total = ext_ref[pl.ds(HALO, GROUP), pl.ds(low, width)] * conv_ref[0:1, pl.ds(low, width)]
    for tap in range(1, CONV):
        total = total + (
            ext_ref[pl.ds(HALO - tap, GROUP), pl.ds(low, width)]
            * conv_ref[tap : tap + 1, pl.ds(low, width)]
        )
    return total


def decay_terms(scal, grow, heads):
    growth = [scal[:, h : h + 1] for h in range(heads)]
    betas = [scal[:, heads + h : heads + h + 1] for h in range(heads)]
    row = lax.broadcasted_iota(jnp.int32, (GROUP, heads * GROUP), 0)
    lane = lax.broadcasted_iota(jnp.int32, (GROUP, heads * GROUP), 1) % GROUP
    lower, strict = (row >= lane, row > lane)
    gap = spread(growth, heads) - grow
    ratio = jnp.where(lower, jnp.exp(jnp.where(lower, gap, 0.0)), 0.0)
    return ratio, spread(betas, heads), strict


def column_stack(scal, kind, heads):
    return jnp.concatenate(
        [scal[:, kind * heads + h : kind * heads + h + 1] for h in range(heads)], axis=0
    )


def forward_kernel(
    heads,
    groups,
    keep_ref,
    fade_ref,
    query_ref,
    key_ref,
    value_ref,
    query_before,
    key_before,
    value_before,
    query_rim,
    key_rim,
    value_rim,
    conv_query,
    conv_key,
    conv_value,
    scal_ref,
    grow_ref,
    query_out,
    key_out,
    value_out,
    wu_out,
    inverse_out,
    state_out,
    linear_out,
    local_out,
    device_out,
    state,
    ext_query,
    ext_key,
    ext_value,
):
    group = pl.program_id(0)
    first = group == 0

    @pl.when(first)
    def _():
        row = lax.broadcasted_iota(jnp.int32, (DK, WIDE), 0)
        lane = lax.broadcasted_iota(jnp.int32, (DK, WIDE), 1)
        unit = jnp.where(row == lane, 1.0, 0.0)
        for h in range(heads):
            state[pl.ds(h * DK, DK), :] = unit

    keep = keep_ref[group]
    fill(ext_query, query_ref, query_before, query_rim, first, keep)
    fill(ext_key, key_ref, key_before, key_rim, first, keep)
    fill(ext_value, value_ref, value_before, value_rim, first, keep)
    scal = scal_ref[...]
    valid = scal[:, 4 * heads : 4 * heads + 1]
    queries, keys, values = ([], [], [])
    for h in range(heads):
        act = jax.nn.silu(tap_sum(ext_query, conv_query, h * DK, DK))
        scale = lax.rsqrt(jnp.sum(act * act, axis=1, keepdims=True) + epsilon_norm)
        queries.append((act * scale * DK ** (-0.5)).astype(bf16))
        act = jax.nn.silu(tap_sum(ext_key, conv_key, h * DK, DK))
        scale = lax.rsqrt(jnp.sum(act * act, axis=1, keepdims=True) + epsilon_norm)
        keys.append((act * scale * valid).astype(bf16))
        act = jax.nn.silu(tap_sum(ext_value, conv_value, h * DV, DV))
        values.append((act * valid).astype(bf16))
    query_out[...] = jnp.concatenate(queries, axis=1)
    key_out[...] = jnp.concatenate(keys, axis=1)
    value_out[...] = jnp.concatenate(values, axis=1)
    query = jnp.concatenate(queries, axis=0)
    key = jnp.concatenate(keys, axis=0)
    value = jnp.concatenate(values, axis=0)
    scores = contract(jnp.concatenate([query, key], axis=0), key, 1, 1)
    mix = packed(scores[: heads * GROUP], heads)
    similar = packed(scores[heads * GROUP :], heads)
    ratio, betas, strict = decay_terms(scal, grow_ref[0], heads)
    mixing = diagonal(ratio * mix, heads)
    inverse = packed_inverse(jnp.where(strict, betas * ratio * similar, 0.0), heads).astype(bf16)
    inverse_out[...] = inverse
    beta = column_stack(scal, 1, heads)
    growth = column_stack(scal, 2, heads)
    closing = column_stack(scal, 3, heads)
    key_wide = key.astype(f32)
    right = jnp.concatenate([beta * growth * key_wide, beta * value.astype(f32)], axis=1)
    wu = contract(diagonal(inverse, heads), right.astype(bf16))
    wu_low = wu.astype(bf16)
    wu_out[0] = wu_low
    grown = (growth * query.astype(f32)).astype(bf16)
    fading = (closing * key_wide).astype(bf16)
    lane = lax.broadcasted_iota(jnp.int32, (1, WIDE), 1)
    fresh, seen = ([], [])
    for h in range(heads):
        rows = slice(h * GROUP, (h + 1) * GROUP)
        used = state[pl.ds(h * DK, DK), :] * keep
        used_low = used.astype(bf16)
        state_out[0, pl.ds(h * DK, DK), :] = used_low
        part = jnp.where(lane >= DK, wu[rows], 0.0) - contract(wu_low[rows, :DK], used_low)
        part = part.astype(bf16)
        after = fade_ref[group * heads + h] * used + contract(fading[rows], part, 0, 0)
        state[pl.ds(h * DK, DK), :] = after
        fresh.append(part)
        seen.append(contract(grown[rows], used_low))
    both = jnp.concatenate(seen, axis=0) + contract(mixing, jnp.concatenate(fresh, axis=0))
    for h in range(heads):
        rows = slice(h * GROUP, (h + 1) * GROUP)
        linear_out[:, pl.ds(h * DK, DK)] = (both[rows, :DK] * valid).astype(bf16)
        local_out[:, pl.ds(h * DV, DV)] = both[rows, DK:] * valid

    @pl.when(group == groups - 1)
    def _():
        device_out[...] = state[...]


def token_block(width, back=None):
    if back is None:
        return pl.BlockSpec((GROUP, width), lambda g: (g, 0))
    return pl.BlockSpec((GROUP, width), lambda g: (back - 1 - g, 0))


def before_block(width, back=None):
    ratio = GROUP // HALO
    if back is None:
        return pl.BlockSpec((HALO, width), lambda g: (jnp.maximum(g * ratio - 1, 0), 0))
    return pl.BlockSpec((HALO, width), lambda g: (jnp.maximum((back - 1 - g) * ratio - 1, 0), 0))


def whole(shape):
    return pl.BlockSpec(shape, lambda g: (0,) * len(shape))


def scalars(decay, beta, valid):
    tokens, heads = decay.shape
    groups = tokens // GROUP
    ones = jnp.tril(jnp.ones((GROUP, GROUP), f32))
    sums = jnp.einsum(
        "ij,gjh->gih", ones, decay.reshape(groups, GROUP, heads), precision=lax.Precision.HIGHEST
    )
    last = sums[:, -1:, :]
    flat = lambda part: part.reshape(tokens, heads)
    scal = jnp.concatenate(
        [flat(sums), beta, flat(jnp.exp(sums)), flat(jnp.exp(last - sums)), valid[:, None]], axis=1
    )
    grow = jnp.swapaxes(sums, 1, 2).reshape(groups, 1, heads * GROUP)
    return scal, grow, jnp.exp(last[:, 0, :])


def delta_forward(pres, rims, convs, scal, grow, fade, keep):
    tokens = scal.shape[0]
    heads, groups = (fade.shape[1], tokens // GROUP)
    widths = [pre.shape[1] for pre in pres]
    smem = pl.BlockSpec(memory_space=pltpu.SMEM)
    return pl.pallas_call(
        functools.partial(forward_kernel, heads, groups),
        grid=(groups,),
        in_specs=[smem, smem]
        + [token_block(w) for w in widths]
        + [before_block(w) for w in widths]
        + [whole((HALO, w)) for w in widths]
        + [whole((CONV, w)) for w in widths]
        + [token_block(scal.shape[1]), pl.BlockSpec((1, 1, heads * GROUP), lambda g: (g, 0, 0))],
        out_specs=[token_block(w) for w in widths]
        + [
            pl.BlockSpec((1, heads * GROUP, WIDE), lambda g: (g, 0, 0)),
            token_block(heads * GROUP),
            pl.BlockSpec((1, heads * DK, WIDE), lambda g: (g, 0, 0)),
            token_block(heads * DK),
            token_block(heads * DV),
            whole((heads * DK, WIDE)),
        ],
        out_shape=[jax.ShapeDtypeStruct((tokens, w), bf16) for w in widths]
        + [
            jax.ShapeDtypeStruct((groups, heads * GROUP, WIDE), bf16),
            jax.ShapeDtypeStruct((tokens, heads * GROUP), bf16),
            jax.ShapeDtypeStruct((groups, heads * DK, WIDE), bf16),
            jax.ShapeDtypeStruct((tokens, heads * DK), bf16),
            jax.ShapeDtypeStruct((tokens, heads * DV), f32),
            jax.ShapeDtypeStruct((heads * DK, WIDE), f32),
        ],
        scratch_shapes=[pltpu.VMEM((heads * DK, WIDE), f32)]
        + [pltpu.VMEM((HALO + GROUP, w), f32) for w in widths],
        compiler_params=pltpu.CompilerParams(vmem_limit_bytes=40 * 2**20),
        cost_estimate=pl.CostEstimate(flops=4 * 10**9, bytes_accessed=2 * 10**7, transcendentals=0),
        name="delta_forward",
    )(keep, fade.reshape(-1), *pres, *pres, *rims, *convs, scal, grow)


def backward_kernel(
    heads,
    groups,
    keep_ref,
    fade_ref,
    query_pre,
    key_pre,
    value_pre,
    query_before,
    key_before,
    value_before,
    query_rim,
    key_rim,
    value_rim,
    conv_query,
    conv_key,
    conv_value,
    scal_ref,
    grow_ref,
    query_ref,
    key_ref,
    value_ref,
    wu_ref,
    inverse_ref,
    state_ref,
    entry_ref,
    exit_ref,
    grad_ref,
    query_out,
    key_out,
    value_out,
    query_conv_out,
    key_conv_out,
    value_conv_out,
    query_back_out,
    key_back_out,
    value_back_out,
    query_tail_out,
    key_tail_out,
    value_tail_out,
    scal_out,
    row_out,
    carry,
    ext_query,
    ext_key,
    ext_value,
    dy_query,
    dy_key,
    dy_value,
):
    step = pl.program_id(0)
    group = groups - 1 - step
    keep = keep_ref[group]

    @pl.when(step == 0)
    def _():
        carry[...] = exit_ref[...]
        for ref in (dy_query, dy_key, dy_value):
            ref[...] = jnp.zeros_like(ref)
        for ref in (query_conv_out, key_conv_out, value_conv_out):
            ref[...] = jnp.zeros_like(ref)

    scal = scal_ref[...]
    valid = scal[:, 4 * heads : 4 * heads + 1]
    beta = column_stack(scal, 1, heads)
    growth = column_stack(scal, 2, heads)
    closing = column_stack(scal, 3, heads)
    query = stacked(query_ref[...], heads)
    key = stacked(key_ref[...], heads)
    value = stacked(value_ref[...], heads)
    grad = stacked(grad_ref[...], heads)
    query_wide, key_wide = (query.astype(f32), key.astype(f32))
    scores = contract(jnp.concatenate([query, key], axis=0), key, 1, 1)
    mix = packed(scores[: heads * GROUP], heads)
    similar = packed(scores[heads * GROUP :], heads)
    ratio, betas, strict = decay_terms(scal, grow_ref[0], heads)
    mixing = ratio * mix
    wu = wu_ref[0]
    grown_wide = growth * query_wide
    fading_wide = closing * key_wide
    grown = grown_wide.astype(bf16)
    fading = fading_wide.astype(bf16)
    mixed_back = contract(diagonal(mixing, heads), grad, 0, 0)
    fresh, d_fresh, d_grown, d_fading, d_weights = ([], [], [], [], [])
    for h in range(heads):
        rows = slice(h * GROUP, (h + 1) * GROUP)
        states = pl.ds(h * DK, DK)
        pair = state_ref[0, states, :]
        used = pair[:, DK:].astype(f32) + contract(pair[:, :DK], entry_ref[states, :])
        used_low = used.astype(bf16)
        weights = wu[rows, :DK]
        part = (wu[rows, DK:].astype(f32) - contract(weights, used_low)).astype(bf16)
        after = carry[states, :]
        after_low = after.astype(bf16)
        d_part = mixed_back[rows] + contract(fading[rows], after_low)
        d_part_low = d_part.astype(bf16)
        stack = jnp.concatenate([grad[rows], d_part_low], axis=0)
        seen = contract(stack, used_low, 1, 1)
        d_grown.append(seen[:GROUP])
        d_weights.append(-seen[GROUP:])
        d_fading.append(contract(part, after_low, 1, 1))
        fade = fade_ref[group * heads + h]
        carry[states, :] = keep * (
            fade * after
            + contract(jnp.concatenate([grown[rows], -weights], axis=0), stack, 0, 0)
        )
        row_out[0, heads + h : heads + h + 1, :] = fade * jnp.sum(
            after * used, axis=0, keepdims=True
        )
        fresh.append(part)
        d_fresh.append(d_part_low)
    d_grown = jnp.concatenate(d_grown, axis=0)
    d_fading = jnp.concatenate(d_fading, axis=0)
    d_weights = jnp.concatenate(d_weights, axis=0).astype(bf16)
    d_fresh = jnp.concatenate(d_fresh, axis=0)
    d_mixing = packed(contract(grad, jnp.concatenate(fresh, axis=0), 1, 1), heads)
    d_right = contract(
        diagonal(inverse_ref[...], heads), jnp.concatenate([d_weights, d_fresh], axis=1), 0, 0
    )
    d_coupling = -packed(contract(d_right.astype(bf16), wu, 1, 1), heads)
    d_coupling = jnp.where(strict, d_coupling, 0.0)
    ratio_grad = ratio * d_coupling
    from_similar = diagonal(betas * ratio_grad, heads)
    from_mix = diagonal(ratio * d_mixing, heads)
    plain = contract(jnp.concatenate([from_mix, from_similar], axis=0), key)
    turned = contract(
        jnp.concatenate([from_similar, from_mix], axis=0),
        jnp.concatenate([key, query], axis=0),
        0,
        0,
    )
    count = heads * GROUP
    d_scaled = d_right[:, :DK]
    d_query = growth * d_grown + plain[:count]
    d_key = beta * growth * d_scaled + closing * d_fading + plain[count:] + turned
    d_value = beta * d_right[:, DK:]
    grown_key = growth * key_wide
    ratio_similar = ratio_grad * similar
    flows = betas * ratio_similar + mixing * d_mixing
    fading_flow = d_fading * fading_wide
    sum_growth = jnp.sum(
        d_grown * grown_wide + d_scaled * (beta * grown_key) - fading_flow, axis=1, keepdims=True
    )
    sum_fading = jnp.sum(fading_flow, axis=1, keepdims=True)
    value_flow = d_right[:, DK:] * value.astype(f32)
    sum_beta = jnp.sum(
        d_scaled * grown_key + value_flow[:, :DK] + value_flow[:, DK:], axis=1, keepdims=True
    )
    row_out[0, 0:1, :] = jnp.sum(flows, axis=0, keepdims=True)
    owner = lane_heads(heads)
    lane = lax.broadcasted_iota(jnp.int32, (GROUP, scal_out.shape[1]), 1)
    columns = jnp.zeros((GROUP, scal_out.shape[1]), f32)
    for h in range(heads):
        rows = slice(h * GROUP, (h + 1) * GROUP)
        flow = jnp.sum(jnp.where(owner == h, flows, 0.0), axis=1, keepdims=True)
        more = jnp.sum(jnp.where(owner == h, ratio_similar, 0.0), axis=1, keepdims=True)
        columns = jnp.where(lane == h, sum_growth[rows] + flow, columns)
        columns = jnp.where(lane == heads + h, sum_beta[rows] + more, columns)
        columns = jnp.where(lane == 2 * heads + h, sum_fading[rows], columns)
    scal_out[...] = columns

    first = group == 0
    after_keep = jnp.where(step == 0, 0.0, keep_ref[jnp.minimum(group + 1, groups - 1)])
    sections = (
        (query_pre, query_before, query_rim, conv_query, ext_query, dy_query, DK, d_query),
        (key_pre, key_before, key_rim, conv_key, ext_key, dy_key, DK, d_key),
        (value_pre, value_before, value_rim, conv_value, ext_value, dy_value, DV, d_value),
    )
    outs = (
        (query_out, query_conv_out, query_back_out, query_tail_out),
        (key_out, key_conv_out, key_back_out, key_tail_out),
        (value_out, value_conv_out, value_back_out, value_tail_out),
    )
    for kind, (section, out) in enumerate(zip(sections, outs)):
        now_ref, before_ref, rim_ref, conv_ref, ext_ref, dy_ref, width, cotangent = section
        pre_out, conv_out, back_out, tail_out = out
        fill(ext_ref, now_ref, before_ref, rim_ref, first, keep)
        dy_ref[8 + GROUP :, :] = dy_ref[8:16, :] * after_keep
        for h in range(heads):
            lanes = pl.ds(h * width, width)
            rows = slice(h * GROUP, (h + 1) * GROUP)
            total = tap_sum(ext_ref, conv_ref, h * width, width)
            sigmoid = jax.nn.sigmoid(total)
            act = total * sigmoid
            d_act = cotangent[rows]
            if kind > 0:
                d_act = d_act * valid
            if kind < 2:
                scale = lax.rsqrt(jnp.sum(act * act, axis=1, keepdims=True) + epsilon_norm)
                inner = jnp.sum(act * d_act, axis=1, keepdims=True)
                d_act = scale * (d_act - act * (scale * scale * inner))
            if kind == 0:
                d_act = d_act * DK ** (-0.5)
            d_total = d_act * (sigmoid * (1.0 + total * (1.0 - sigmoid)))
            dy_ref[pl.ds(8, GROUP), lanes] = d_total
            for tap in range(CONV):
                product = d_total * ext_ref[pl.ds(HALO - tap, GROUP), lanes]
                conv_out[pl.ds(tap * 8, 8), lanes] += jnp.sum(
                    product.reshape(GROUP // 8, 8, width), axis=0
                )
            d_pre = d_total * conv_ref[0:1, lanes]
            for tap in range(1, CONV):
                d_pre = d_pre + dy_ref[pl.ds(8 + tap, GROUP), lanes] * conv_ref[tap : tap + 1, lanes]
            pre_out[:, lanes] = d_pre.astype(bf16)

            @pl.when(step == 0)
            def _():
                tail_out[:, lanes] = d_pre[GROUP - 8 :]

            @pl.when(first)
            def _():
                d_back = dy_ref[pl.ds(1, 8), lanes] * conv_ref[1:2, lanes]
                for tap in range(2, CONV):
                    d_back = d_back + dy_ref[pl.ds(tap, 8), lanes] * conv_ref[tap : tap + 1, lanes]
                back_out[:, lanes] = d_back * keep


def delta_backward(pres, rims, convs, scal, grow, fade, keep, made, entry, exit_grad, grad):
    tokens = scal.shape[0]
    heads, groups = (fade.shape[1], tokens // GROUP)
    widths = [pre.shape[1] for pre in pres]
    smem = pl.BlockSpec(memory_space=pltpu.SMEM)
    turn = lambda *shape: pl.BlockSpec(shape, lambda g: (groups - 1 - g, 0, 0))
    columns = 3 * heads
    return pl.pallas_call(
        functools.partial(backward_kernel, heads, groups),
        grid=(groups,),
        in_specs=[smem, smem]
        + [token_block(w, groups) for w in widths]
        + [before_block(w, groups) for w in widths]
        + [whole((HALO, w)) for w in widths]
        + [whole((CONV, w)) for w in widths]
        + [token_block(scal.shape[1], groups), turn(1, 1, heads * GROUP)]
        + [token_block(w, groups) for w in widths]
        + [
            turn(1, heads * GROUP, WIDE),
            token_block(heads * GROUP, groups),
            turn(1, heads * DK, WIDE),
            whole((heads * DK, DV)),
            whole((heads * DK, DV)),
            token_block(heads * DV, groups),
        ],
        out_specs=[token_block(w, groups) for w in widths]
        + [whole((CONV * 8, w)) for w in widths]
        + [whole((8, w)) for w in widths]
        + [whole((8, w)) for w in widths]
        + [token_block(columns, groups), turn(1, 2 * heads, heads * GROUP)],
        out_shape=[jax.ShapeDtypeStruct((tokens, w), bf16) for w in widths]
        + [jax.ShapeDtypeStruct((CONV * 8, w), f32) for w in widths]
        + [jax.ShapeDtypeStruct((8, w), f32) for w in widths]
        + [jax.ShapeDtypeStruct((8, w), f32) for w in widths]
        + [
            jax.ShapeDtypeStruct((tokens, columns), f32),
            jax.ShapeDtypeStruct((groups, 2 * heads, heads * GROUP), f32),
        ],
        scratch_shapes=[pltpu.VMEM((heads * DK, DV), f32)]
        + [pltpu.VMEM((HALO + GROUP, w), f32) for w in widths]
        + [pltpu.VMEM((16 + GROUP, w), f32) for w in widths],
        compiler_params=pltpu.CompilerParams(vmem_limit_bytes=40 * 2**20),
        cost_estimate=pl.CostEstimate(flops=9 * 10**9, bytes_accessed=3 * 10**7, transcendentals=0),
        name="delta_backward",
    )(keep, fade.reshape(-1), *pres, *pres, *rims, *convs, scal, grow, *made, entry, exit_grad, grad)


def scalar_grads(columns, rows):
    groups, heads = (rows.shape[0], columns.shape[1] // 3)
    parts = columns.reshape(groups, GROUP, 3, heads)
    turned = jnp.swapaxes(rows[:, 0, :].reshape(groups, heads, GROUP), 1, 2)
    sums = parts[:, :, 0] - turned
    last = jnp.sum(parts[:, :, 2], axis=1) + jnp.sum(rows[:, heads:], axis=2)
    ones = jnp.triu(jnp.ones((GROUP, GROUP), f32))
    d_decay = jnp.einsum("ij,gjh->gih", ones, sums, precision=lax.Precision.HIGHEST)
    d_decay = d_decay + last[:, None, :]
    tokens = columns.shape[0]
    return d_decay.reshape(tokens, heads), parts[:, :, 1].reshape(tokens, heads)


def gated_forward_kernel(heads, linear_ref, local_ref, gate_ref, entry_ref, gain_ref, gated_out):
    for h in range(heads):
        wide = pl.ds(h * DV, DV)
        out = local_ref[:, wide] + contract(
            linear_ref[:, pl.ds(h * DK, DK)], entry_ref[pl.ds(h * DK, DK), :]
        )
        scale = lax.rsqrt(jnp.mean(out * out, axis=1, keepdims=True) + epsilon_gate)
        gate = gate_ref[:, wide]
        gated_out[:, wide] = (out * scale * gain_ref[...] * jax.nn.silu(gate)).astype(bf16)


def row_block(rows, width):
    return pl.BlockSpec((rows, width), lambda g: (g, 0))


def gated_forward(linear, local, gate, entry, gain):
    tokens, heads = (local.shape[0], local.shape[1] // DV)
    rows = 2 * GROUP
    return pl.pallas_call(
        functools.partial(gated_forward_kernel, heads),
        grid=(tokens // rows,),
        in_specs=[
            row_block(rows, heads * DK),
            row_block(rows, heads * DV),
            row_block(rows, heads * DV),
            whole((heads * DK, DV)),
            whole((1, DV)),
        ],
        out_specs=row_block(rows, heads * DV),
        out_shape=jax.ShapeDtypeStruct((tokens, heads * DV), bf16),
        compiler_params=pltpu.CompilerParams(vmem_limit_bytes=24 * 2**20),
        cost_estimate=pl.CostEstimate(flops=10**9, bytes_accessed=10**7, transcendentals=0),
        name="gated_forward",
    )(linear, local, gate, entry, gain[None, :])


def gated_backward_kernel(
    heads,
    linear_ref,
    local_ref,
    gate_ref,
    entry_ref,
    gain_ref,
    grad_ref,
    valid_ref,
    delta_out,
    gate_out,
    gain_out,
    entry_out,
):
    @pl.when(pl.program_id(0) == 0)
    def _():
        gain_out[...] = jnp.zeros_like(gain_out)
        entry_out[...] = jnp.zeros_like(entry_out)

    rows = local_ref.shape[0]
    for h in range(heads):
        wide = pl.ds(h * DV, DV)
        linear = linear_ref[:, pl.ds(h * DK, DK)]
        out = local_ref[:, wide] + contract(linear, entry_ref[pl.ds(h * DK, DK), :])
        scale = lax.rsqrt(jnp.mean(out * out, axis=1, keepdims=True) + epsilon_gate)
        unit = out * scale
        gate = gate_ref[:, wide]
        sigmoid = jax.nn.sigmoid(gate)
        grad = grad_ref[:, wide]
        silu = gate * sigmoid
        product = grad * unit
        gain_out[...] += jnp.sum((product * silu).reshape(rows // 8, 8, DV), axis=0)
        gate_out[:, wide] = (
            product * gain_ref[...] * (sigmoid * (1.0 + gate * (1.0 - sigmoid)))
        ).astype(bf16)
        d_unit = grad * gain_ref[...] * silu
        inner = jnp.mean(d_unit * unit, axis=1, keepdims=True)
        delta = (scale * (d_unit - unit * inner) * valid_ref[...]).astype(bf16)
        delta_out[:, wide] = delta
        entry_out[pl.ds(h * DK, DK), :] += contract(linear, delta, 0, 0)


def gated_backward(linear, local, gate, entry, gain, grad, valid):
    tokens, heads = (local.shape[0], local.shape[1] // DV)
    rows = 2 * GROUP
    return pl.pallas_call(
        functools.partial(gated_backward_kernel, heads),
        grid=(tokens // rows,),
        in_specs=[
            row_block(rows, heads * DK),
            row_block(rows, heads * DV),
            row_block(rows, heads * DV),
            whole((heads * DK, DV)),
            whole((1, DV)),
            row_block(rows, heads * DV),
            row_block(rows, 1),
        ],
        out_specs=[
            row_block(rows, heads * DV),
            row_block(rows, heads * DV),
            whole((8, DV)),
            whole((heads * DK, DV)),
        ],
        out_shape=[
            jax.ShapeDtypeStruct((tokens, heads * DV), bf16),
            jax.ShapeDtypeStruct((tokens, heads * DV), bf16),
            jax.ShapeDtypeStruct((8, DV), f32),
            jax.ShapeDtypeStruct((heads * DK, DV), f32),
        ],
        compiler_params=pltpu.CompilerParams(vmem_limit_bytes=24 * 2**20),
        cost_estimate=pl.CostEstimate(flops=2 * 10**9, bytes_accessed=2 * 10**7, transcendentals=0),
        name="gated_backward",
    )(linear, local, gate, entry, gain[None, :], grad, valid[:, None])


def column_place(tile, tiles, place):
    block, inner = (tile // (tiles // 4), tile % (tiles // 4))
    core = jnp.where(block < 2, 1 - place % 2, place % 2)
    chip = jnp.where(block % 2 == 0, 1 - place // 2, place // 2)
    return (chip * 2 + core) * (tiles // 4) + inner


def plain_dense_kernel(place_ref, left_ref, right_ref, out_ref):
    out_ref[...] = contract(left_ref[...], right_ref[...]).astype(bf16)


def plain_dense(left, right, place, tile=256):
    rows, cols = (left.shape[0], right.shape[1])
    tiles = cols // tile
    return pl.pallas_call(
        plain_dense_kernel,
        grid_spec=pltpu.PrefetchScalarGridSpec(
            num_scalar_prefetch=1,
            grid=(tiles,),
            in_specs=[
                pl.BlockSpec(left.shape, lambda i, place: (0, 0)),
                pl.BlockSpec(
                    (right.shape[0], tile), lambda i, place: (0, column_place(i, tiles, place[0]))
                ),
            ],
            out_specs=pl.BlockSpec((rows, tile), lambda i, place: (0, i)),
        ),
        out_shape=jax.ShapeDtypeStruct((rows, cols), bf16),
        compiler_params=pltpu.CompilerParams(vmem_limit_bytes=24 * 2**20),
        cost_estimate=pl.CostEstimate(
            flops=2 * rows * cols * left.shape[1], bytes_accessed=10**7, transcendentals=0
        ),
        name="plain_dense",
    )(place, left, right)


def norm_dense_kernel(count, place_ref, *refs):
    lefts, rights = (refs[:count], refs[count : 2 * count])
    rows_ref, scale_ref, gain_ref, out_ref, gain_out, dots_out = refs[2 * count :]
    total = contract(lefts[0][...], rights[0][...], 1, 1)
    for left, right in zip(lefts[1:], rights[1:]):
        total = total + contract(left[...], right[...], 1, 1)
    out_ref[...] = total.astype(bf16)
    weighted = total * (rows_ref[...].astype(f32) * scale_ref[...])
    gain_out[...] = jnp.sum(weighted, axis=0, keepdims=True)
    dots = jnp.sum(weighted * gain_ref[...], axis=1, keepdims=True)

    @pl.when(pl.program_id(0) == 0)
    def _():
        dots_out[...] = dots

    @pl.when(pl.program_id(0) > 0)
    def _():
        dots_out[...] += dots


def norm_dense(pairs, rows, scale, gain, place, tile=256):
    tokens, cols = rows.shape
    tiles = cols // tile
    lefts, rights = ([left for left, _ in pairs], [right for _, right in pairs])
    placed = lambda i, place: (0, column_place(i, tiles, place[0]))
    return pl.pallas_call(
        functools.partial(norm_dense_kernel, len(pairs)),
        grid_spec=pltpu.PrefetchScalarGridSpec(
            num_scalar_prefetch=1,
            grid=(tiles,),
            in_specs=[pl.BlockSpec(left.shape, lambda i, place: (0, 0)) for left in lefts]
            + [
                pl.BlockSpec(
                    (tile, right.shape[1]),
                    lambda i, place: (column_place(i, tiles, place[0]), 0),
                )
                for right in rights
            ]
            + [
                pl.BlockSpec((tokens, tile), placed),
                pl.BlockSpec((tokens, 1), lambda i, place: (0, 0)),
                pl.BlockSpec((1, tile), placed),
            ],
            out_specs=[
                pl.BlockSpec((tokens, tile), lambda i, place: (0, i)),
                pl.BlockSpec((1, tile), placed),
                pl.BlockSpec((tokens, 1), lambda i, place: (0, 0)),
            ],
        ),
        out_shape=[
            jax.ShapeDtypeStruct((tokens, cols), bf16),
            jax.ShapeDtypeStruct((1, cols), f32),
            jax.ShapeDtypeStruct((tokens, 1), f32),
        ],
        compiler_params=pltpu.CompilerParams(vmem_limit_bytes=32 * 2**20),
        cost_estimate=pl.CostEstimate(
            flops=2 * tokens * cols * sum(right.shape[1] for right in rights),
            bytes_accessed=2 * 10**7,
            transcendentals=0,
        ),
        name="norm_dense",
    )(place, *lefts, *rights, rows, scale, gain[None, :])


def shifted(block, axis, distance):
    devices = range(lax.axis_size(axis))
    route = [(i - distance, i) for i in devices if i - distance in devices]
    return lax.ppermute(block, axis, route)


def exchanged(block, axis, bit):
    route = [(i, i ^ bit) for i in range(lax.axis_size(axis))]
    return lax.ppermute(block, axis, route)


def half(block, axis, at, count):
    width = block.shape[axis] // count
    return lax.dynamic_slice_in_dim(block, at * width, width, axis)


def head_scattered(partial):
    width = partial.shape[1] // 2
    mine = partial[:, width:].astype(f32) + exchanged(partial[:, :width], "head", 1).astype(f32)
    width = width // 2
    return mine[:, width:] + exchanged(mine[:, :width].astype(bf16), "head", 2).astype(f32)


def head_gathered(block):
    place = lax.axis_index("head")
    core, chip = (place % 2, place // 2)
    across = exchanged(block, "head", 2)
    beside = exchanged(block, "head", 1)
    corner = exchanged(across, "head", 1)
    low = jnp.where(core == 0, block, beside)
    high = jnp.where(core == 0, beside, block)
    far_low = jnp.where(core == 0, across, corner)
    far_high = jnp.where(core == 0, corner, across)
    near = jnp.concatenate([low, high], axis=1)
    far = jnp.concatenate([far_low, far_high], axis=1)
    return jnp.where(
        chip == 0,
        jnp.concatenate([near, far], axis=1),
        jnp.concatenate([far, near], axis=1),
    )


def head_summed(values):
    bit = 1
    while bit < lax.axis_size("head"):
        values = values + exchanged(values, "head", bit)
        bit = bit * 2
    return values


def all_summed(values):
    values = head_summed(values)
    bit = 1
    while bit < lax.axis_size("seq"):
        values = values + exchanged(values, "seq", bit)
        bit = bit * 2
    return values


def own_half(rows, odd):
    tokens, width = rows.shape
    devices = lax.axis_size("seq")
    parts = rows.reshape(tokens, devices // 2, 2, width // devices)
    return lax.dynamic_index_in_dim(parts, odd, 2, False).reshape(tokens, width // 2)


def halves_of(rows):
    odd = lax.axis_index("seq") % 2
    return own_half(rows, odd), own_half(rows, 1 - odd)


def seq_scattered(mine):
    devices = lax.axis_size("seq")
    groups = [list(range(first, devices, 2)) for first in range(2)]
    return lax.psum_scatter(
        mine.astype(bf16), "seq", scatter_dimension=0, axis_index_groups=groups, tiled=True
    ).astype(f32)


def weight_grad(rows, cols):
    own, other = rows
    got = exchanged(dense(other.T, cols).astype(bf16), "seq", 1)
    return seq_scattered(dense(own.T, cols) + got.astype(f32))


def prefix(pair, direction):
    pair = shifted(pair.astype(bf16), "seq", direction)
    offset = pair[:, :, DK:].astype(f32)
    distance = 1
    while True:
        last = distance * 2 >= lax.axis_size("seq") - 1
        sent = pair[:, :, DK:] if last else pair
        before = shifted(sent, "seq", direction * distance)
        moved = jnp.einsum("hij,hjk->hik", pair[:, :, :DK], before, preferred_element_type=f32)
        if last:
            return offset + moved
        offset = offset + moved[:, :, DK:]
        pair = jnp.concatenate([moved[:, :, :DK], offset], axis=2).astype(bf16)
        distance = distance * 2


def layout(lengths, positions):
    padded = (lengths + (GROUP - 1)) // GROUP * GROUP
    seq_ends = jnp.cumsum(padded)
    begins = seq_ends - padded
    offset = positions[:, None] - begins[None, :]
    inside = (offset >= 0) & (positions[:, None] < seq_ends[None, :])
    valid_mask = jnp.any(inside & (offset < lengths[None, :]), axis=1).astype(jnp.float32)
    starts = jnp.any(offset == 0, axis=1).astype(jnp.float32)
    return (valid_mask, starts)


def dense(left, right):
    return jnp.dot(left, right, preferred_element_type=jnp.float32)


def shards(
    hidden_in,
    lengths,
    attn_gain,
    w_query,
    w_key,
    w_value,
    w_gate,
    w_alpha,
    w_beta,
    conv_query,
    conv_key,
    conv_value,
    decay_log,
    decay_bias,
    out_gain,
    w_out,
    ffn_gain,
    w_ffn_gate,
    w_ffn_up,
    w_ffn_down,
    grad_out,
):
    token_rows = hidden_in.shape[0]
    head_count = w_alpha.shape[1]
    col_width = grad_out.shape[1]
    devices = lax.axis_size("seq")
    positions = lax.axis_index("seq") * token_rows + jnp.arange(token_rows, dtype=jnp.int32)
    valid_mask, starts = layout(lengths, positions)
    keep_flags = 1.0 - starts[::GROUP]
    head_place = lax.axis_index("head")
    place = head_place[None].astype(jnp.int32)
    head_first = head_place * head_count
    col_first = head_place * col_width
    cols = lambda rows: lax.dynamic_slice_in_dim(rows, col_first, col_width, rows.ndim - 1)
    local_log = lax.dynamic_slice_in_dim(decay_log, head_first, head_count)
    local_bias = lax.dynamic_slice_in_dim(decay_bias, head_first, head_count)

    inputs32 = hidden_in.astype(f32)
    attn_scale = lax.rsqrt(jnp.mean(inputs32 * inputs32, axis=-1, keepdims=True) + epsilon_norm)
    normed = (inputs32 * attn_scale * attn_gain).astype(bf16)
    pres = [dense(normed, weight).astype(bf16) for weight in (w_query, w_key, w_value)]
    widths = [pre.shape[1] for pre in pres]
    edges = [0, widths[0], widths[0] + widths[1], sum(widths)]
    split = lambda rows: [rows[:, a:b] for a, b in zip(edges[:-1], edges[1:])]
    tail_first = token_rows - (CONV - 1)
    rims = shifted(jnp.concatenate([pre[tail_first:] for pre in pres], 1), "seq", 1)
    rims = split(jnp.pad(rims, ((HALO - (CONV - 1), 0), (0, 0))))
    alpha_pre = dense(normed, w_alpha)
    beta_pre = dense(normed, w_beta)

    def decays(alpha_pre, decay_log, decay_bias):
        rate = jnp.exp(decay_log) * jax.nn.softplus(alpha_pre + decay_bias)
        return -rate * valid_mask[:, None]

    decay, decay_pull = jax.vjp(decays, alpha_pre, local_log, local_bias)
    beta = jax.nn.sigmoid(beta_pre)
    scal, grow, fade = scalars(decay, beta, valid_mask)
    convs = [conv_query, conv_key, conv_value]
    *made, linear, local, device_pair = delta_forward(
        pres, rims, convs, scal, grow, fade, keep_flags
    )
    device_pair = device_pair.reshape(head_count, DK, WIDE)
    entry = prefix(device_pair, 1).astype(bf16).reshape(head_count * DK, DV)
    gate_pre = dense(normed, w_gate)
    gated = gated_forward(linear, local, gate_pre, entry, out_gain)
    mixed = head_scattered(plain_dense(gated, w_out, place))
    middle = cols(hidden_in).astype(f32) + mixed
    sent = head_gathered(middle.astype(bf16))
    sent32 = sent.astype(f32)
    ffn_scale = lax.rsqrt(jnp.mean(sent32 * sent32, axis=-1, keepdims=True) + epsilon_norm)
    normed_ffn = (sent32 * ffn_scale * ffn_gain).astype(bf16)
    ffn_gate_pre = dense(normed_ffn, w_ffn_gate)
    ffn_up_pre = dense(normed_ffn, w_ffn_up)
    sigmoid_gate = jax.nn.sigmoid(ffn_gate_pre)
    silu_gate = ffn_gate_pre * sigmoid_gate
    inner_act = (silu_gate * ffn_up_pre).astype(bf16)
    ffn_out = head_scattered(plain_dense(inner_act, w_ffn_down, place))
    hidden_out = (middle + ffn_out).astype(bf16)
    grad_rows = head_gathered(grad_out)
    d_inner = dense(grad_rows, w_ffn_down.T)
    grad_w_ffn_down = weight_grad(halves_of(grad_rows), inner_act)
    d_ffn_gate = (
        d_inner * ffn_up_pre * sigmoid_gate * (1.0 + ffn_gate_pre * (1.0 - sigmoid_gate))
    ).astype(bf16)
    d_ffn_up = (d_inner * silu_gate).astype(bf16)
    ffn_halves = halves_of(normed_ffn)
    grad_w_ffn_gate = weight_grad(ffn_halves, d_ffn_gate)
    grad_w_ffn_up = weight_grad(ffn_halves, d_ffn_up)
    d_normed_ffn, grad_ffn_gain, ffn_dots = norm_dense(
        [(d_ffn_gate, w_ffn_gate), (d_ffn_up, w_ffn_up)], sent, ffn_scale, ffn_gain, place
    )
    ffn_dots = head_summed(ffn_dots[:, 0])[:, None] / sent.shape[1]
    d_sent_cols = ffn_scale * (
        cols(ffn_gain) * head_scattered(d_normed_ffn) - cols(sent32) * ffn_scale * ffn_dots
    )
    d_middle = grad_out.astype(f32) + d_sent_cols
    d_mixed = head_gathered(d_middle.astype(bf16))
    d_gated = dense(d_mixed, w_out.T)
    d_delta, d_gate_pre, gain_part, entry_grad = gated_backward(
        linear, local, gate_pre, entry, out_gain, d_gated, valid_mask
    )
    grad_w_out = weight_grad(halves_of(d_mixed), gated)
    back_pair = jnp.concatenate(
        [
            jnp.swapaxes(device_pair[:, :, :DK], 1, 2),
            entry_grad.reshape(head_count, DK, DV),
        ],
        axis=2,
    )
    exit_grad = prefix(back_pair, -1).reshape(head_count * DK, DV)
    results = delta_backward(
        pres, rims, convs, scal, grow, fade, keep_flags, made, entry, exit_grad, d_delta
    )
    d_pres, conv_parts, backs, tails = (results[i : i + 3] for i in range(0, 12, 3))
    d_decay, d_beta = scalar_grads(*results[12:])
    d_alpha, grad_log_local, grad_bias_local = decay_pull(d_decay)
    d_alpha = d_alpha.astype(bf16)
    d_beta_pre = (d_beta * beta * (1.0 - beta)).astype(bf16)
    backs = shifted(jnp.concatenate(backs, 1)[8 - (CONV - 1) :], "seq", -1)
    tails = split(jnp.concatenate(tails, 1) + jnp.pad(backs, ((8 - (CONV - 1), 0), (0, 0))))
    d_query_pre, d_key_pre, d_value_pre = [
        lax.dynamic_update_slice(d_pre, tail.astype(bf16), (token_rows - 8, 0))
        for d_pre, tail in zip(d_pres, tails)
    ]
    normed_halves = halves_of(normed)
    grad_w_gate = weight_grad(normed_halves, d_gate_pre)
    grad_w_query = weight_grad(normed_halves, d_query_pre)
    grad_w_key = weight_grad(normed_halves, d_key_pre)
    grad_w_value = weight_grad(normed_halves, d_value_pre)
    small = [dense(normed.T, d_alpha).reshape(devices, -1), dense(normed.T, d_beta_pre).reshape(devices, -1)]
    for part in conv_parts:
        part = jnp.sum(part.reshape(CONV, 8, -1), axis=1).reshape(CONV, devices, -1)
        small.append(jnp.swapaxes(part, 0, 1).reshape(devices, -1))
    small = jnp.concatenate(small, axis=1)
    small_width = small.shape[1]
    odd = lax.axis_index("seq") % 2
    small = small.astype(bf16).reshape(devices // 2, 2, small_width // 128, 128)
    got = exchanged(lax.dynamic_index_in_dim(small, 1 - odd, 1, False), "seq", 1)
    small = lax.dynamic_index_in_dim(small, odd, 1, False).astype(f32) + got.astype(f32)
    small = seq_scattered(small.reshape(devices * small_width // 256, 128)).reshape(small_width)
    small_pieces = []
    for rows, width in [(normed.shape[1] // devices, head_count)] * 2 + [
        (CONV, width // devices) for width in widths
    ]:
        small_pieces.append(small[: rows * width].reshape(rows, width))
        small = small[rows * width :]
    d_normed, grad_attn_gain, attn_dots = norm_dense(
        [
            (d_query_pre, w_query),
            (d_key_pre, w_key),
            (d_value_pre, w_value),
            (d_gate_pre, w_gate),
            (d_alpha, w_alpha),
            (d_beta_pre, w_beta),
        ],
        hidden_in,
        attn_scale,
        attn_gain,
        place,
    )
    attn_dots = head_summed(attn_dots[:, 0])[:, None] / hidden_in.shape[1]
    grad_in = d_middle + attn_scale * (
        cols(attn_gain) * head_scattered(d_normed)
        - cols(hidden_in).astype(f32) * attn_scale * attn_dots
    )
    full_log = lax.dynamic_update_slice_in_dim(
        jnp.zeros(decay_log.shape, f32), grad_log_local, head_first, 0
    )
    full_bias = lax.dynamic_update_slice_in_dim(
        jnp.zeros(decay_bias.shape, f32), grad_bias_local, head_first, 0
    )
    sums = all_summed(
        jnp.concatenate(
            [jnp.sum(gain_part, 0), grad_ffn_gain[0], grad_attn_gain[0], full_log, full_bias]
        )
    )
    gain_first = out_gain.shape[0]
    attn_first = gain_first + ffn_gain.shape[0]
    log_first = attn_first + attn_gain.shape[0]
    bias_first = log_first + decay_log.shape[0]
    rows_of = lambda whole: half(whole, 0, lax.axis_index("seq"), devices)
    return (
        hidden_out,
        grad_in,
        rows_of(sums[attn_first:log_first]),
        grad_w_query,
        grad_w_key,
        grad_w_value,
        grad_w_gate,
        *small_pieces,
        sums[log_first:bias_first],
        sums[bias_first:],
        sums[:gain_first],
        grad_w_out.T,
        rows_of(sums[gain_first:attn_first]),
        grad_w_ffn_gate,
        grad_w_ffn_up,
        grad_w_ffn_down.T,
    )


def solution(mesh):
    return jax.shard_map(
        shards,
        mesh=mesh,
        in_specs=(
            P("seq", None),
            P(),
            P(),
            P(None, "head"),
            P(None, "head"),
            P(None, "head"),
            P(None, "head"),
            P(None, "head"),
            P(None, "head"),
            P(None, "head"),
            P(None, "head"),
            P(None, "head"),
            P(),
            P(),
            P(),
            P("head", None),
            P(),
            P(None, "head"),
            P(None, "head"),
            P("head", None),
            P("seq", "head"),
        ),
        out_specs=(
            P("seq", "head"),
            P("seq", "head"),
            P("seq"),
            P("seq", "head"),
            P("seq", "head"),
            P("seq", "head"),
            P("seq", "head"),
            P("seq", "head"),
            P("seq", "head"),
            P(None, ("head", "seq")),
            P(None, ("head", "seq")),
            P(None, ("head", "seq")),
            P(),
            P(),
            P(),
            P("head", "seq"),
            P("seq"),
            P("seq", "head"),
            P("seq", "head"),
            P("head", "seq"),
        ),
        check_vma=False,
    )
```

```python
import functools

import jax
import jax.numpy as jnp
from jax import lax
from jax.experimental import pallas as pl
from jax.experimental.pallas import tpu as pltpu
from jax.sharding import PartitionSpec as P

DK = 128
DV = 256
GROUP = 64
CONV = 4
HALO = 16
WIDE = DK + DV
VMEM = 60 * 2**20
SMALL = 30 * 2**20

epsilon_norm = 1e-06
epsilon_gate = 1e-05

f32 = jnp.float32
bf16 = jnp.bfloat16


def contract(left, right, left_dim=1, right_dim=0):
    return lax.dot_general(
        left, right, (((left_dim,), (right_dim,)), ((), ())), preferred_element_type=f32
    )


def lane_heads(heads):
    return lax.broadcasted_iota(jnp.int32, (1, heads * GROUP), 1) // GROUP


def packed(full, heads):
    owner = lane_heads(heads)
    result = full[:GROUP]
    for head in range(1, heads):
        result = jnp.where(owner == head, full[head * GROUP : (head + 1) * GROUP], result)
    return result


def diagonal(values, heads):
    owner = lane_heads(heads)
    low = values.astype(bf16)
    return jnp.concatenate(
        [low * jnp.where(owner == head, 1.0, 0.0).astype(bf16) for head in range(heads)], axis=0
    )


def spread(columns, heads):
    owner = lane_heads(heads)
    result = jnp.broadcast_to(columns[0], (GROUP, heads * GROUP))
    for head in range(1, heads):
        result = jnp.where(owner == head, columns[head], result)
    return result


def halves(values):
    high = values.astype(bf16)
    return high, (values - high.astype(f32)).astype(bf16)


def product3(left, right, heads):
    left_high, left_low = halves(left)
    right_high, right_low = halves(right)
    rows = left.shape[0]
    first = contract(jnp.concatenate([left_high, left_low], axis=0), diagonal(right_high, heads))
    return first[:rows] + first[rows:] + contract(left_high, diagonal(right_low, heads))


def packed_inverse(coupling, heads):
    row = lax.broadcasted_iota(jnp.int32, coupling.shape, 0)
    lane = lax.broadcasted_iota(jnp.int32, coupling.shape, 1) % GROUP
    power = -coupling
    result = jnp.where(row == lane, 1.0, 0.0) + power
    power = product3(power, power, heads)
    degree = 2
    while degree * 2 < GROUP:
        both = product3(jnp.concatenate([result, power], axis=0), power, heads)
        result = result + both[:GROUP]
        power = both[GROUP:]
        degree = degree * 2
    return result + product3(result, power, heads)


def stacked(block, heads):
    width = block.shape[1] // heads
    return jnp.concatenate([block[:, h * width : (h + 1) * width] for h in range(heads)], axis=0)


def unstacked(block, heads):
    return jnp.concatenate([block[h * GROUP : (h + 1) * GROUP] for h in range(heads)], axis=1)


def fill(ext_ref, now_ref, before_ref, rim_ref, first, keep):
    before = jnp.where(first, rim_ref[...].astype(f32), before_ref[...].astype(f32))
    ext_ref[:HALO, :] = before * keep
    ext_ref[HALO:, :] = now_ref[...].astype(f32)


def tap_sum(ext_ref, conv_ref, low, width):
    total = ext_ref[pl.ds(HALO, GROUP), pl.ds(low, width)] * conv_ref[0:1, pl.ds(low, width)]
    for tap in range(1, CONV):
        total = total + (
            ext_ref[pl.ds(HALO - tap, GROUP), pl.ds(low, width)]
            * conv_ref[tap : tap + 1, pl.ds(low, width)]
        )
    return total


def summed_rows(mask, values, pieces=3):
    parts = []
    for _ in range(pieces):
        parts.append(values.astype(bf16))
        values = values - parts[-1].astype(f32)
    width = values.shape[1]
    sums = contract(mask.astype(bf16), jnp.concatenate(parts, axis=1))
    return sum(sums[:, i * width : (i + 1) * width] for i in range(pieces))


def token_terms(scal_ref, rate_ref, heads):
    scal = scal_ref[...]
    rate = rate_ref[...]
    shifted_alpha = scal[:, :heads] + rate[1:2]
    valid = scal[:, 2 * heads : 2 * heads + 1]
    decay = -rate[0:1] * jax.nn.softplus(shifted_alpha) * valid
    beta = jax.nn.sigmoid(scal[:, heads : 2 * heads])
    row = lax.broadcasted_iota(jnp.int32, (GROUP, heads * GROUP), 0)
    lane = lax.broadcasted_iota(jnp.int32, (GROUP, heads * GROUP), 1) % GROUP
    wide = spread([decay[:, h : h + 1] for h in range(heads)], heads)
    square_row = lax.broadcasted_iota(jnp.int32, (GROUP, GROUP), 0)
    square_lane = lax.broadcasted_iota(jnp.int32, (GROUP, GROUP), 1)
    sums = summed_rows(jnp.where(square_row >= square_lane, 1.0, 0.0), wide)
    across = jnp.sum(jnp.where(row <= lane, wide, 0.0), axis=0, keepdims=True)
    lower, strict = (row >= lane, row > lane)
    ratio = jnp.where(lower, jnp.exp(jnp.where(lower, sums - across, 0.0)), 0.0)
    betas = [beta[:, h : h + 1] for h in range(heads)]
    last = sums[GROUP - 1 :]
    grown, closing = (jnp.exp(sums), jnp.exp(last - sums))
    column = lambda values: jnp.concatenate(
        [values[:, h * GROUP : h * GROUP + 1] for h in range(heads)], axis=0
    )
    fade = jnp.exp(last)
    fades = [fade[:, h * GROUP : h * GROUP + 1] for h in range(heads)]
    return dict(
        alpha=shifted_alpha,
        rate=rate[0:1],
        valid=valid,
        decay=decay,
        beta=beta,
        ratio=ratio,
        strict=strict,
        betas=spread(betas, heads),
        beta_column=jnp.concatenate(betas, axis=0),
        growth=column(grown),
        closing=column(closing),
        fades=fades,
    )


def forward_kernel(
    heads,
    groups,
    keep_ref,
    query_ref,
    key_ref,
    value_ref,
    query_before,
    key_before,
    value_before,
    query_rim,
    key_rim,
    value_rim,
    conv_query,
    conv_key,
    conv_value,
    scal_ref,
    rate_ref,
    query_out,
    key_out,
    value_out,
    wu_out,
    inverse_out,
    state_out,
    linear_out,
    local_out,
    device_out,
    state,
    ext_query,
    ext_key,
    ext_value,
):
    group = pl.program_id(0)
    first = group == 0

    @pl.when(first)
    def _():
        row = lax.broadcasted_iota(jnp.int32, (DK, WIDE), 0)
        lane = lax.broadcasted_iota(jnp.int32, (DK, WIDE), 1)
        unit = jnp.where(row == lane, 1.0, 0.0)
        for h in range(heads):
            state[pl.ds(h * DK, DK), :] = unit

    keep = keep_ref[group]
    fill(ext_query, query_ref, query_before, query_rim, first, keep)
    fill(ext_key, key_ref, key_before, key_rim, first, keep)
    fill(ext_value, value_ref, value_before, value_rim, first, keep)
    terms = token_terms(scal_ref, rate_ref, heads)
    valid = terms["valid"]
    queries, keys, values = ([], [], [])
    for h in range(heads):
        act = jax.nn.silu(tap_sum(ext_query, conv_query, h * DK, DK))
        scale = lax.rsqrt(jnp.sum(act * act, axis=1, keepdims=True) + epsilon_norm)
        queries.append((act * scale * DK ** (-0.5)).astype(bf16))
        act = jax.nn.silu(tap_sum(ext_key, conv_key, h * DK, DK))
        scale = lax.rsqrt(jnp.sum(act * act, axis=1, keepdims=True) + epsilon_norm)
        keys.append((act * scale * valid).astype(bf16))
        act = jax.nn.silu(tap_sum(ext_value, conv_value, h * DV, DV))
        values.append((act * valid).astype(bf16))
    query_out[...] = jnp.concatenate(queries, axis=1)
    key_out[...] = jnp.concatenate(keys, axis=1)
    value_out[...] = jnp.concatenate(values, axis=1)
    query = jnp.concatenate(queries, axis=0)
    key = jnp.concatenate(keys, axis=0)
    value = jnp.concatenate(values, axis=0)
    scores = contract(jnp.concatenate([query, key], axis=0), key, 1, 1)
    mix = packed(scores[: heads * GROUP], heads)
    similar = packed(scores[heads * GROUP :], heads)
    ratio, betas, strict = (terms["ratio"], terms["betas"], terms["strict"])
    mixing = diagonal(ratio * mix, heads)
    inverse = packed_inverse(jnp.where(strict, betas * ratio * similar, 0.0), heads).astype(bf16)
    inverse_out[...] = inverse
    beta, growth, closing = (terms["beta_column"], terms["growth"], terms["closing"])
    key_wide = key.astype(f32)
    right = jnp.concatenate([beta * growth * key_wide, beta * value.astype(f32)], axis=1)
    wu = contract(diagonal(inverse, heads), right.astype(bf16))
    wu_low = wu.astype(bf16)
    wu_out[0] = wu_low
    grown = (growth * query.astype(f32)).astype(bf16)
    fading = (closing * key_wide).astype(bf16)
    lane = lax.broadcasted_iota(jnp.int32, (1, WIDE), 1)
    fresh, seen = ([], [])
    for h in range(heads):
        rows = slice(h * GROUP, (h + 1) * GROUP)
        used = state[pl.ds(h * DK, DK), :] * keep
        used_low = used.astype(bf16)
        state_out[0, pl.ds(h * DK, DK), :] = used_low
        part = jnp.where(lane >= DK, wu[rows], 0.0) - contract(wu_low[rows, :DK], used_low)
        part = part.astype(bf16)
        after = terms["fades"][h] * used + contract(fading[rows], part, 0, 0)
        state[pl.ds(h * DK, DK), :] = after
        fresh.append(part)
        seen.append(contract(grown[rows], used_low))
    both = jnp.concatenate(seen, axis=0) + contract(mixing, jnp.concatenate(fresh, axis=0))
    for h in range(heads):
        rows = slice(h * GROUP, (h + 1) * GROUP)
        linear_out[:, pl.ds(h * DK, DK)] = (both[rows, :DK] * valid).astype(bf16)
        local_out[:, pl.ds(h * DV, DV)] = both[rows, DK:] * valid

    @pl.when(group == groups - 1)
    def _():
        device_out[...] = state[...]


def token_block(width, back=None):
    if back is None:
        return pl.BlockSpec((GROUP, width), lambda g: (g, 0))
    return pl.BlockSpec((GROUP, width), lambda g: (back - 1 - g, 0))


def before_block(width, back=None):
    ratio = GROUP // HALO
    if back is None:
        return pl.BlockSpec((HALO, width), lambda g: (jnp.maximum(g * ratio - 1, 0), 0))
    return pl.BlockSpec((HALO, width), lambda g: (jnp.maximum((back - 1 - g) * ratio - 1, 0), 0))


def whole(shape):
    return pl.BlockSpec(shape, lambda g: (0,) * len(shape))


def delta_forward(pres, rims, convs, scal, rate, keep):
    tokens = scal.shape[0]
    heads, groups = (rate.shape[1], tokens // GROUP)
    widths = [pre.shape[1] for pre in pres]
    smem = pl.BlockSpec(memory_space=pltpu.SMEM)
    return pl.pallas_call(
        functools.partial(forward_kernel, heads, groups),
        grid=(groups,),
        in_specs=[smem]
        + [token_block(w) for w in widths]
        + [before_block(w) for w in widths]
        + [whole((HALO, w)) for w in widths]
        + [whole((CONV, w)) for w in widths]
        + [token_block(scal.shape[1]), whole(rate.shape)],
        out_specs=[token_block(w) for w in widths]
        + [
            pl.BlockSpec((1, heads * GROUP, WIDE), lambda g: (g, 0, 0)),
            token_block(heads * GROUP),
            pl.BlockSpec((1, heads * DK, WIDE), lambda g: (g, 0, 0)),
            token_block(heads * DK),
            token_block(heads * DV),
            whole((heads * DK, WIDE)),
        ],
        out_shape=[jax.ShapeDtypeStruct((tokens, w), bf16) for w in widths]
        + [
            jax.ShapeDtypeStruct((groups, heads * GROUP, WIDE), bf16),
            jax.ShapeDtypeStruct((tokens, heads * GROUP), bf16),
            jax.ShapeDtypeStruct((groups, heads * DK, WIDE), bf16),
            jax.ShapeDtypeStruct((tokens, heads * DK), bf16),
            jax.ShapeDtypeStruct((tokens, heads * DV), f32),
            jax.ShapeDtypeStruct((heads * DK, WIDE), f32),
        ],
        scratch_shapes=[pltpu.VMEM((heads * DK, WIDE), f32)]
        + [pltpu.VMEM((HALO + GROUP, w), f32) for w in widths],
        compiler_params=pltpu.CompilerParams(vmem_limit_bytes=VMEM),
        cost_estimate=pl.CostEstimate(flops=10**6, bytes_accessed=10**4, transcendentals=0),
        name="delta_forward",
    )(keep, *pres, *pres, *rims, *convs, scal, rate)


def backward_kernel(
    heads,
    groups,
    keep_ref,
    query_pre,
    key_pre,
    value_pre,
    query_before,
    key_before,
    value_before,
    query_rim,
    key_rim,
    value_rim,
    conv_query,
    conv_key,
    conv_value,
    scal_ref,
    rate_ref,
    query_ref,
    key_ref,
    value_ref,
    wu_ref,
    inverse_ref,
    state_ref,
    entry_ref,
    exit_ref,
    grad_ref,
    query_out,
    key_out,
    value_out,
    query_conv_out,
    key_conv_out,
    value_conv_out,
    query_back_out,
    key_back_out,
    value_back_out,
    query_tail_out,
    key_tail_out,
    value_tail_out,
    scal_out,
    rate_out,
    carry,
    ext_query,
    ext_key,
    ext_value,
    dy_query,
    dy_key,
    dy_value,
):
    step = pl.program_id(0)
    group = groups - 1 - step
    keep = keep_ref[group]

    @pl.when(step == 0)
    def _():
        carry[...] = exit_ref[...]
        for ref in (dy_query, dy_key, dy_value):
            ref[...] = jnp.zeros_like(ref)
        for ref in (query_conv_out, key_conv_out, value_conv_out, rate_out):
            ref[...] = jnp.zeros_like(ref)

    terms = token_terms(scal_ref, rate_ref, heads)
    valid = terms["valid"]
    beta, growth, closing = (terms["beta_column"], terms["growth"], terms["closing"])
    query = stacked(query_ref[...], heads)
    key = stacked(key_ref[...], heads)
    value = stacked(value_ref[...], heads)
    grad = stacked(grad_ref[...], heads)
    query_wide, key_wide = (query.astype(f32), key.astype(f32))
    scores = contract(jnp.concatenate([query, key], axis=0), key, 1, 1)
    mix = packed(scores[: heads * GROUP], heads)
    similar = packed(scores[heads * GROUP :], heads)
    ratio, betas, strict = (terms["ratio"], terms["betas"], terms["strict"])
    mixing = ratio * mix
    wu = wu_ref[0]
    grown_wide = growth * query_wide
    fading_wide = closing * key_wide
    grown = grown_wide.astype(bf16)
    fading = fading_wide.astype(bf16)
    mixed_back = contract(diagonal(mixing, heads), grad, 0, 0)
    fresh, d_fresh, d_grown, d_fading, d_weights, d_fades = ([], [], [], [], [], [])
    for h in range(heads):
        rows = slice(h * GROUP, (h + 1) * GROUP)
        states = pl.ds(h * DK, DK)
        pair = state_ref[0, states, :]
        used = pair[:, DK:].astype(f32) + contract(pair[:, :DK], entry_ref[states, :])
        used_low = used.astype(bf16)
        weights = wu[rows, :DK]
        part = (wu[rows, DK:].astype(f32) - contract(weights, used_low)).astype(bf16)
        after = carry[states, :]
        after_low = after.astype(bf16)
        d_part = mixed_back[rows] + contract(fading[rows], after_low)
        d_part_low = d_part.astype(bf16)
        stack = jnp.concatenate([grad[rows], d_part_low], axis=0)
        seen = contract(stack, used_low, 1, 1)
        d_grown.append(seen[:GROUP])
        d_weights.append(-seen[GROUP:])
        d_fading.append(contract(part, after_low, 1, 1))
        fade = terms["fades"][h]
        carry[states, :] = keep * (
            fade * after
            + contract(jnp.concatenate([grown[rows], -weights], axis=0), stack, 0, 0)
        )
        d_fade = jnp.sum(after * used, axis=0, keepdims=True)
        d_fades.append(fade * jnp.sum(d_fade, axis=1, keepdims=True))
        fresh.append(part)
        d_fresh.append(d_part_low)
    d_grown = jnp.concatenate(d_grown, axis=0)
    d_fading = jnp.concatenate(d_fading, axis=0)
    d_weights = jnp.concatenate(d_weights, axis=0).astype(bf16)
    d_fresh = jnp.concatenate(d_fresh, axis=0)
    d_mixing = packed(contract(grad, jnp.concatenate(fresh, axis=0), 1, 1), heads)
    d_right = contract(
        diagonal(inverse_ref[...], heads), jnp.concatenate([d_weights, d_fresh], axis=1), 0, 0
    )
    d_coupling = -packed(contract(d_right.astype(bf16), wu, 1, 1), heads)
    d_coupling = jnp.where(strict, d_coupling, 0.0)
    ratio_grad = ratio * d_coupling
    from_similar = diagonal(betas * ratio_grad, heads)
    from_mix = diagonal(ratio * d_mixing, heads)
    plain = contract(jnp.concatenate([from_mix, from_similar], axis=0), key)
    turned = contract(
        jnp.concatenate([from_similar, from_mix], axis=0),
        jnp.concatenate([key, query], axis=0),
        0,
        0,
    )
    count = heads * GROUP
    d_scaled = d_right[:, :DK]
    d_query = growth * d_grown + plain[:count]
    d_key = beta * growth * d_scaled + closing * d_fading + plain[count:] + turned
    d_value = beta * d_right[:, DK:]
    grown_key = growth * key_wide
    ratio_similar = ratio_grad * similar
    flows = betas * ratio_similar + mixing * d_mixing
    fading_flow = d_fading * fading_wide
    sum_growth = jnp.sum(
        d_grown * grown_wide + d_scaled * (beta * grown_key) - fading_flow, axis=1, keepdims=True
    )
    sum_fading = jnp.sum(fading_flow, axis=1, keepdims=True)
    value_flow = d_right[:, DK:] * value.astype(f32)
    sum_beta = jnp.sum(
        d_scaled * grown_key + value_flow[:, :DK] + value_flow[:, DK:], axis=1, keepdims=True
    )
    flow_high, flow_low = halves(flows)
    ones = jnp.full((GROUP, 128), 1.0, bf16)
    turned_flow = contract(
        jnp.concatenate([flow_high, flow_low], axis=0),
        jnp.concatenate([ones, ones], axis=0),
        0,
        0,
    )[:, :1]
    owner = lane_heads(heads)
    lane = lax.broadcasted_iota(jnp.int32, (GROUP, 128), 1)
    d_sums = jnp.zeros((GROUP, 128), f32)
    d_beta = jnp.zeros((GROUP, 128), f32)
    d_last = jnp.zeros((1, 128), f32)
    for h in range(heads):
        rows = slice(h * GROUP, (h + 1) * GROUP)
        flow = jnp.sum(jnp.where(owner == h, flows, 0.0), axis=1, keepdims=True)
        more = jnp.sum(jnp.where(owner == h, ratio_similar, 0.0), axis=1, keepdims=True)
        d_sums = jnp.where(lane == h, sum_growth[rows] + flow - turned_flow[rows], d_sums)
        d_beta = jnp.where(lane == h, sum_beta[rows] + more, d_beta)
        total = jnp.sum(sum_fading[rows], axis=0, keepdims=True) + d_fades[h]
        d_last = jnp.where(lane[:1] == h, total, d_last)
    square_row = lax.broadcasted_iota(jnp.int32, (GROUP, GROUP), 0)
    square_lane = lax.broadcasted_iota(jnp.int32, (GROUP, GROUP), 1)
    later = jnp.where(square_row <= square_lane, 1.0, 0.0)
    d_decay = (summed_rows(later, d_sums) + d_last)[:, :heads]
    d_beta = d_beta[:, :heads]
    d_alpha = -d_decay * terms["rate"] * jax.nn.sigmoid(terms["alpha"]) * valid
    d_beta = d_beta * terms["beta"] * (1.0 - terms["beta"])
    scal_out[...] = jnp.concatenate([d_alpha, d_beta], axis=1).astype(bf16)
    rate_out[0:1, :] += jnp.sum(d_decay * terms["decay"], axis=0, keepdims=True)
    rate_out[1:2, :] += jnp.sum(d_alpha, axis=0, keepdims=True)

    first = group == 0
    after_keep = jnp.where(step == 0, 0.0, keep_ref[jnp.minimum(group + 1, groups - 1)])
    sections = (
        (query_pre, query_before, query_rim, conv_query, ext_query, dy_query, DK, d_query),
        (key_pre, key_before, key_rim, conv_key, ext_key, dy_key, DK, d_key),
        (value_pre, value_before, value_rim, conv_value, ext_value, dy_value, DV, d_value),
    )
    outs = (
        (query_out, query_conv_out, query_back_out, query_tail_out),
        (key_out, key_conv_out, key_back_out, key_tail_out),
        (value_out, value_conv_out, value_back_out, value_tail_out),
    )
    for kind, (section, out) in enumerate(zip(sections, outs)):
        now_ref, before_ref, rim_ref, conv_ref, ext_ref, dy_ref, width, cotangent = section
        pre_out, conv_out, back_out, tail_out = out
        fill(ext_ref, now_ref, before_ref, rim_ref, first, keep)
        dy_ref[8 + GROUP :, :] = dy_ref[8:16, :] * after_keep
        for h in range(heads):
            lanes = pl.ds(h * width, width)
            rows = slice(h * GROUP, (h + 1) * GROUP)
            total = tap_sum(ext_ref, conv_ref, h * width, width)
            sigmoid = jax.nn.sigmoid(total)
            act = total * sigmoid
            d_act = cotangent[rows]
            if kind > 0:
                d_act = d_act * valid
            if kind < 2:
                scale = lax.rsqrt(jnp.sum(act * act, axis=1, keepdims=True) + epsilon_norm)
                inner = jnp.sum(act * d_act, axis=1, keepdims=True)
                d_act = scale * (d_act - act * (scale * scale * inner))
            if kind == 0:
                d_act = d_act * DK ** (-0.5)
            d_total = d_act * (sigmoid * (1.0 + total * (1.0 - sigmoid)))
            dy_ref[pl.ds(8, GROUP), lanes] = d_total
            for tap in range(CONV):
                product = d_total * ext_ref[pl.ds(HALO - tap, GROUP), lanes]
                conv_out[pl.ds(tap * 8, 8), lanes] += jnp.sum(
                    product.reshape(GROUP // 8, 8, width), axis=0
                )
            d_pre = d_total * conv_ref[0:1, lanes]
            for tap in range(1, CONV):
                d_pre = d_pre + dy_ref[pl.ds(8 + tap, GROUP), lanes] * conv_ref[tap : tap + 1, lanes]
            pre_out[:, lanes] = d_pre.astype(bf16)

            @pl.when(step == 0)
            def _():
                tail_out[:, lanes] = d_pre[GROUP - 8 :]

            @pl.when(first)
            def _():
                d_back = dy_ref[pl.ds(1, 8), lanes] * conv_ref[1:2, lanes]
                for tap in range(2, CONV):
                    d_back = d_back + dy_ref[pl.ds(tap, 8), lanes] * conv_ref[tap : tap + 1, lanes]
                back_out[:, lanes] = d_back * keep


def delta_backward(pres, rims, convs, scal, rate, keep, made, entry, exit_grad, grad):
    tokens = scal.shape[0]
    heads, groups = (rate.shape[1], tokens // GROUP)
    widths = [pre.shape[1] for pre in pres]
    smem = pl.BlockSpec(memory_space=pltpu.SMEM)
    turn = lambda *shape: pl.BlockSpec(shape, lambda g: (groups - 1 - g, 0, 0))
    columns = 2 * heads
    return pl.pallas_call(
        functools.partial(backward_kernel, heads, groups),
        grid=(groups,),
        in_specs=[smem]
        + [token_block(w, groups) for w in widths]
        + [before_block(w, groups) for w in widths]
        + [whole((HALO, w)) for w in widths]
        + [whole((CONV, w)) for w in widths]
        + [token_block(scal.shape[1], groups), whole(rate.shape)]
        + [token_block(w, groups) for w in widths]
        + [
            turn(1, heads * GROUP, WIDE),
            token_block(heads * GROUP, groups),
            turn(1, heads * DK, WIDE),
            whole((heads * DK, DV)),
            whole((heads * DK, DV)),
            token_block(heads * DV, groups),
        ],
        out_specs=[token_block(w, groups) for w in widths]
        + [whole((CONV * 8, w)) for w in widths]
        + [whole((8, w)) for w in widths]
        + [whole((8, w)) for w in widths]
        + [token_block(columns, groups), whole((8, heads))],
        out_shape=[jax.ShapeDtypeStruct((tokens, w), bf16) for w in widths]
        + [jax.ShapeDtypeStruct((CONV * 8, w), f32) for w in widths]
        + [jax.ShapeDtypeStruct((8, w), f32) for w in widths]
        + [jax.ShapeDtypeStruct((8, w), f32) for w in widths]
        + [
            jax.ShapeDtypeStruct((tokens, columns), bf16),
            jax.ShapeDtypeStruct((8, heads), f32),
        ],
        scratch_shapes=[pltpu.VMEM((heads * DK, DV), f32)]
        + [pltpu.VMEM((HALO + GROUP, w), f32) for w in widths]
        + [pltpu.VMEM((16 + GROUP, w), f32) for w in widths],
        compiler_params=pltpu.CompilerParams(vmem_limit_bytes=VMEM),
        cost_estimate=pl.CostEstimate(flops=10**6, bytes_accessed=10**4, transcendentals=0),
        name="delta_backward",
    )(keep, *pres, *pres, *rims, *convs, scal, rate, *made, entry, exit_grad, grad)


def gated_forward_kernel(heads, linear_ref, local_ref, gate_ref, entry_ref, gain_ref, gated_out):
    for h in range(heads):
        wide = pl.ds(h * DV, DV)
        out = local_ref[:, wide] + contract(
            linear_ref[:, pl.ds(h * DK, DK)], entry_ref[pl.ds(h * DK, DK), :]
        )
        scale = lax.rsqrt(jnp.mean(out * out, axis=1, keepdims=True) + epsilon_gate)
        gate = gate_ref[:, wide]
        gated_out[:, wide] = (out * scale * gain_ref[...] * jax.nn.silu(gate)).astype(bf16)


def row_block(rows, width):
    return pl.BlockSpec((rows, width), lambda g: (g, 0))


def gated_forward(linear, local, gate, entry, gain):
    tokens, heads = (local.shape[0], local.shape[1] // DV)
    rows = 2 * GROUP
    return pl.pallas_call(
        functools.partial(gated_forward_kernel, heads),
        grid=(tokens // rows,),
        in_specs=[
            row_block(rows, heads * DK),
            row_block(rows, heads * DV),
            row_block(rows, heads * DV),
            whole((heads * DK, DV)),
            whole((1, DV)),
        ],
        out_specs=row_block(rows, heads * DV),
        out_shape=jax.ShapeDtypeStruct((tokens, heads * DV), bf16),
        compiler_params=pltpu.CompilerParams(vmem_limit_bytes=SMALL),
        cost_estimate=pl.CostEstimate(flops=10**9, bytes_accessed=10**7, transcendentals=0),
        name="gated_forward",
    )(linear, local, gate, entry, gain[None, :])


def gated_backward_kernel(
    heads,
    linear_ref,
    local_ref,
    gate_ref,
    entry_ref,
    gain_ref,
    grad_ref,
    valid_ref,
    delta_out,
    gate_out,
    gain_out,
    entry_out,
):
    @pl.when(pl.program_id(0) == 0)
    def _():
        gain_out[...] = jnp.zeros_like(gain_out)
        entry_out[...] = jnp.zeros_like(entry_out)

    rows = local_ref.shape[0]
    for h in range(heads):
        wide = pl.ds(h * DV, DV)
        linear = linear_ref[:, pl.ds(h * DK, DK)]
        out = local_ref[:, wide] + contract(linear, entry_ref[pl.ds(h * DK, DK), :])
        scale = lax.rsqrt(jnp.mean(out * out, axis=1, keepdims=True) + epsilon_gate)
        unit = out * scale
        gate = gate_ref[:, wide]
        sigmoid = jax.nn.sigmoid(gate)
        grad = grad_ref[:, wide]
        silu = gate * sigmoid
        product = grad * unit
        gain_out[...] += jnp.sum((product * silu).reshape(rows // 8, 8, DV), axis=0)
        gate_out[:, wide] = (
            product * gain_ref[...] * (sigmoid * (1.0 + gate * (1.0 - sigmoid)))
        ).astype(bf16)
        d_unit = grad * gain_ref[...] * silu
        inner = jnp.mean(d_unit * unit, axis=1, keepdims=True)
        delta = (scale * (d_unit - unit * inner) * valid_ref[...]).astype(bf16)
        delta_out[:, wide] = delta
        entry_out[pl.ds(h * DK, DK), :] += contract(linear, delta, 0, 0)


def gated_backward(linear, local, gate, entry, gain, grad, valid):
    tokens, heads = (local.shape[0], local.shape[1] // DV)
    rows = 2 * GROUP
    return pl.pallas_call(
        functools.partial(gated_backward_kernel, heads),
        grid=(tokens // rows,),
        in_specs=[
            row_block(rows, heads * DK),
            row_block(rows, heads * DV),
            row_block(rows, heads * DV),
            whole((heads * DK, DV)),
            whole((1, DV)),
            row_block(rows, heads * DV),
            row_block(rows, 1),
        ],
        out_specs=[
            row_block(rows, heads * DV),
            row_block(rows, heads * DV),
            whole((8, DV)),
            whole((heads * DK, DV)),
        ],
        out_shape=[
            jax.ShapeDtypeStruct((tokens, heads * DV), bf16),
            jax.ShapeDtypeStruct((tokens, heads * DV), bf16),
            jax.ShapeDtypeStruct((8, DV), f32),
            jax.ShapeDtypeStruct((heads * DK, DV), f32),
        ],
        compiler_params=pltpu.CompilerParams(vmem_limit_bytes=SMALL),
        cost_estimate=pl.CostEstimate(flops=10**6, bytes_accessed=10**4, transcendentals=0),
        name="gated_backward",
    )(linear, local, gate, entry, gain[None, :], grad, valid[:, None])


def column_place(tile, tiles, place):
    block, inner = (tile // (tiles // 4), tile % (tiles // 4))
    core = jnp.where(block < 2, 1 - place % 2, place % 2)
    chip = jnp.where(block % 2 == 0, 1 - place // 2, place // 2)
    return (chip * 2 + core) * (tiles // 4) + inner


def plain_dense_kernel(place_ref, left_ref, right_ref, out_ref):
    left = left_ref[:, : right_ref.shape[0]]
    out_ref[...] = contract(left, right_ref[...]).astype(bf16)


def plain_dense(left, right, place, tile=256):
    rows, cols = (left.shape[0], right.shape[1])
    tiles = cols // tile
    return pl.pallas_call(
        plain_dense_kernel,
        grid_spec=pltpu.PrefetchScalarGridSpec(
            num_scalar_prefetch=1,
            grid=(tiles,),
            in_specs=[
                pl.BlockSpec(left.shape, lambda i, place: (0, 0)),
                pl.BlockSpec(
                    (right.shape[0], tile), lambda i, place: (0, column_place(i, tiles, place[0]))
                ),
            ],
            out_specs=pl.BlockSpec((rows, tile), lambda i, place: (0, i)),
        ),
        out_shape=jax.ShapeDtypeStruct((rows, cols), bf16),
        compiler_params=pltpu.CompilerParams(vmem_limit_bytes=SMALL),
        cost_estimate=pl.CostEstimate(
            flops=2 * rows * cols * left.shape[1], bytes_accessed=10**7, transcendentals=0
        ),
        name="plain_dense",
    )(place, left, right)


def norm_dense_kernel(sides, place_ref, *refs):
    count = len(sides)
    lefts, rights = (refs[:count], refs[count : 2 * count])
    rows_ref, scale_ref, gain_ref, out_ref, gain_out, dots_out = refs[2 * count :]
    total = 0.0
    for left, right, side in zip(lefts, rights, sides):
        total = total + contract(left[:, : right.shape[side]], right[...], 1, side)
    out_ref[...] = total.astype(bf16)
    weighted = total * (rows_ref[...].astype(f32) * scale_ref[...])
    gain_out[...] = jnp.sum(weighted, axis=0, keepdims=True)
    dots = jnp.sum(weighted * gain_ref[...], axis=1, keepdims=True)

    @pl.when(pl.program_id(0) == 0)
    def _():
        dots_out[...] = dots

    @pl.when(pl.program_id(0) > 0)
    def _():
        dots_out[...] += dots


def norm_dense(pairs, rows, scale, gain, place, tile=256):
    tokens, cols = rows.shape
    tiles = cols // tile
    lefts, rights = ([left for left, _ in pairs], [right for _, right in pairs])
    placed = lambda i, place: (0, column_place(i, tiles, place[0]))
    upright = lambda i, place: (column_place(i, tiles, place[0]), 0)
    sides = [1 if right.shape[0] == cols else 0 for right in rights]
    return pl.pallas_call(
        functools.partial(norm_dense_kernel, sides),
        grid_spec=pltpu.PrefetchScalarGridSpec(
            num_scalar_prefetch=1,
            grid=(tiles,),
            in_specs=[pl.BlockSpec(left.shape, lambda i, place: (0, 0)) for left in lefts]
            + [
                pl.BlockSpec((tile, right.shape[1]), upright)
                if side
                else pl.BlockSpec((right.shape[0], tile), placed)
                for right, side in zip(rights, sides)
            ]
            + [
                pl.BlockSpec((tokens, tile), placed),
                pl.BlockSpec((tokens, 1), lambda i, place: (0, 0)),
                pl.BlockSpec((1, tile), placed),
            ],
            out_specs=[
                pl.BlockSpec((tokens, tile), lambda i, place: (0, i)),
                pl.BlockSpec((1, tile), placed),
                pl.BlockSpec((tokens, 1), lambda i, place: (0, 0)),
            ],
        ),
        out_shape=[
            jax.ShapeDtypeStruct((tokens, cols), bf16),
            jax.ShapeDtypeStruct((1, cols), f32),
            jax.ShapeDtypeStruct((tokens, 1), f32),
        ],
        compiler_params=pltpu.CompilerParams(vmem_limit_bytes=VMEM),
        cost_estimate=pl.CostEstimate(
            flops=2 * tokens * cols * sum(left.shape[1] for left in lefts),
            bytes_accessed=2 * 10**7,
            transcendentals=0,
        ),
        name="norm_dense",
    )(place, *lefts, *rights, rows, scale, gain[None, :])


def shifted(block, axis, distance):
    devices = range(lax.axis_size(axis))
    route = [(i - distance, i) for i in devices if i - distance in devices]
    return lax.ppermute(block, axis, route)


def exchanged(block, axis, bit):
    route = [(i, i ^ bit) for i in range(lax.axis_size(axis))]
    return lax.ppermute(block, axis, route)


def half(block, axis, at, count):
    width = block.shape[axis] // count
    return lax.dynamic_slice_in_dim(block, at * width, width, axis)


def weight_grad_kernel(turned, place_ref, rows_ref, got_rows_ref, cols_ref, got_cols_ref, out_ref):
    if turned:
        total = contract(cols_ref[...], rows_ref[...], 0, 0)
        total = total + contract(got_cols_ref[...], got_rows_ref[...], 0, 0)
        total = total[: out_ref.shape[0]]
    else:
        total = contract(rows_ref[...], cols_ref[...], 0, 0)
        total = total + contract(got_rows_ref[...], got_cols_ref[...], 0, 0)
    out_ref[...] = total.astype(bf16)


def pair_grad(rows, got_rows, cols, got_cols, turned, kept=None):
    odd = lax.axis_index("seq").astype(jnp.int32) % 2
    devices = lax.axis_size("seq")
    tokens, padded = cols.shape
    count = padded if kept is None else kept
    width = rows.shape[1] // devices
    if width % 128:
        part = jnp.concatenate([own_half(rows, odd, width), got_rows], axis=0)
        cols = jnp.concatenate([cols, got_cols], axis=0)[:, :count]
        if turned:
            part = part.reshape(2 * tokens, devices // 2, width)
            total = jnp.einsum("tn,tcw->cnw", cols, part, preferred_element_type=f32)
            return total.reshape(devices // 2 * count, width).astype(bf16)
        return dense(part.T, cols).astype(bf16)
    block = (count, width) if turned else (width, count)
    still = pl.BlockSpec((tokens, padded), lambda i, place: (0, 0))
    return pl.pallas_call(
        functools.partial(weight_grad_kernel, turned),
        grid_spec=pltpu.PrefetchScalarGridSpec(
            num_scalar_prefetch=1,
            grid=(devices // 2,),
            in_specs=[
                pl.BlockSpec((tokens, width), lambda i, place: (0, 2 * i + place[0])),
                pl.BlockSpec((tokens, width), lambda i, place: (0, i)),
                still,
                still,
            ],
            out_specs=pl.BlockSpec(block, lambda i, place: (i, 0)),
        ),
        out_shape=jax.ShapeDtypeStruct((devices // 2 * block[0], block[1]), bf16),
        compiler_params=pltpu.CompilerParams(vmem_limit_bytes=SMALL),
        cost_estimate=pl.CostEstimate(
            flops=2 * tokens * count * rows.shape[1], bytes_accessed=10**7, transcendentals=0
        ),
        name="weight_grad",
    )(odd[None], rows, got_rows, cols, got_cols)


def partner_rows(block):
    width = block.shape[1] * 4 // lax.axis_size("seq")
    odd = lax.axis_index("seq") % 2
    if block.shape[1] == 2 * width:
        part = half(block, 1, 1 - odd, 2)
    else:
        part = own_half(block, 1 - odd, width)
    return exchanged(part, "seq", 1)


def gather_kernel(norm, place_ref, *refs):
    blocks = [ref[...] for ref in refs[:4]]
    width = blocks[0].shape[1]
    place = place_ref[0]
    out_ref = refs[5] if norm else refs[4]
    spots = [pl.ds(pl.multiple_of((place ^ at) * width, 128), width) for at in range(4)]
    for block, spot in zip(blocks, spots):
        out_ref[:, spot] = block
    if norm:
        gain_ref, normed_out, scale_out = (refs[4], refs[6], refs[7])
        wides = [block.astype(f32) for block in blocks]
        total = sum(jnp.sum(wide * wide, axis=1, keepdims=True) for wide in wides)
        scale = lax.rsqrt(total / (4 * width) + epsilon_norm)
        scale_out[...] = scale
        for wide, spot in zip(wides, spots):
            normed_out[:, spot] = (wide * scale * gain_ref[:, spot]).astype(bf16)


def head_gathered(block, gain=None):
    place = lax.axis_index("head").astype(jnp.int32)
    tokens, width = block.shape
    across = exchanged(block, "head", 2)
    beside = exchanged(block, "head", 1)
    corner = exchanged(across, "head", 1)
    rows = 4 * GROUP
    norm = gain is not None
    spec = lambda cols: pl.BlockSpec((rows, cols), lambda i, place: (i, 0))
    whole_shape = jax.ShapeDtypeStruct((tokens, 4 * width), bf16)
    out_specs, out_shape = (spec(4 * width), whole_shape)
    if norm:
        out_specs = [out_specs, spec(4 * width), spec(1)]
        out_shape = [whole_shape, whole_shape, jax.ShapeDtypeStruct((tokens, 1), f32)]
    gain_spec = pl.BlockSpec((1, 4 * width), lambda i, place: (0, 0))
    return pl.pallas_call(
        functools.partial(gather_kernel, norm),
        grid_spec=pltpu.PrefetchScalarGridSpec(
            num_scalar_prefetch=1,
            grid=(tokens // rows,),
            in_specs=[spec(width)] * 4 + ([gain_spec] if norm else []),
            out_specs=out_specs,
        ),
        out_shape=out_shape,
        compiler_params=pltpu.CompilerParams(vmem_limit_bytes=SMALL),
        cost_estimate=pl.CostEstimate(flops=10**6, bytes_accessed=6 * 10**6, transcendentals=0),
        name="gather",
    )(place[None], block, beside, across, corner, *([gain[None, :]] if norm else []))


def rows_dense_kernel(left_ref, right_ref, out_ref):
    out_ref[...] = contract(left_ref[...], right_ref[...], 1, 1)


def rows_dense(left, right):
    tokens, rows = (left.shape[0], 4 * GROUP)
    return pl.pallas_call(
        rows_dense_kernel,
        grid=(tokens // rows,),
        in_specs=[row_block(rows, left.shape[1]), whole(right.shape)],
        out_specs=row_block(rows, right.shape[0]),
        out_shape=jax.ShapeDtypeStruct((tokens, right.shape[0]), f32),
        compiler_params=pltpu.CompilerParams(vmem_limit_bytes=SMALL),
        cost_estimate=pl.CostEstimate(
            flops=2 * left.size * right.shape[0], bytes_accessed=10**7, transcendentals=0
        ),
        name="rows_dense",
    )(left, right)


def ffn_kernel(normed_ref, gate_ref, up_ref, grad_ref, inner_out, d_gate_out, d_up_out):
    normed = normed_ref[...]
    gate = contract(normed, gate_ref[...], 1, 1)
    up = contract(normed, up_ref[...], 1, 1)
    sigmoid = jax.nn.sigmoid(gate)
    silu = gate * sigmoid
    grad = grad_ref[...]
    padding = inner_out.shape[1] - gate.shape[1]
    for ref, values in (
        (inner_out, silu * up),
        (d_gate_out, grad * up * (sigmoid * (1.0 + gate * (1.0 - sigmoid)))),
        (d_up_out, grad * silu),
    ):
        values = values.astype(bf16)
        if padding:
            values = jnp.pad(values, ((0, 0), (0, padding)))
        ref[...] = values


def ffn(normed, w_gate, w_up, grad):
    tokens, count = grad.shape
    rows, padded = (4 * GROUP, -(-count // 128) * 128)
    return pl.pallas_call(
        ffn_kernel,
        grid=(tokens // rows,),
        in_specs=[row_block(rows, normed.shape[1])]
        + [whole(w_gate.shape)] * 2
        + [row_block(rows, count)],
        out_specs=[row_block(rows, padded)] * 3,
        out_shape=[jax.ShapeDtypeStruct((tokens, padded), bf16)] * 3,
        compiler_params=pltpu.CompilerParams(vmem_limit_bytes=VMEM),
        cost_estimate=pl.CostEstimate(
            flops=4 * normed.size * count, bytes_accessed=2 * 10**7, transcendentals=0
        ),
        name="ffn",
    )(normed, w_gate, w_up, grad)


def tied(*values):
    return lax.optimization_barrier(values)


def head_scattered(partial):
    width = partial.shape[1] // 2
    mine = partial[:, width:].astype(f32) + exchanged(partial[:, :width], "head", 1).astype(f32)
    width = width // 2
    return mine[:, width:] + exchanged(mine[:, :width].astype(bf16), "head", 2).astype(f32)


def head_summed(values):
    bit = 1
    while bit < lax.axis_size("head"):
        values = values + exchanged(values, "head", bit)
        bit = bit * 2
    return values


def all_summed(values):
    values = head_summed(values)
    bit = 1
    while bit < lax.axis_size("seq"):
        values = values + exchanged(values, "seq", bit)
        bit = bit * 2
    return values


def own_half(rows, odd, width):
    tokens, total = rows.shape
    parts = rows.reshape(tokens, total // (2 * width), 2, width)
    return lax.dynamic_index_in_dim(parts, odd, 2, False).reshape(tokens, total // 2)


def seq_scattered(mine):
    devices = lax.axis_size("seq")
    groups = [list(range(first, devices, 2)) for first in range(2)]
    return lax.psum_scatter(
        mine.astype(bf16), "seq", scatter_dimension=0, axis_index_groups=groups, tiled=True
    ).astype(f32)


def line_step(send, step, planes, upward):
    devices = 2 * planes
    route = []
    for i in range(devices):
        plane = i // 2
        if upward and plane < step and plane + 1 < planes:
            route.append((i, i + 2))
        if not upward and planes - 1 - plane < step and plane > 0:
            route.append((i, i - 2))
    return lax.ppermute(send, "seq", route)


def line_scattered(kept):
    planes = lax.axis_size("seq") // 2
    if planes > 4:
        return seq_scattered(kept)
    plane = lax.axis_index("seq") // 2
    rows = kept.shape[0] // planes

    def chunk(at):
        return lax.dynamic_slice_in_dim(kept, at * rows, rows, 0).astype(f32)

    up, down = (None, None)
    for step in range(1, planes):
        to_up = chunk(jnp.minimum(plane + planes - step, planes - 1))
        to_down = chunk(jnp.maximum(plane - planes + step, 0))
        if up is not None:
            to_up, to_down = (to_up + up.astype(f32), to_down + down.astype(f32))
        up = line_step(to_up.astype(bf16), step, planes, True)
        down = line_step(to_down.astype(bf16), step, planes, False)
    return chunk(plane) + up.astype(f32) + down.astype(f32)


def composed(later, before):
    moved = jnp.einsum(
        "hij,hjk->hik", later[:, :, :DK].astype(bf16), before, preferred_element_type=f32
    )
    linear = moved.shape[2] - DV
    offset = later[:, :, DK:] + moved[:, :, linear:]
    return jnp.concatenate([moved[:, :, :linear], offset], axis=2)


def prefix(pair, got, direction):
    odd = lax.axis_index("seq") % 2
    front = odd == 1 if direction == 1 else odd == 0
    wide = got.astype(f32)
    low = pair.astype(bf16)
    closed = composed(jnp.where(front, pair, wide), jnp.where(front, got, low))
    distance = 2
    before = shifted(closed.astype(bf16), "seq", direction * distance)
    opened = before.astype(f32)
    while True:
        closed = composed(closed, before)
        distance = distance * 2
        last = distance * 2 >= lax.axis_size("seq")
        sent = closed[:, :, DK:] if last else closed
        before = shifted(sent.astype(bf16), "seq", direction * distance)
        opened = composed(opened, before)
        if last:
            break
    opened = opened[:, :, -DV:]
    moved = composed(wide, opened.astype(bf16))[:, :, -DV:]
    return jnp.where(front, moved, opened)


def layout(lengths, positions):
    padded = (lengths + (GROUP - 1)) // GROUP * GROUP
    seq_ends = jnp.cumsum(padded)
    begins = seq_ends - padded
    offset = positions[:, None] - begins[None, :]
    inside = (offset >= 0) & (positions[:, None] < seq_ends[None, :])
    valid_mask = jnp.any(inside & (offset < lengths[None, :]), axis=1).astype(jnp.float32)
    starts = jnp.any(offset == 0, axis=1).astype(jnp.float32)
    return (valid_mask, starts)


def dense(left, right):
    return jnp.dot(left, right, preferred_element_type=jnp.float32)


def shards(
    hidden_in,
    lengths,
    attn_gain,
    w_query,
    w_key,
    w_value,
    w_gate,
    w_alpha,
    w_beta,
    conv_query,
    conv_key,
    conv_value,
    decay_log,
    decay_bias,
    out_gain,
    w_out,
    ffn_gain,
    w_ffn_gate,
    w_ffn_up,
    w_ffn_down,
    grad_out,
):
    token_rows = hidden_in.shape[0]
    head_count = w_alpha.shape[1]
    col_width = grad_out.shape[1]
    devices = lax.axis_size("seq")
    positions = lax.axis_index("seq") * token_rows + jnp.arange(token_rows, dtype=jnp.int32)
    valid_mask, starts = layout(lengths, positions)
    keep_flags = 1.0 - starts[::GROUP]
    head_place = lax.axis_index("head")
    place = head_place[None].astype(jnp.int32)
    head_first = head_place * head_count
    col_first = head_place * col_width
    cols = lambda rows: lax.dynamic_slice_in_dim(rows, col_first, col_width, rows.ndim - 1)
    local_log = lax.dynamic_slice_in_dim(decay_log, head_first, head_count)
    local_bias = lax.dynamic_slice_in_dim(decay_bias, head_first, head_count)

    inputs32 = hidden_in.astype(f32)
    attn_scale = lax.rsqrt(jnp.mean(inputs32 * inputs32, axis=-1, keepdims=True) + epsilon_norm)
    normed = (inputs32 * attn_scale * attn_gain).astype(bf16)
    pres = [dense(normed, weight).astype(bf16) for weight in (w_query, w_key, w_value)]
    widths = [pre.shape[1] for pre in pres]
    edges = [0, widths[0], widths[0] + widths[1], sum(widths)]
    split = lambda rows: [rows[:, a:b] for a, b in zip(edges[:-1], edges[1:])]
    tail_first = token_rows - (CONV - 1)
    rims = shifted(jnp.concatenate([pre[tail_first:] for pre in pres], 1), "seq", 1)
    rims, grad_cols, normed_cols = tied(rims, grad_out, cols(normed))
    got_grad_rows = head_gathered(partner_rows(grad_cols))
    got_normed = head_gathered(partner_rows(normed_cols))
    rims = split(jnp.pad(rims, ((HALO - (CONV - 1), 0), (0, 0))))
    w_scal = jnp.concatenate([w_alpha, w_beta], axis=1)
    scal = jnp.concatenate([dense(normed, w_scal), valid_mask[:, None]], axis=1)
    rate = jnp.stack([jnp.exp(local_log), local_bias])
    convs = [conv_query, conv_key, conv_value]
    *made, linear, local, device_pair = delta_forward(
        pres, rims, convs, scal, rate, keep_flags
    )
    grad_rows = head_gathered(grad_out)
    device_pair, grad_rows = tied(device_pair, grad_rows)
    device_pair = device_pair.reshape(head_count, DK, WIDE)
    got_pair = exchanged(device_pair.astype(bf16), "seq", 1)
    entry = prefix(device_pair, got_pair, 1).astype(bf16).reshape(head_count * DK, DV)
    gate_pre = dense(normed, w_gate)
    d_inner = rows_dense(grad_rows, w_ffn_down)
    entry, d_inner, gate_pre, got_grad_rows, got_normed = tied(
        entry, d_inner, gate_pre, got_grad_rows, got_normed
    )
    gated = gated_forward(linear, local, gate_pre, entry, out_gain)
    mixed = head_scattered(plain_dense(gated, w_out, place))
    middle = cols(hidden_in).astype(f32) + mixed
    sent, normed_ffn, ffn_scale = head_gathered(middle.astype(bf16), ffn_gain)
    got_gated = exchanged(gated, "seq", 1)
    d_inner, got_gated = tied(d_inner, got_gated)
    inner_act, d_ffn_gate, d_ffn_up = ffn(normed_ffn, w_ffn_gate.T, w_ffn_up.T, d_inner)
    ffn_out = head_scattered(plain_dense(inner_act, w_ffn_down, place))
    hidden_out = (middle + ffn_out).astype(bf16)
    units = w_ffn_gate.shape[1]
    got_ffn_cols = partner_rows(cols(normed_ffn))
    inner_sent, got_ffn_cols = tied(inner_act, got_ffn_cols)
    got_inner = exchanged(inner_sent, "seq", 1)
    got_normed_ffn = head_gathered(got_ffn_cols)
    d_normed_ffn, grad_ffn_gain, ffn_dots = norm_dense(
        [(d_ffn_gate, w_ffn_gate.T), (d_ffn_up, w_ffn_up.T)], sent, ffn_scale, ffn_gain, place
    )
    ffn_dots = head_summed(ffn_dots[:, 0])[:, None] / sent.shape[1]
    d_sent_cols = ffn_scale * (
        cols(ffn_gain) * head_scattered(d_normed_ffn)
        - cols(sent).astype(f32) * ffn_scale * ffn_dots
    )
    d_middle = grad_out.astype(f32) + d_sent_cols
    d_mixed = head_gathered(d_middle.astype(bf16))
    d_gated = dense(d_mixed, w_out.T)
    got_mixed_cols = partner_rows(d_middle.astype(bf16))
    d_gate_sent, got_inner, got_mixed_cols = tied(d_ffn_gate, got_inner, got_mixed_cols)
    got_d_gate = exchanged(d_gate_sent, "seq", 1)
    got_d_mixed = head_gathered(got_mixed_cols)
    kept_down = pair_grad(grad_rows, got_grad_rows, inner_act, got_inner, True, units)
    d_gated, kept_down, got_normed_ffn = tied(d_gated, kept_down, got_normed_ffn)
    grad_w_ffn_down = seq_scattered(kept_down)
    d_delta, d_gate_pre, gain_part, entry_grad = gated_backward(
        linear, local, gate_pre, entry, out_gain, d_gated, valid_mask
    )
    back_pair = jnp.concatenate(
        [
            jnp.swapaxes(device_pair[:, :, :DK], 1, 2),
            entry_grad.reshape(head_count, DK, DV),
        ],
        axis=2,
    )
    kept_gate = pair_grad(normed_ffn, got_normed_ffn, d_ffn_gate, got_d_gate, True, units)
    got_back = exchanged(back_pair.astype(bf16), "seq", 1)
    d_ffn_up, d_gate_pre, got_back = tied(d_ffn_up, d_gate_pre, got_back)
    got_d_up = exchanged(d_ffn_up, "seq", 1)
    got_d_gate_pre = exchanged(d_gate_pre, "seq", 1)
    kept_out = pair_grad(d_mixed, got_d_mixed, gated, got_gated, True)
    exit_grad = prefix(back_pair, got_back, -1).reshape(head_count * DK, DV)
    exit_grad, kept_gate, kept_out, grad_w_ffn_down, hidden_out = tied(
        exit_grad, kept_gate, kept_out, grad_w_ffn_down, hidden_out
    )
    grad_w_ffn_gate = seq_scattered(kept_gate)
    grad_w_out = seq_scattered(kept_out)
    results = delta_backward(
        pres, rims, convs, scal, rate, keep_flags, made, entry, exit_grad, d_delta
    )
    d_pres, conv_parts, backs, tails = (results[i : i + 3] for i in range(0, 12, 3))
    d_scal, d_rate = results[12:]
    backs = shifted(jnp.concatenate(backs, 1)[8 - (CONV - 1) :], "seq", -1)
    tails = split(jnp.concatenate(tails, 1) + jnp.pad(backs, ((8 - (CONV - 1), 0), (0, 0))))
    d_query_pre, d_key_pre, d_value_pre = [
        lax.dynamic_update_slice(d_pre, tail.astype(bf16), (token_rows - 8, 0))
        for d_pre, tail in zip(d_pres, tails)
    ]
    d_query_pre, d_key_pre, d_value_pre, d_scal, got_d_up, got_d_gate_pre = tied(
        d_query_pre, d_key_pre, d_value_pre, d_scal, got_d_up, got_d_gate_pre
    )
    kept_up = pair_grad(normed_ffn, got_normed_ffn, d_ffn_up, got_d_up, True, units)
    kept_w_gate = pair_grad(normed, got_normed, d_gate_pre, got_d_gate_pre, False)
    got_last = [exchanged(d_pre, "seq", 1) for d_pre in (d_query_pre, d_key_pre, d_value_pre)]
    small = dense(normed.T, d_scal)
    small = [part.reshape(devices, -1) for part in (small[:, :head_count], small[:, head_count:])]
    for part in conv_parts:
        part = jnp.sum(part.reshape(CONV, 8, -1), axis=1).reshape(CONV, devices, -1)
        small.append(jnp.swapaxes(part, 0, 1).reshape(devices, -1))
    small = jnp.concatenate(small, axis=1)
    small_width = small.shape[1]
    odd = lax.axis_index("seq") % 2
    small = small.astype(bf16).reshape(devices // 2, 2, small_width // 128, 128)
    got = exchanged(lax.dynamic_index_in_dim(small, 1 - odd, 1, False), "seq", 1)
    small = lax.dynamic_index_in_dim(small, odd, 1, False).astype(f32) + got.astype(f32)
    small = seq_scattered(small.reshape(devices * small_width // 256, 128)).reshape(small_width)
    small_pieces = []
    for rows, width in [(normed.shape[1] // devices, head_count)] * 2 + [
        (CONV, width // devices) for width in widths
    ]:
        small_pieces.append(small[: rows * width].reshape(rows, width))
        small = small[rows * width :]
    d_normed, grad_attn_gain, attn_dots = norm_dense(
        [
            (d_query_pre, w_query),
            (d_key_pre, w_key),
            (d_value_pre, w_value),
            (d_gate_pre, w_gate),
            (d_scal, w_scal),
        ],
        hidden_in,
        attn_scale,
        attn_gain,
        place,
    )
    d_normed, kept_up, kept_w_gate, grad_w_ffn_gate, *got_last[:2] = tied(
        d_normed, kept_up, kept_w_gate, grad_w_ffn_gate, *got_last[:2]
    )
    grad_w_ffn_up = seq_scattered(kept_up)
    grad_w_gate = seq_scattered(kept_w_gate)
    kept_last = [
        pair_grad(normed, got_normed, d_pre, got, False)
        for d_pre, got in zip((d_query_pre, d_key_pre, d_value_pre), got_last)
    ]
    d_normed = head_scattered(d_normed)
    grad_w_query, grad_w_key, grad_w_value = [line_scattered(kept) for kept in kept_last]
    attn_dots = head_summed(attn_dots[:, 0])[:, None] / hidden_in.shape[1]
    grad_in = d_middle + attn_scale * (
        cols(attn_gain) * d_normed
        - cols(hidden_in).astype(f32) * attn_scale * attn_dots
    )
    full_log = lax.dynamic_update_slice_in_dim(
        jnp.zeros(decay_log.shape, f32), d_rate[0], head_first, 0
    )
    full_bias = lax.dynamic_update_slice_in_dim(
        jnp.zeros(decay_bias.shape, f32), d_rate[1], head_first, 0
    )
    sums = all_summed(
        jnp.concatenate(
            [jnp.sum(gain_part, 0), grad_ffn_gain[0], grad_attn_gain[0], full_log, full_bias]
        )
    )
    gain_first = out_gain.shape[0]
    attn_first = gain_first + ffn_gain.shape[0]
    log_first = attn_first + attn_gain.shape[0]
    bias_first = log_first + decay_log.shape[0]
    rows_of = lambda whole: half(whole, 0, lax.axis_index("seq"), devices)
    return (
        hidden_out,
        grad_in,
        rows_of(sums[attn_first:log_first]),
        grad_w_query,
        grad_w_key,
        grad_w_value,
        grad_w_gate,
        *small_pieces,
        sums[log_first:bias_first],
        sums[bias_first:],
        sums[:gain_first],
        grad_w_out,
        rows_of(sums[gain_first:attn_first]),
        grad_w_ffn_gate.T,
        grad_w_ffn_up.T,
        grad_w_ffn_down,
    )


def solution(mesh):
    return jax.shard_map(
        shards,
        mesh=mesh,
        in_specs=(
            P("seq", None),
            P(),
            P(),
            P(None, "head"),
            P(None, "head"),
            P(None, "head"),
            P(None, "head"),
            P(None, "head"),
            P(None, "head"),
            P(None, "head"),
            P(None, "head"),
            P(None, "head"),
            P(),
            P(),
            P(),
            P("head", None),
            P(),
            P(None, "head"),
            P(None, "head"),
            P("head", None),
            P("seq", "head"),
        ),
        out_specs=(
            P("seq", "head"),
            P("seq", "head"),
            P("seq"),
            P("seq", "head"),
            P("seq", "head"),
            P("seq", "head"),
            P("seq", "head"),
            P("seq", "head"),
            P("seq", "head"),
            P(None, ("head", "seq")),
            P(None, ("head", "seq")),
            P(None, ("head", "seq")),
            P(),
            P(),
            P(),
            P("head", "seq"),
            P("seq"),
            P("seq", "head"),
            P("seq", "head"),
            P("head", "seq"),
        ),
        check_vma=False,
    )
```

```python
import functools

import jax
import jax.numpy as jnp
from jax import lax
from jax.experimental import pallas as pl
from jax.experimental.pallas import tpu as pltpu
from jax.sharding import PartitionSpec as P

DK = 128
DV = 256
GROUP = 64
CONV = 4
HALO = 16
WIDE = DK + DV
VMEM = 60 * 2**20
SMALL = 30 * 2**20

epsilon_norm = 1e-06
epsilon_gate = 1e-05

f32 = jnp.float32
bf16 = jnp.bfloat16


def contract(left, right, left_dim=1, right_dim=0):
    return lax.dot_general(
        left, right, (((left_dim,), (right_dim,)), ((), ())), preferred_element_type=f32
    )


def lane_heads(heads):
    return lax.broadcasted_iota(jnp.int32, (1, heads * GROUP), 1) // GROUP


def packed(full, heads):
    owner = lane_heads(heads)
    result = full[:GROUP]
    for head in range(1, heads):
        result = jnp.where(owner == head, full[head * GROUP : (head + 1) * GROUP], result)
    return result


def diagonal(values, heads):
    owner = lane_heads(heads)
    low = values.astype(bf16)
    return jnp.concatenate(
        [low * jnp.where(owner == head, 1.0, 0.0).astype(bf16) for head in range(heads)], axis=0
    )


def spread(columns, heads):
    owner = lane_heads(heads)
    result = jnp.broadcast_to(columns[0], (GROUP, heads * GROUP))
    for head in range(1, heads):
        result = jnp.where(owner == head, columns[head], result)
    return result


def halves(values):
    high = values.astype(bf16)
    return high, (values - high.astype(f32)).astype(bf16)


def product3(left, right, heads):
    left_high, left_low = halves(left)
    right_high, right_low = halves(right)
    rows = left.shape[0]
    first = contract(jnp.concatenate([left_high, left_low], axis=0), diagonal(right_high, heads))
    return first[:rows] + first[rows:] + contract(left_high, diagonal(right_low, heads))


def packed_inverse(coupling, heads):
    row = lax.broadcasted_iota(jnp.int32, coupling.shape, 0)
    lane = lax.broadcasted_iota(jnp.int32, coupling.shape, 1) % GROUP
    power = -coupling
    result = jnp.where(row == lane, 1.0, 0.0) + power
    power = product3(power, power, heads)
    degree = 2
    while degree * 2 < GROUP:
        both = product3(jnp.concatenate([result, power], axis=0), power, heads)
        result = result + both[:GROUP]
        power = both[GROUP:]
        degree = degree * 2
    return result + product3(result, power, heads)


def stacked(block, heads):
    width = block.shape[1] // heads
    return jnp.concatenate([block[:, h * width : (h + 1) * width] for h in range(heads)], axis=0)


def unstacked(block, heads):
    return jnp.concatenate([block[h * GROUP : (h + 1) * GROUP] for h in range(heads)], axis=1)


def fill(ext_ref, now_ref, before_ref, rim_ref, first, keep):
    before = jnp.where(first, rim_ref[...].astype(f32), before_ref[...].astype(f32))
    ext_ref[:HALO, :] = before * keep
    ext_ref[HALO:, :] = now_ref[...].astype(f32)


def tap_sum(ext_ref, conv_ref, low, width):
    total = ext_ref[pl.ds(HALO, GROUP), pl.ds(low, width)] * conv_ref[0:1, pl.ds(low, width)]
    for tap in range(1, CONV):
        total = total + (
            ext_ref[pl.ds(HALO - tap, GROUP), pl.ds(low, width)]
            * conv_ref[tap : tap + 1, pl.ds(low, width)]
        )
    return total


def summed_rows(mask, values, pieces=3):
    parts = []
    for _ in range(pieces):
        parts.append(values.astype(bf16))
        values = values - parts[-1].astype(f32)
    width = values.shape[1]
    sums = contract(mask.astype(bf16), jnp.concatenate(parts, axis=1))
    return sum(sums[:, i * width : (i + 1) * width] for i in range(pieces))


def token_terms(scal_ref, rate_ref, heads):
    scal = scal_ref[...]
    rate = rate_ref[...]
    shifted_alpha = scal[:, :heads] + rate[1:2]
    valid = scal[:, 2 * heads : 2 * heads + 1]
    decay = -rate[0:1] * jax.nn.softplus(shifted_alpha) * valid
    beta = jax.nn.sigmoid(scal[:, heads : 2 * heads])
    row = lax.broadcasted_iota(jnp.int32, (GROUP, heads * GROUP), 0)
    lane = lax.broadcasted_iota(jnp.int32, (GROUP, heads * GROUP), 1) % GROUP
    wide = spread([decay[:, h : h + 1] for h in range(heads)], heads)
    square_row = lax.broadcasted_iota(jnp.int32, (GROUP, GROUP), 0)
    square_lane = lax.broadcasted_iota(jnp.int32, (GROUP, GROUP), 1)
    sums = summed_rows(jnp.where(square_row >= square_lane, 1.0, 0.0), wide)
    across = jnp.sum(jnp.where(row <= lane, wide, 0.0), axis=0, keepdims=True)
    lower, strict = (row >= lane, row > lane)
    ratio = jnp.where(lower, jnp.exp(jnp.where(lower, sums - across, 0.0)), 0.0)
    betas = [beta[:, h : h + 1] for h in range(heads)]
    last = sums[GROUP - 1 :]
    grown, closing = (jnp.exp(sums), jnp.exp(last - sums))
    column = lambda values: jnp.concatenate(
        [values[:, h * GROUP : h * GROUP + 1] for h in range(heads)], axis=0
    )
    fade = jnp.exp(last)
    fades = [fade[:, h * GROUP : h * GROUP + 1] for h in range(heads)]
    return dict(
        alpha=shifted_alpha,
        rate=rate[0:1],
        valid=valid,
        decay=decay,
        beta=beta,
        ratio=ratio,
        strict=strict,
        betas=spread(betas, heads),
        beta_column=jnp.concatenate(betas, axis=0),
        growth=column(grown),
        closing=column(closing),
        fades=fades,
    )


def forward_kernel(
    heads,
    groups,
    keep_ref,
    query_ref,
    key_ref,
    value_ref,
    query_before,
    key_before,
    value_before,
    query_rim,
    key_rim,
    value_rim,
    conv_query,
    conv_key,
    conv_value,
    scal_ref,
    rate_ref,
    query_out,
    key_out,
    value_out,
    wu_out,
    inverse_out,
    state_out,
    linear_out,
    local_out,
    device_out,
    state,
    ext_query,
    ext_key,
    ext_value,
):
    group = pl.program_id(0)
    first = group == 0

    @pl.when(first)
    def _():
        row = lax.broadcasted_iota(jnp.int32, (DK, WIDE), 0)
        lane = lax.broadcasted_iota(jnp.int32, (DK, WIDE), 1)
        unit = jnp.where(row == lane, 1.0, 0.0)
        for h in range(heads):
            state[pl.ds(h * DK, DK), :] = unit

    keep = keep_ref[group]
    fill(ext_query, query_ref, query_before, query_rim, first, keep)
    fill(ext_key, key_ref, key_before, key_rim, first, keep)
    fill(ext_value, value_ref, value_before, value_rim, first, keep)
    terms = token_terms(scal_ref, rate_ref, heads)
    valid = terms["valid"]
    queries, keys, values = ([], [], [])
    for h in range(heads):
        act = jax.nn.silu(tap_sum(ext_query, conv_query, h * DK, DK))
        scale = lax.rsqrt(jnp.sum(act * act, axis=1, keepdims=True) + epsilon_norm)
        queries.append((act * scale * DK ** (-0.5)).astype(bf16))
        act = jax.nn.silu(tap_sum(ext_key, conv_key, h * DK, DK))
        scale = lax.rsqrt(jnp.sum(act * act, axis=1, keepdims=True) + epsilon_norm)
        keys.append((act * scale * valid).astype(bf16))
        act = jax.nn.silu(tap_sum(ext_value, conv_value, h * DV, DV))
        values.append((act * valid).astype(bf16))
    query_out[...] = jnp.concatenate(queries, axis=1)
    key_out[...] = jnp.concatenate(keys, axis=1)
    value_out[...] = jnp.concatenate(values, axis=1)
    query = jnp.concatenate(queries, axis=0)
    key = jnp.concatenate(keys, axis=0)
    value = jnp.concatenate(values, axis=0)
    scores = contract(jnp.concatenate([query, key], axis=0), key, 1, 1)
    mix = packed(scores[: heads * GROUP], heads)
    similar = packed(scores[heads * GROUP :], heads)
    ratio, betas, strict = (terms["ratio"], terms["betas"], terms["strict"])
    mixing = diagonal(ratio * mix, heads)
    inverse = packed_inverse(jnp.where(strict, betas * ratio * similar, 0.0), heads).astype(bf16)
    inverse_out[...] = inverse
    beta, growth, closing = (terms["beta_column"], terms["growth"], terms["closing"])
    key_wide = key.astype(f32)
    right = jnp.concatenate([beta * growth * key_wide, beta * value.astype(f32)], axis=1)
    wu = contract(diagonal(inverse, heads), right.astype(bf16))
    wu_low = wu.astype(bf16)
    wu_out[0] = wu_low
    grown = (growth * query.astype(f32)).astype(bf16)
    fading = (closing * key_wide).astype(bf16)
    lane = lax.broadcasted_iota(jnp.int32, (1, WIDE), 1)
    fresh, seen = ([], [])
    for h in range(heads):
        rows = slice(h * GROUP, (h + 1) * GROUP)
        used = state[pl.ds(h * DK, DK), :] * keep
        used_low = used.astype(bf16)
        state_out[0, pl.ds(h * DK, DK), :] = used_low
        part = jnp.where(lane >= DK, wu[rows], 0.0) - contract(wu_low[rows, :DK], used_low)
        part = part.astype(bf16)
        after = terms["fades"][h] * used + contract(fading[rows], part, 0, 0)
        state[pl.ds(h * DK, DK), :] = after
        fresh.append(part)
        seen.append(contract(grown[rows], used_low))
    both = jnp.concatenate(seen, axis=0) + contract(mixing, jnp.concatenate(fresh, axis=0))
    for h in range(heads):
        rows = slice(h * GROUP, (h + 1) * GROUP)
        linear_out[:, pl.ds(h * DK, DK)] = (both[rows, :DK] * valid).astype(bf16)
        local_out[:, pl.ds(h * DV, DV)] = both[rows, DK:] * valid

    @pl.when(group == groups - 1)
    def _():
        device_out[...] = state[...]


def token_block(width, back=None):
    if back is None:
        return pl.BlockSpec((GROUP, width), lambda g: (g, 0))
    return pl.BlockSpec((GROUP, width), lambda g: (back - 1 - g, 0))


def before_block(width, back=None):
    ratio = GROUP // HALO
    if back is None:
        return pl.BlockSpec((HALO, width), lambda g: (jnp.maximum(g * ratio - 1, 0), 0))
    return pl.BlockSpec((HALO, width), lambda g: (jnp.maximum((back - 1 - g) * ratio - 1, 0), 0))


def whole(shape):
    return pl.BlockSpec(shape, lambda g: (0,) * len(shape))


def delta_forward(pres, rims, convs, scal, rate, keep):
    tokens = scal.shape[0]
    heads, groups = (rate.shape[1], tokens // GROUP)
    widths = [pre.shape[1] for pre in pres]
    smem = pl.BlockSpec(memory_space=pltpu.SMEM)
    return pl.pallas_call(
        functools.partial(forward_kernel, heads, groups),
        grid=(groups,),
        in_specs=[smem]
        + [token_block(w) for w in widths]
        + [before_block(w) for w in widths]
        + [whole((HALO, w)) for w in widths]
        + [whole((CONV, w)) for w in widths]
        + [token_block(scal.shape[1]), whole(rate.shape)],
        out_specs=[token_block(w) for w in widths]
        + [
            pl.BlockSpec((1, heads * GROUP, WIDE), lambda g: (g, 0, 0)),
            token_block(heads * GROUP),
            pl.BlockSpec((1, heads * DK, WIDE), lambda g: (g, 0, 0)),
            token_block(heads * DK),
            token_block(heads * DV),
            whole((heads * DK, WIDE)),
        ],
        out_shape=[jax.ShapeDtypeStruct((tokens, w), bf16) for w in widths]
        + [
            jax.ShapeDtypeStruct((groups, heads * GROUP, WIDE), bf16),
            jax.ShapeDtypeStruct((tokens, heads * GROUP), bf16),
            jax.ShapeDtypeStruct((groups, heads * DK, WIDE), bf16),
            jax.ShapeDtypeStruct((tokens, heads * DK), bf16),
            jax.ShapeDtypeStruct((tokens, heads * DV), f32),
            jax.ShapeDtypeStruct((heads * DK, WIDE), f32),
        ],
        scratch_shapes=[pltpu.VMEM((heads * DK, WIDE), f32)]
        + [pltpu.VMEM((HALO + GROUP, w), f32) for w in widths],
        compiler_params=pltpu.CompilerParams(vmem_limit_bytes=VMEM),
        cost_estimate=pl.CostEstimate(flops=10**6, bytes_accessed=10**4, transcendentals=0),
        name="delta_forward",
    )(keep, *pres, *pres, *rims, *convs, scal, rate)


def backward_kernel(
    heads,
    groups,
    keep_ref,
    query_pre,
    key_pre,
    value_pre,
    query_before,
    key_before,
    value_before,
    query_rim,
    key_rim,
    value_rim,
    conv_query,
    conv_key,
    conv_value,
    scal_ref,
    rate_ref,
    query_ref,
    key_ref,
    value_ref,
    wu_ref,
    inverse_ref,
    state_ref,
    entry_ref,
    exit_ref,
    grad_ref,
    query_out,
    key_out,
    value_out,
    query_conv_out,
    key_conv_out,
    value_conv_out,
    query_back_out,
    key_back_out,
    value_back_out,
    query_tail_out,
    key_tail_out,
    value_tail_out,
    scal_out,
    rate_out,
    got_out,
    carry,
    ext_query,
    ext_key,
    ext_value,
    dy_query,
    dy_key,
    dy_value,
    sending,
    send_sem,
    recv_sem,
):
    step = pl.program_id(0)
    group = groups - 1 - step
    keep = keep_ref[group]
    seq, head = (lax.axis_index("seq"), lax.axis_index("head"))
    partner = seq + 1 - 2 * (seq % 2)

    def transfer(at, block):
        return pltpu.make_async_remote_copy(
            src_ref=sending.at[at % 2],
            dst_ref=got_out.at[pl.ds(block * GROUP, GROUP), :],
            send_sem=send_sem.at[at % 2],
            recv_sem=recv_sem.at[block],
            device_id=(partner, head),
            device_id_type=pl.DeviceIdType.MESH,
        )

    @pl.when(step == 0)
    def _():
        barrier = pltpu.get_barrier_semaphore()
        pl.semaphore_signal(
            barrier, inc=1, device_id=(partner, head), device_id_type=pl.DeviceIdType.MESH
        )
        pl.semaphore_wait(barrier, 1)

    @pl.when(step >= 2)
    def _():
        transfer(step, group + 2).wait_send()

    @pl.when(step == 0)
    def _():
        carry[...] = exit_ref[...]
        for ref in (dy_query, dy_key, dy_value):
            ref[...] = jnp.zeros_like(ref)
        for ref in (query_conv_out, key_conv_out, value_conv_out, rate_out):
            ref[...] = jnp.zeros_like(ref)

    terms = token_terms(scal_ref, rate_ref, heads)
    valid = terms["valid"]
    beta, growth, closing = (terms["beta_column"], terms["growth"], terms["closing"])
    query = stacked(query_ref[...], heads)
    key = stacked(key_ref[...], heads)
    value = stacked(value_ref[...], heads)
    grad = stacked(grad_ref[...], heads)
    query_wide, key_wide = (query.astype(f32), key.astype(f32))
    scores = contract(jnp.concatenate([query, key], axis=0), key, 1, 1)
    mix = packed(scores[: heads * GROUP], heads)
    similar = packed(scores[heads * GROUP :], heads)
    ratio, betas, strict = (terms["ratio"], terms["betas"], terms["strict"])
    mixing = ratio * mix
    wu = wu_ref[0]
    grown_wide = growth * query_wide
    fading_wide = closing * key_wide
    grown = grown_wide.astype(bf16)
    fading = fading_wide.astype(bf16)
    mixed_back = contract(diagonal(mixing, heads), grad, 0, 0)
    fresh, d_fresh, d_grown, d_fading, d_weights, d_fades = ([], [], [], [], [], [])
    for h in range(heads):
        rows = slice(h * GROUP, (h + 1) * GROUP)
        states = pl.ds(h * DK, DK)
        pair = state_ref[0, states, :]
        used = pair[:, DK:].astype(f32) + contract(pair[:, :DK], entry_ref[states, :])
        used_low = used.astype(bf16)
        weights = wu[rows, :DK]
        part = (wu[rows, DK:].astype(f32) - contract(weights, used_low)).astype(bf16)
        after = carry[states, :]
        after_low = after.astype(bf16)
        d_part = mixed_back[rows] + contract(fading[rows], after_low)
        d_part_low = d_part.astype(bf16)
        stack = jnp.concatenate([grad[rows], d_part_low], axis=0)
        seen = contract(stack, used_low, 1, 1)
        d_grown.append(seen[:GROUP])
        d_weights.append(-seen[GROUP:])
        d_fading.append(contract(part, after_low, 1, 1))
        fade = terms["fades"][h]
        carry[states, :] = keep * (
            fade * after
            + contract(jnp.concatenate([grown[rows], -weights], axis=0), stack, 0, 0)
        )
        d_fade = jnp.sum(after * used, axis=0, keepdims=True)
        d_fades.append(fade * jnp.sum(d_fade, axis=1, keepdims=True))
        fresh.append(part)
        d_fresh.append(d_part_low)
    d_grown = jnp.concatenate(d_grown, axis=0)
    d_fading = jnp.concatenate(d_fading, axis=0)
    d_weights = jnp.concatenate(d_weights, axis=0).astype(bf16)
    d_fresh = jnp.concatenate(d_fresh, axis=0)
    d_mixing = packed(contract(grad, jnp.concatenate(fresh, axis=0), 1, 1), heads)
    d_right = contract(
        diagonal(inverse_ref[...], heads), jnp.concatenate([d_weights, d_fresh], axis=1), 0, 0
    )
    d_coupling = -packed(contract(d_right.astype(bf16), wu, 1, 1), heads)
    d_coupling = jnp.where(strict, d_coupling, 0.0)
    ratio_grad = ratio * d_coupling
    from_similar = diagonal(betas * ratio_grad, heads)
    from_mix = diagonal(ratio * d_mixing, heads)
    plain = contract(jnp.concatenate([from_mix, from_similar], axis=0), key)
    turned = contract(
        jnp.concatenate([from_similar, from_mix], axis=0),
        jnp.concatenate([key, query], axis=0),
        0,
        0,
    )
    count = heads * GROUP
    d_scaled = d_right[:, :DK]
    d_query = growth * d_grown + plain[:count]
    d_key = beta * growth * d_scaled + closing * d_fading + plain[count:] + turned
    d_value = beta * d_right[:, DK:]
    grown_key = growth * key_wide
    ratio_similar = ratio_grad * similar
    flows = betas * ratio_similar + mixing * d_mixing
    fading_flow = d_fading * fading_wide
    sum_growth = jnp.sum(
        d_grown * grown_wide + d_scaled * (beta * grown_key) - fading_flow, axis=1, keepdims=True
    )
    sum_fading = jnp.sum(fading_flow, axis=1, keepdims=True)
    value_flow = d_right[:, DK:] * value.astype(f32)
    sum_beta = jnp.sum(
        d_scaled * grown_key + value_flow[:, :DK] + value_flow[:, DK:], axis=1, keepdims=True
    )
    flow_high, flow_low = halves(flows)
    ones = jnp.full((GROUP, 128), 1.0, bf16)
    turned_flow = contract(
        jnp.concatenate([flow_high, flow_low], axis=0),
        jnp.concatenate([ones, ones], axis=0),
        0,
        0,
    )[:, :1]
    owner = lane_heads(heads)
    lane = lax.broadcasted_iota(jnp.int32, (GROUP, 128), 1)
    d_sums = jnp.zeros((GROUP, 128), f32)
    d_beta = jnp.zeros((GROUP, 128), f32)
    d_last = jnp.zeros((1, 128), f32)
    for h in range(heads):
        rows = slice(h * GROUP, (h + 1) * GROUP)
        flow = jnp.sum(jnp.where(owner == h, flows, 0.0), axis=1, keepdims=True)
        more = jnp.sum(jnp.where(owner == h, ratio_similar, 0.0), axis=1, keepdims=True)
        d_sums = jnp.where(lane == h, sum_growth[rows] + flow - turned_flow[rows], d_sums)
        d_beta = jnp.where(lane == h, sum_beta[rows] + more, d_beta)
        total = jnp.sum(sum_fading[rows], axis=0, keepdims=True) + d_fades[h]
        d_last = jnp.where(lane[:1] == h, total, d_last)
    square_row = lax.broadcasted_iota(jnp.int32, (GROUP, GROUP), 0)
    square_lane = lax.broadcasted_iota(jnp.int32, (GROUP, GROUP), 1)
    later = jnp.where(square_row <= square_lane, 1.0, 0.0)
    d_decay = (summed_rows(later, d_sums) + d_last)[:, :heads]
    d_beta = d_beta[:, :heads]
    d_alpha = -d_decay * terms["rate"] * jax.nn.sigmoid(terms["alpha"]) * valid
    d_beta = d_beta * terms["beta"] * (1.0 - terms["beta"])
    scal_out[...] = jnp.concatenate([d_alpha, d_beta], axis=1).astype(bf16)
    rate_out[0:1, :] += jnp.sum(d_decay * terms["decay"], axis=0, keepdims=True)
    rate_out[1:2, :] += jnp.sum(d_alpha, axis=0, keepdims=True)

    first = group == 0
    after_keep = jnp.where(step == 0, 0.0, keep_ref[jnp.minimum(group + 1, groups - 1)])
    sections = (
        (query_pre, query_before, query_rim, conv_query, ext_query, dy_query, DK, d_query),
        (key_pre, key_before, key_rim, conv_key, ext_key, dy_key, DK, d_key),
        (value_pre, value_before, value_rim, conv_value, ext_value, dy_value, DV, d_value),
    )
    outs = (
        (query_out, query_conv_out, query_back_out, query_tail_out),
        (key_out, key_conv_out, key_back_out, key_tail_out),
        (value_out, value_conv_out, value_back_out, value_tail_out),
    )
    for kind, (section, out) in enumerate(zip(sections, outs)):
        now_ref, before_ref, rim_ref, conv_ref, ext_ref, dy_ref, width, cotangent = section
        pre_out, conv_out, back_out, tail_out = out
        first_lane = kind * heads * DK
        fill(ext_ref, now_ref, before_ref, rim_ref, first, keep)
        dy_ref[8 + GROUP :, :] = dy_ref[8:16, :] * after_keep
        for h in range(heads):
            lanes = pl.ds(h * width, width)
            rows = slice(h * GROUP, (h + 1) * GROUP)
            total = tap_sum(ext_ref, conv_ref, h * width, width)
            sigmoid = jax.nn.sigmoid(total)
            act = total * sigmoid
            d_act = cotangent[rows]
            if kind > 0:
                d_act = d_act * valid
            if kind < 2:
                scale = lax.rsqrt(jnp.sum(act * act, axis=1, keepdims=True) + epsilon_norm)
                inner = jnp.sum(act * d_act, axis=1, keepdims=True)
                d_act = scale * (d_act - act * (scale * scale * inner))
            if kind == 0:
                d_act = d_act * DK ** (-0.5)
            d_total = d_act * (sigmoid * (1.0 + total * (1.0 - sigmoid)))
            dy_ref[pl.ds(8, GROUP), lanes] = d_total
            for tap in range(CONV):
                product = d_total * ext_ref[pl.ds(HALO - tap, GROUP), lanes]
                conv_out[pl.ds(tap * 8, 8), lanes] += jnp.sum(
                    product.reshape(GROUP // 8, 8, width), axis=0
                )
            d_pre = d_total * conv_ref[0:1, lanes]
            for tap in range(1, CONV):
                d_pre = d_pre + dy_ref[pl.ds(8 + tap, GROUP), lanes] * conv_ref[tap : tap + 1, lanes]
            pre_out[:, lanes] = d_pre.astype(bf16)
            sending[step % 2, :, pl.ds(first_lane + h * width, width)] = d_pre.astype(bf16)

            @pl.when(step == 0)
            def _():
                tail_out[:, lanes] = d_pre[GROUP - 8 :]

            @pl.when(first)
            def _():
                d_back = dy_ref[pl.ds(1, 8), lanes] * conv_ref[1:2, lanes]
                for tap in range(2, CONV):
                    d_back = d_back + dy_ref[pl.ds(tap, 8), lanes] * conv_ref[tap : tap + 1, lanes]
                back_out[:, lanes] = d_back * keep

    transfer(step, group).start()

    @pl.when(step == groups - 1)
    def _():
        transfer(step - 1, group + 1).wait_send()
        transfer(step, group).wait_send()
        for block in range(groups):
            transfer(step, block).wait_recv()


def delta_backward(pres, rims, convs, scal, rate, keep, made, entry, exit_grad, grad):
    tokens = scal.shape[0]
    heads, groups = (rate.shape[1], tokens // GROUP)
    widths = [pre.shape[1] for pre in pres]
    smem = pl.BlockSpec(memory_space=pltpu.SMEM)
    turn = lambda *shape: pl.BlockSpec(shape, lambda g: (groups - 1 - g, 0, 0))
    columns = 2 * heads
    return pl.pallas_call(
        functools.partial(backward_kernel, heads, groups),
        grid=(groups,),
        in_specs=[smem]
        + [token_block(w, groups) for w in widths]
        + [before_block(w, groups) for w in widths]
        + [whole((HALO, w)) for w in widths]
        + [whole((CONV, w)) for w in widths]
        + [token_block(scal.shape[1], groups), whole(rate.shape)]
        + [token_block(w, groups) for w in widths]
        + [
            turn(1, heads * GROUP, WIDE),
            token_block(heads * GROUP, groups),
            turn(1, heads * DK, WIDE),
            whole((heads * DK, DV)),
            whole((heads * DK, DV)),
            token_block(heads * DV, groups),
        ],
        out_specs=[token_block(w, groups) for w in widths]
        + [whole((CONV * 8, w)) for w in widths]
        + [whole((8, w)) for w in widths]
        + [whole((8, w)) for w in widths]
        + [token_block(columns, groups), whole((8, heads))]
        + [pl.BlockSpec(memory_space=pl.ANY)],
        out_shape=[jax.ShapeDtypeStruct((tokens, w), bf16) for w in widths]
        + [jax.ShapeDtypeStruct((CONV * 8, w), f32) for w in widths]
        + [jax.ShapeDtypeStruct((8, w), f32) for w in widths]
        + [jax.ShapeDtypeStruct((8, w), f32) for w in widths]
        + [
            jax.ShapeDtypeStruct((tokens, columns), bf16),
            jax.ShapeDtypeStruct((8, heads), f32),
            jax.ShapeDtypeStruct((tokens, sum(widths)), bf16),
        ],
        scratch_shapes=[pltpu.VMEM((heads * DK, DV), f32)]
        + [pltpu.VMEM((HALO + GROUP, w), f32) for w in widths]
        + [pltpu.VMEM((16 + GROUP, w), f32) for w in widths]
        + [
            pltpu.VMEM((2, GROUP, sum(widths)), bf16),
            pltpu.SemaphoreType.DMA((2,)),
            pltpu.SemaphoreType.DMA((groups,)),
        ],
        compiler_params=pltpu.CompilerParams(
            vmem_limit_bytes=VMEM, collective_id=1, has_side_effects=True
        ),
        cost_estimate=pl.CostEstimate(flops=10**6, bytes_accessed=10**4, transcendentals=0),
        name="delta_backward",
    )(keep, *pres, *pres, *rims, *convs, scal, rate, *made, entry, exit_grad, grad)


def gated_forward_kernel(heads, linear_ref, local_ref, gate_ref, entry_ref, gain_ref, gated_out):
    for h in range(heads):
        wide = pl.ds(h * DV, DV)
        out = local_ref[:, wide] + contract(
            linear_ref[:, pl.ds(h * DK, DK)], entry_ref[pl.ds(h * DK, DK), :]
        )
        scale = lax.rsqrt(jnp.mean(out * out, axis=1, keepdims=True) + epsilon_gate)
        gate = gate_ref[:, wide]
        gated_out[:, wide] = (out * scale * gain_ref[...] * jax.nn.silu(gate)).astype(bf16)


def row_block(rows, width):
    return pl.BlockSpec((rows, width), lambda g: (g, 0))


def gated_forward(linear, local, gate, entry, gain):
    tokens, heads = (local.shape[0], local.shape[1] // DV)
    rows = 2 * GROUP
    return pl.pallas_call(
        functools.partial(gated_forward_kernel, heads),
        grid=(tokens // rows,),
        in_specs=[
            row_block(rows, heads * DK),
            row_block(rows, heads * DV),
            row_block(rows, heads * DV),
            whole((heads * DK, DV)),
            whole((1, DV)),
        ],
        out_specs=row_block(rows, heads * DV),
        out_shape=jax.ShapeDtypeStruct((tokens, heads * DV), bf16),
        compiler_params=pltpu.CompilerParams(vmem_limit_bytes=SMALL),
        cost_estimate=pl.CostEstimate(flops=10**9, bytes_accessed=10**7, transcendentals=0),
        name="gated_forward",
    )(linear, local, gate, entry, gain[None, :])


def gated_backward_kernel(
    heads,
    linear_ref,
    local_ref,
    gate_ref,
    entry_ref,
    gain_ref,
    grad_ref,
    valid_ref,
    delta_out,
    gate_out,
    gain_out,
    entry_out,
):
    @pl.when(pl.program_id(0) == 0)
    def _():
        gain_out[...] = jnp.zeros_like(gain_out)
        entry_out[...] = jnp.zeros_like(entry_out)

    rows = local_ref.shape[0]
    for h in range(heads):
        wide = pl.ds(h * DV, DV)
        linear = linear_ref[:, pl.ds(h * DK, DK)]
        out = local_ref[:, wide] + contract(linear, entry_ref[pl.ds(h * DK, DK), :])
        scale = lax.rsqrt(jnp.mean(out * out, axis=1, keepdims=True) + epsilon_gate)
        unit = out * scale
        gate = gate_ref[:, wide]
        sigmoid = jax.nn.sigmoid(gate)
        grad = grad_ref[:, wide]
        silu = gate * sigmoid
        product = grad * unit
        gain_out[...] += jnp.sum((product * silu).reshape(rows // 8, 8, DV), axis=0)
        gate_out[:, wide] = (
            product * gain_ref[...] * (sigmoid * (1.0 + gate * (1.0 - sigmoid)))
        ).astype(bf16)
        d_unit = grad * gain_ref[...] * silu
        inner = jnp.mean(d_unit * unit, axis=1, keepdims=True)
        delta = (scale * (d_unit - unit * inner) * valid_ref[...]).astype(bf16)
        delta_out[:, wide] = delta
        entry_out[pl.ds(h * DK, DK), :] += contract(linear, delta, 0, 0)


def gated_backward(linear, local, gate, entry, gain, grad, valid):
    tokens, heads = (local.shape[0], local.shape[1] // DV)
    rows = 2 * GROUP
    return pl.pallas_call(
        functools.partial(gated_backward_kernel, heads),
        grid=(tokens // rows,),
        in_specs=[
            row_block(rows, heads * DK),
            row_block(rows, heads * DV),
            row_block(rows, heads * DV),
            whole((heads * DK, DV)),
            whole((1, DV)),
            row_block(rows, heads * DV),
            row_block(rows, 1),
        ],
        out_specs=[
            row_block(rows, heads * DV),
            row_block(rows, heads * DV),
            whole((8, DV)),
            whole((heads * DK, DV)),
        ],
        out_shape=[
            jax.ShapeDtypeStruct((tokens, heads * DV), bf16),
            jax.ShapeDtypeStruct((tokens, heads * DV), bf16),
            jax.ShapeDtypeStruct((8, DV), f32),
            jax.ShapeDtypeStruct((heads * DK, DV), f32),
        ],
        compiler_params=pltpu.CompilerParams(vmem_limit_bytes=SMALL),
        cost_estimate=pl.CostEstimate(flops=10**6, bytes_accessed=10**4, transcendentals=0),
        name="gated_backward",
    )(linear, local, gate, entry, gain[None, :], grad, valid[:, None])


def column_place(tile, tiles, place):
    block, inner = (tile // (tiles // 4), tile % (tiles // 4))
    core = jnp.where(block < 2, 1 - place % 2, place % 2)
    chip = jnp.where(block % 2 == 0, 1 - place // 2, place // 2)
    return (chip * 2 + core) * (tiles // 4) + inner


def plain_dense_kernel(place_ref, left_ref, right_ref, out_ref):
    left = left_ref[:, : right_ref.shape[0]]
    out_ref[...] = contract(left, right_ref[...]).astype(bf16)


def plain_dense(left, right, place, tile=256):
    rows, cols = (left.shape[0], right.shape[1])
    tiles = cols // tile
    return pl.pallas_call(
        plain_dense_kernel,
        grid_spec=pltpu.PrefetchScalarGridSpec(
            num_scalar_prefetch=1,
            grid=(tiles,),
            in_specs=[
                pl.BlockSpec(left.shape, lambda i, place: (0, 0)),
                pl.BlockSpec(
                    (right.shape[0], tile), lambda i, place: (0, column_place(i, tiles, place[0]))
                ),
            ],
            out_specs=pl.BlockSpec((rows, tile), lambda i, place: (0, i)),
        ),
        out_shape=jax.ShapeDtypeStruct((rows, cols), bf16),
        compiler_params=pltpu.CompilerParams(vmem_limit_bytes=SMALL),
        cost_estimate=pl.CostEstimate(
            flops=2 * rows * cols * left.shape[1], bytes_accessed=10**7, transcendentals=0
        ),
        name="plain_dense",
    )(place, left, right)


def norm_dense_kernel(sides, place_ref, *refs):
    count = len(sides)
    lefts, rights = (refs[:count], refs[count : 2 * count])
    rows_ref, scale_ref, gain_ref, out_ref, gain_out, dots_out = refs[2 * count :]
    total = 0.0
    for left, right, side in zip(lefts, rights, sides):
        total = total + contract(left[:, : right.shape[side]], right[...], 1, side)
    out_ref[...] = total.astype(bf16)
    weighted = total * (rows_ref[...].astype(f32) * scale_ref[...])
    gain_out[...] = jnp.sum(weighted, axis=0, keepdims=True)
    dots = jnp.sum(weighted * gain_ref[...], axis=1, keepdims=True)

    @pl.when(pl.program_id(0) == 0)
    def _():
        dots_out[...] = dots

    @pl.when(pl.program_id(0) > 0)
    def _():
        dots_out[...] += dots


def norm_dense(pairs, rows, scale, gain, place, tile=256):
    tokens, cols = rows.shape
    tiles = cols // tile
    lefts, rights = ([left for left, _ in pairs], [right for _, right in pairs])
    placed = lambda i, place: (0, column_place(i, tiles, place[0]))
    upright = lambda i, place: (column_place(i, tiles, place[0]), 0)
    sides = [1 if right.shape[0] == cols else 0 for right in rights]
    return pl.pallas_call(
        functools.partial(norm_dense_kernel, sides),
        grid_spec=pltpu.PrefetchScalarGridSpec(
            num_scalar_prefetch=1,
            grid=(tiles,),
            in_specs=[pl.BlockSpec(left.shape, lambda i, place: (0, 0)) for left in lefts]
            + [
                pl.BlockSpec((tile, right.shape[1]), upright)
                if side
                else pl.BlockSpec((right.shape[0], tile), placed)
                for right, side in zip(rights, sides)
            ]
            + [
                pl.BlockSpec((tokens, tile), placed),
                pl.BlockSpec((tokens, 1), lambda i, place: (0, 0)),
                pl.BlockSpec((1, tile), placed),
            ],
            out_specs=[
                pl.BlockSpec((tokens, tile), lambda i, place: (0, i)),
                pl.BlockSpec((1, tile), placed),
                pl.BlockSpec((tokens, 1), lambda i, place: (0, 0)),
            ],
        ),
        out_shape=[
            jax.ShapeDtypeStruct((tokens, cols), bf16),
            jax.ShapeDtypeStruct((1, cols), f32),
            jax.ShapeDtypeStruct((tokens, 1), f32),
        ],
        compiler_params=pltpu.CompilerParams(vmem_limit_bytes=VMEM),
        cost_estimate=pl.CostEstimate(
            flops=2 * tokens * cols * sum(left.shape[1] for left in lefts),
            bytes_accessed=2 * 10**7,
            transcendentals=0,
        ),
        name="norm_dense",
    )(place, *lefts, *rights, rows, scale, gain[None, :])


def shifted(block, axis, distance):
    devices = range(lax.axis_size(axis))
    route = [(i - distance, i) for i in devices if i - distance in devices]
    return lax.ppermute(block, axis, route)


def exchanged(block, axis, bit):
    route = [(i, i ^ bit) for i in range(lax.axis_size(axis))]
    return lax.ppermute(block, axis, route)


def half(block, axis, at, count):
    width = block.shape[axis] // count
    return lax.dynamic_slice_in_dim(block, at * width, width, axis)


def weight_grad_kernel(turned, place_ref, rows_ref, got_rows_ref, cols_ref, got_cols_ref, out_ref):
    if turned:
        total = contract(cols_ref[...], rows_ref[...], 0, 0)
        total = total + contract(got_cols_ref[...], got_rows_ref[...], 0, 0)
        total = total[: out_ref.shape[0]]
    else:
        total = contract(rows_ref[...], cols_ref[...], 0, 0)
        total = total + contract(got_rows_ref[...], got_cols_ref[...], 0, 0)
    out_ref[...] = total.astype(bf16)


def pair_grad(rows, got_rows, cols, got_cols, turned, kept=None, spot=0):
    odd = lax.axis_index("seq").astype(jnp.int32) % 2
    devices = lax.axis_size("seq")
    tokens, padded = cols.shape
    count = padded if kept is None else kept
    width = rows.shape[1] // devices
    if width % 128:
        part = jnp.concatenate([own_half(rows, odd, width), got_rows], axis=0)
        got_cols = lax.slice_in_dim(got_cols, spot * padded, (spot + 1) * padded, axis=1)
        cols = jnp.concatenate([cols, got_cols], axis=0)[:, :count]
        if turned:
            part = part.reshape(2 * tokens, devices // 2, width)
            total = jnp.einsum("tn,tcw->cnw", cols, part, preferred_element_type=f32)
            return total.reshape(devices // 2 * count, width).astype(bf16)
        return dense(part.T, cols).astype(bf16)
    block = (count, width) if turned else (width, count)
    still = pl.BlockSpec((tokens, padded), lambda i, place: (0, 0))
    return pl.pallas_call(
        functools.partial(weight_grad_kernel, turned),
        grid_spec=pltpu.PrefetchScalarGridSpec(
            num_scalar_prefetch=1,
            grid=(devices // 2,),
            in_specs=[
                pl.BlockSpec((tokens, width), lambda i, place: (0, 2 * i + place[0])),
                pl.BlockSpec((tokens, width), lambda i, place: (0, i)),
                still,
                pl.BlockSpec((tokens, padded), lambda i, place: (0, spot)),
            ],
            out_specs=pl.BlockSpec(block, lambda i, place: (i, 0)),
        ),
        out_shape=jax.ShapeDtypeStruct((devices // 2 * block[0], block[1]), bf16),
        compiler_params=pltpu.CompilerParams(vmem_limit_bytes=SMALL),
        cost_estimate=pl.CostEstimate(flops=10**6, bytes_accessed=10**4, transcendentals=0),
        name="weight_grad",
    )(odd[None], rows, got_rows, cols, got_cols)


def partner_rows(block):
    width = block.shape[1] * 4 // lax.axis_size("seq")
    odd = lax.axis_index("seq") % 2
    if block.shape[1] == 2 * width:
        part = half(block, 1, 1 - odd, 2)
    else:
        part = own_half(block, 1 - odd, width)
    return exchanged(part, "seq", 1)


def gather_kernel(norm, place_ref, *refs):
    blocks = [ref[...] for ref in refs[:4]]
    width = blocks[0].shape[1]
    place = place_ref[0]
    out_ref = refs[5] if norm else refs[4]
    spots = [pl.ds(pl.multiple_of((place ^ at) * width, 128), width) for at in range(4)]
    for block, spot in zip(blocks, spots):
        out_ref[:, spot] = block
    if norm:
        gain_ref, normed_out, scale_out = (refs[4], refs[6], refs[7])
        wides = [block.astype(f32) for block in blocks]
        total = sum(jnp.sum(wide * wide, axis=1, keepdims=True) for wide in wides)
        scale = lax.rsqrt(total / (4 * width) + epsilon_norm)
        scale_out[...] = scale
        for wide, spot in zip(wides, spots):
            normed_out[:, spot] = (wide * scale * gain_ref[:, spot]).astype(bf16)


def head_gathered(block, gain=None):
    place = lax.axis_index("head").astype(jnp.int32)
    tokens, width = block.shape
    across = exchanged(block, "head", 2)
    beside = exchanged(block, "head", 1)
    corner = exchanged(across, "head", 1)
    rows = 4 * GROUP
    norm = gain is not None
    spec = lambda cols: pl.BlockSpec((rows, cols), lambda i, place: (i, 0))
    whole_shape = jax.ShapeDtypeStruct((tokens, 4 * width), bf16)
    out_specs, out_shape = (spec(4 * width), whole_shape)
    if norm:
        out_specs = [out_specs, spec(4 * width), spec(1)]
        out_shape = [whole_shape, whole_shape, jax.ShapeDtypeStruct((tokens, 1), f32)]
    gain_spec = pl.BlockSpec((1, 4 * width), lambda i, place: (0, 0))
    return pl.pallas_call(
        functools.partial(gather_kernel, norm),
        grid_spec=pltpu.PrefetchScalarGridSpec(
            num_scalar_prefetch=1,
            grid=(tokens // rows,),
            in_specs=[spec(width)] * 4 + ([gain_spec] if norm else []),
            out_specs=out_specs,
        ),
        out_shape=out_shape,
        compiler_params=pltpu.CompilerParams(vmem_limit_bytes=SMALL),
        cost_estimate=pl.CostEstimate(flops=10**6, bytes_accessed=6 * 10**6, transcendentals=0),
        name="gather",
    )(place[None], block, beside, across, corner, *([gain[None, :]] if norm else []))


def rows_dense_kernel(left_ref, right_ref, out_ref):
    out_ref[...] = contract(left_ref[...], right_ref[...], 1, 1)


def rows_dense(left, right):
    tokens, rows = (left.shape[0], 4 * GROUP)
    return pl.pallas_call(
        rows_dense_kernel,
        grid=(tokens // rows,),
        in_specs=[row_block(rows, left.shape[1]), whole(right.shape)],
        out_specs=row_block(rows, right.shape[0]),
        out_shape=jax.ShapeDtypeStruct((tokens, right.shape[0]), f32),
        compiler_params=pltpu.CompilerParams(vmem_limit_bytes=SMALL),
        cost_estimate=pl.CostEstimate(
            flops=2 * left.size * right.shape[0], bytes_accessed=10**7, transcendentals=0
        ),
        name="rows_dense",
    )(left, right)


def ffn_kernel(normed_ref, gate_ref, up_ref, grad_ref, inner_out, d_gate_out, d_up_out):
    normed = normed_ref[...]
    gate = contract(normed, gate_ref[...], 1, 1)
    up = contract(normed, up_ref[...], 1, 1)
    sigmoid = jax.nn.sigmoid(gate)
    silu = gate * sigmoid
    grad = grad_ref[...]
    padding = inner_out.shape[1] - gate.shape[1]
    for ref, values in (
        (inner_out, silu * up),
        (d_gate_out, grad * up * (sigmoid * (1.0 + gate * (1.0 - sigmoid)))),
        (d_up_out, grad * silu),
    ):
        values = values.astype(bf16)
        if padding:
            values = jnp.pad(values, ((0, 0), (0, padding)))
        ref[...] = values


def ffn(normed, w_gate, w_up, grad):
    tokens, count = grad.shape
    rows, padded = (4 * GROUP, -(-count // 128) * 128)
    return pl.pallas_call(
        ffn_kernel,
        grid=(tokens // rows,),
        in_specs=[row_block(rows, normed.shape[1])]
        + [whole(w_gate.shape)] * 2
        + [row_block(rows, count)],
        out_specs=[row_block(rows, padded)] * 3,
        out_shape=[jax.ShapeDtypeStruct((tokens, padded), bf16)] * 3,
        compiler_params=pltpu.CompilerParams(vmem_limit_bytes=VMEM),
        cost_estimate=pl.CostEstimate(
            flops=4 * normed.size * count, bytes_accessed=2 * 10**7, transcendentals=0
        ),
        name="ffn",
    )(normed, w_gate, w_up, grad)


def tied(*values):
    return lax.optimization_barrier(values)


def head_scattered(partial):
    width = partial.shape[1] // 2
    mine = partial[:, width:].astype(f32) + exchanged(partial[:, :width], "head", 1).astype(f32)
    width = width // 2
    return mine[:, width:] + exchanged(mine[:, :width].astype(bf16), "head", 2).astype(f32)


def head_summed(values):
    bit = 1
    while bit < lax.axis_size("head"):
        values = values + exchanged(values, "head", bit)
        bit = bit * 2
    return values


def all_summed(values):
    values = head_summed(values)
    bit = 1
    while bit < lax.axis_size("seq"):
        values = values + exchanged(values, "seq", bit)
        bit = bit * 2
    return values


def own_half(rows, odd, width):
    tokens, total = rows.shape
    parts = rows.reshape(tokens, total // (2 * width), 2, width)
    return lax.dynamic_index_in_dim(parts, odd, 2, False).reshape(tokens, total // 2)


def seq_scattered(mine):
    devices = lax.axis_size("seq")
    groups = [list(range(first, devices, 2)) for first in range(2)]
    return lax.psum_scatter(
        mine.astype(bf16), "seq", scatter_dimension=0, axis_index_groups=groups, tiled=True
    ).astype(f32)


def line_step(send, step, planes, upward):
    devices = 2 * planes
    route = []
    for i in range(devices):
        plane = i // 2
        if upward and plane < step and plane + 1 < planes:
            route.append((i, i + 2))
        if not upward and planes - 1 - plane < step and plane > 0:
            route.append((i, i - 2))
    return lax.ppermute(send, "seq", route)


def line_scattered(kept):
    planes = lax.axis_size("seq") // 2
    if planes > 4:
        return seq_scattered(kept)
    plane = lax.axis_index("seq") // 2
    rows = kept.shape[0] // planes

    def chunk(at):
        return lax.dynamic_slice_in_dim(kept, at * rows, rows, 0).astype(f32)

    up, down = (None, None)
    for step in range(1, planes):
        to_up = chunk(jnp.minimum(plane + planes - step, planes - 1))
        to_down = chunk(jnp.maximum(plane - planes + step, 0))
        if up is not None:
            to_up, to_down = (to_up + up.astype(f32), to_down + down.astype(f32))
        up = line_step(to_up.astype(bf16), step, planes, True)
        down = line_step(to_down.astype(bf16), step, planes, False)
    return chunk(plane) + up.astype(f32) + down.astype(f32)


def composed(later, before):
    moved = jnp.einsum(
        "hij,hjk->hik", later[:, :, :DK].astype(bf16), before, preferred_element_type=f32
    )
    linear = moved.shape[2] - DV
    offset = later[:, :, DK:] + moved[:, :, linear:]
    return jnp.concatenate([moved[:, :, :linear], offset], axis=2)


def prefix(pair, got, direction):
    odd = lax.axis_index("seq") % 2
    front = odd == 1 if direction == 1 else odd == 0
    wide = got.astype(f32)
    low = pair.astype(bf16)
    closed = composed(jnp.where(front, pair, wide), jnp.where(front, got, low))
    distance = 2
    before = shifted(closed.astype(bf16), "seq", direction * distance)
    opened = before.astype(f32)
    while True:
        closed = composed(closed, before)
        distance = distance * 2
        last = distance * 2 >= lax.axis_size("seq")
        sent = closed[:, :, DK:] if last else closed
        before = shifted(sent.astype(bf16), "seq", direction * distance)
        opened = composed(opened, before)
        if last:
            break
    opened = opened[:, :, -DV:]
    moved = composed(wide, opened.astype(bf16))[:, :, -DV:]
    return jnp.where(front, moved, opened)


def layout(lengths, positions):
    padded = (lengths + (GROUP - 1)) // GROUP * GROUP
    seq_ends = jnp.cumsum(padded)
    begins = seq_ends - padded
    offset = positions[:, None] - begins[None, :]
    inside = (offset >= 0) & (positions[:, None] < seq_ends[None, :])
    valid_mask = jnp.any(inside & (offset < lengths[None, :]), axis=1).astype(jnp.float32)
    starts = jnp.any(offset == 0, axis=1).astype(jnp.float32)
    return (valid_mask, starts)


def dense(left, right):
    return jnp.dot(left, right, preferred_element_type=jnp.float32)


def shards(
    hidden_in,
    lengths,
    attn_gain,
    w_query,
    w_key,
    w_value,
    w_gate,
    w_alpha,
    w_beta,
    conv_query,
    conv_key,
    conv_value,
    decay_log,
    decay_bias,
    out_gain,
    w_out,
    ffn_gain,
    w_ffn_gate,
    w_ffn_up,
    w_ffn_down,
    grad_out,
):
    token_rows = hidden_in.shape[0]
    head_count = w_alpha.shape[1]
    col_width = grad_out.shape[1]
    devices = lax.axis_size("seq")
    positions = lax.axis_index("seq") * token_rows + jnp.arange(token_rows, dtype=jnp.int32)
    valid_mask, starts = layout(lengths, positions)
    keep_flags = 1.0 - starts[::GROUP]
    head_place = lax.axis_index("head")
    place = head_place[None].astype(jnp.int32)
    head_first = head_place * head_count
    col_first = head_place * col_width
    cols = lambda rows: lax.dynamic_slice_in_dim(rows, col_first, col_width, rows.ndim - 1)
    local_log = lax.dynamic_slice_in_dim(decay_log, head_first, head_count)
    local_bias = lax.dynamic_slice_in_dim(decay_bias, head_first, head_count)

    inputs32 = hidden_in.astype(f32)
    attn_scale = lax.rsqrt(jnp.mean(inputs32 * inputs32, axis=-1, keepdims=True) + epsilon_norm)
    normed = (inputs32 * attn_scale * attn_gain).astype(bf16)
    pres = [dense(normed, weight).astype(bf16) for weight in (w_query, w_key, w_value)]
    widths = [pre.shape[1] for pre in pres]
    edges = [0, widths[0], widths[0] + widths[1], sum(widths)]
    split = lambda rows: [rows[:, a:b] for a, b in zip(edges[:-1], edges[1:])]
    tail_first = token_rows - (CONV - 1)
    rims = shifted(jnp.concatenate([pre[tail_first:] for pre in pres], 1), "seq", 1)
    rims, grad_cols, normed_cols = tied(rims, grad_out, cols(normed))
    got_grad_rows = head_gathered(partner_rows(grad_cols))
    got_normed = head_gathered(partner_rows(normed_cols))
    rims = split(jnp.pad(rims, ((HALO - (CONV - 1), 0), (0, 0))))
    w_scal = jnp.concatenate([w_alpha, w_beta], axis=1)
    scal = jnp.concatenate([dense(normed, w_scal), valid_mask[:, None]], axis=1)
    rate = jnp.stack([jnp.exp(local_log), local_bias])
    convs = [conv_query, conv_key, conv_value]
    *made, linear, local, device_pair = delta_forward(
        pres, rims, convs, scal, rate, keep_flags
    )
    grad_rows = head_gathered(grad_out)
    device_pair, grad_rows = tied(device_pair, grad_rows)
    device_pair = device_pair.reshape(head_count, DK, WIDE)
    got_pair = exchanged(device_pair.astype(bf16), "seq", 1)
    entry = prefix(device_pair, got_pair, 1).astype(bf16).reshape(head_count * DK, DV)
    gate_pre = dense(normed, w_gate)
    d_inner = rows_dense(grad_rows, w_ffn_down)
    entry, d_inner, gate_pre, got_grad_rows, got_normed = tied(
        entry, d_inner, gate_pre, got_grad_rows, got_normed
    )
    gated = gated_forward(linear, local, gate_pre, entry, out_gain)
    mixed = head_scattered(plain_dense(gated, w_out, place))
    middle = cols(hidden_in).astype(f32) + mixed
    sent, normed_ffn, ffn_scale = head_gathered(middle.astype(bf16), ffn_gain)
    got_gated = exchanged(gated, "seq", 1)
    d_inner, got_gated = tied(d_inner, got_gated)
    inner_act, d_ffn_gate, d_ffn_up = ffn(normed_ffn, w_ffn_gate.T, w_ffn_up.T, d_inner)
    units = w_ffn_gate.shape[1]
    got_ffn_cols = partner_rows(cols(normed_ffn))
    inner_sent, d_ffn_gate, got_ffn_cols = tied(inner_act, d_ffn_gate, got_ffn_cols)
    got_inner = exchanged(inner_sent, "seq", 1)
    d_normed_ffn, grad_ffn_gain, ffn_dots = norm_dense(
        [(d_ffn_gate, w_ffn_gate.T), (d_ffn_up, w_ffn_up.T)], sent, ffn_scale, ffn_gain, place
    )
    ffn_dots = head_summed(ffn_dots[:, 0])[:, None] / sent.shape[1]
    d_sent_cols = ffn_scale * (
        cols(ffn_gain) * head_scattered(d_normed_ffn)
        - cols(sent).astype(f32) * ffn_scale * ffn_dots
    )
    d_middle = grad_out.astype(f32) + d_sent_cols
    got_normed_ffn = head_gathered(got_ffn_cols)
    middle_cols, got_normed_ffn = tied(d_middle.astype(bf16), got_normed_ffn)
    d_mixed = head_gathered(middle_cols)
    d_gated = dense(d_mixed, w_out.T)
    got_mixed_cols = partner_rows(middle_cols)
    d_gate_sent, got_inner, got_mixed_cols = tied(d_ffn_gate, got_inner, got_mixed_cols)
    got_d_gate = exchanged(d_gate_sent, "seq", 1)
    kept_down = pair_grad(grad_rows, got_grad_rows, inner_act, got_inner, True, units)
    grad_w_ffn_down = seq_scattered(kept_down)
    d_gated, kept_down = tied(d_gated, kept_down)
    d_delta, d_gate_pre, gain_part, entry_grad = gated_backward(
        linear, local, gate_pre, entry, out_gain, d_gated, valid_mask
    )
    back_pair = jnp.concatenate(
        [
            jnp.swapaxes(device_pair[:, :, :DK], 1, 2),
            entry_grad.reshape(head_count, DK, DV),
        ],
        axis=2,
    )
    back_pair, got_d_gate = tied(back_pair, got_d_gate)
    got_back = exchanged(back_pair.astype(bf16), "seq", 1)
    d_up_sent, got_mixed_cols, inner_late, got_back = tied(
        d_ffn_up, got_mixed_cols, inner_act, got_back
    )
    got_d_up = exchanged(d_up_sent, "seq", 1)
    kept_gate = pair_grad(normed_ffn, got_normed_ffn, d_ffn_gate, got_d_gate, True, units)
    got_d_mixed = head_gathered(got_mixed_cols)
    kept_out = pair_grad(d_mixed, got_d_mixed, gated, got_gated, True)
    ffn_out = head_scattered(plain_dense(inner_late, w_ffn_down, place))
    hidden_out = (middle + ffn_out).astype(bf16)
    exit_grad = prefix(back_pair, got_back, -1).reshape(head_count * DK, DV)
    exit_grad, kept_gate, kept_out, grad_w_ffn_down, hidden_out, got_d_up = tied(
        exit_grad, kept_gate, kept_out, grad_w_ffn_down, hidden_out, got_d_up
    )
    grad_w_ffn_gate = seq_scattered(kept_gate)
    grad_w_out = seq_scattered(kept_out)
    results = delta_backward(
        pres, rims, convs, scal, rate, keep_flags, made, entry, exit_grad, d_delta
    )
    d_pres, conv_parts, backs, tails = (results[i : i + 3] for i in range(0, 12, 3))
    d_scal, d_rate, got_all = results[12:]
    backs = jnp.concatenate(backs, 1)[8 - (CONV - 1) :]
    tails = jnp.concatenate(tails, 1)
    backs, tails, gate_sent, d_up_late = tied(backs, tails, d_gate_pre, d_ffn_up)
    got_d_gate_pre = exchanged(gate_sent, "seq", 1)
    kept_up = pair_grad(normed_ffn, got_normed_ffn, d_up_late, got_d_up, True, units)
    grad_w_ffn_up = seq_scattered(kept_up)
    crossing = [(i, (i - 1) ^ 1) for i in range(1, devices)]
    got_tails = exchanged(tails, "seq", 1)
    more = jnp.pad(lax.ppermute(backs, "seq", crossing), ((8 - (CONV - 1), 0), (0, 0)))
    backs = jnp.pad(shifted(backs, "seq", -1), ((8 - (CONV - 1), 0), (0, 0)))
    got_tails, more, backs, kept_up = tied(got_tails, more, backs, kept_up)
    got_all = lax.dynamic_update_slice(
        got_all, (got_tails + more).astype(bf16), (token_rows - 8, 0)
    )
    d_query_pre, d_key_pre, d_value_pre = [
        lax.dynamic_update_slice(d_pre, tail.astype(bf16), (token_rows - 8, 0))
        for d_pre, tail in zip(d_pres, split(tails + backs))
    ]
    kept_value = pair_grad(normed, got_normed, d_value_pre, got_all, False, None, 1)
    kept_query = pair_grad(normed, got_normed, d_query_pre, got_all, False, None, 0)
    kept_key = pair_grad(normed, got_normed, d_key_pre, got_all, False, None, 1)
    query_key = jnp.concatenate([kept_query, kept_key], axis=1)
    d_scal, kept_value, query_key, got_d_gate_pre, grad_w_ffn_gate = tied(
        d_scal, kept_value, query_key, got_d_gate_pre, grad_w_ffn_gate
    )
    kept_w_gate = pair_grad(normed, got_normed, d_gate_pre, got_d_gate_pre, False)
    grad_w_gate = seq_scattered(kept_w_gate)
    d_scal, kept_w_gate = tied(d_scal, kept_w_gate)
    small = dense(normed.T, d_scal)
    small = [part.reshape(devices, -1) for part in (small[:, :head_count], small[:, head_count:])]
    for part in conv_parts:
        part = jnp.sum(part.reshape(CONV, 8, -1), axis=1).reshape(CONV, devices, -1)
        small.append(jnp.swapaxes(part, 0, 1).reshape(devices, -1))
    small = jnp.concatenate(small, axis=1)
    small_width = small.shape[1]
    odd = lax.axis_index("seq") % 2
    small = small.astype(bf16).reshape(devices // 2, 2, small_width // 128, 128)
    got = exchanged(lax.dynamic_index_in_dim(small, 1 - odd, 1, False), "seq", 1)
    small = lax.dynamic_index_in_dim(small, odd, 1, False).astype(f32) + got.astype(f32)
    small = seq_scattered(small.reshape(devices * small_width // 256, 128)).reshape(small_width)
    small_pieces = []
    for rows, width in [(normed.shape[1] // devices, head_count)] * 2 + [
        (CONV, width // devices) for width in widths
    ]:
        small_pieces.append(small[: rows * width].reshape(rows, width))
        small = small[rows * width :]
    d_normed, grad_attn_gain, attn_dots = norm_dense(
        [
            (d_query_pre, w_query),
            (d_key_pre, w_key),
            (d_value_pre, w_value),
            (d_gate_pre, w_gate),
            (d_scal, w_scal),
        ],
        hidden_in,
        attn_scale,
        attn_gain,
        place,
    )
    query_key = line_scattered(query_key)
    grad_w_query, grad_w_key = (query_key[:, : widths[0]], query_key[:, widths[0] :])
    grad_w_value = line_scattered(kept_value)
    d_normed = head_scattered(d_normed)
    attn_dots = head_summed(attn_dots[:, 0])[:, None] / hidden_in.shape[1]
    grad_in = d_middle + attn_scale * (
        cols(attn_gain) * d_normed
        - cols(hidden_in).astype(f32) * attn_scale * attn_dots
    )
    full_log = lax.dynamic_update_slice_in_dim(
        jnp.zeros(decay_log.shape, f32), d_rate[0], head_first, 0
    )
    full_bias = lax.dynamic_update_slice_in_dim(
        jnp.zeros(decay_bias.shape, f32), d_rate[1], head_first, 0
    )
    sums = all_summed(
        jnp.concatenate(
            [jnp.sum(gain_part, 0), grad_ffn_gain[0], grad_attn_gain[0], full_log, full_bias]
        )
    )
    gain_first = out_gain.shape[0]
    attn_first = gain_first + ffn_gain.shape[0]
    log_first = attn_first + attn_gain.shape[0]
    bias_first = log_first + decay_log.shape[0]
    rows_of = lambda whole: half(whole, 0, lax.axis_index("seq"), devices)
    return (
        hidden_out,
        grad_in,
        rows_of(sums[attn_first:log_first]),
        grad_w_query,
        grad_w_key,
        grad_w_value,
        grad_w_gate,
        *small_pieces,
        sums[log_first:bias_first],
        sums[bias_first:],
        sums[:gain_first],
        grad_w_out,
        rows_of(sums[gain_first:attn_first]),
        grad_w_ffn_gate.T,
        grad_w_ffn_up.T,
        grad_w_ffn_down,
    )


def solution(mesh):
    return jax.shard_map(
        shards,
        mesh=mesh,
        in_specs=(
            P("seq", None),
            P(),
            P(),
            P(None, "head"),
            P(None, "head"),
            P(None, "head"),
            P(None, "head"),
            P(None, "head"),
            P(None, "head"),
            P(None, "head"),
            P(None, "head"),
            P(None, "head"),
            P(),
            P(),
            P(),
            P("head", None),
            P(),
            P(None, "head"),
            P(None, "head"),
            P("head", None),
            P("seq", "head"),
        ),
        out_specs=(
            P("seq", "head"),
            P("seq", "head"),
            P("seq"),
            P("seq", "head"),
            P("seq", "head"),
            P("seq", "head"),
            P("seq", "head"),
            P("seq", "head"),
            P("seq", "head"),
            P(None, ("head", "seq")),
            P(None, ("head", "seq")),
            P(None, ("head", "seq")),
            P(),
            P(),
            P(),
            P("head", "seq"),
            P("seq"),
            P("seq", "head"),
            P("seq", "head"),
            P("head", "seq"),
        ),
        check_vma=False,
    )
```

```python
import functools

import jax
import jax.numpy as jnp
from jax import lax
from jax.experimental import pallas as pl
from jax.experimental.pallas import tpu as pltpu
from jax.sharding import PartitionSpec as P

DK = 128
DV = 256
GROUP = 64
CONV = 4
HALO = 16
WIDE = DK + DV
VMEM = 60 * 2**20
SMALL = 30 * 2**20

epsilon_norm = 1e-06
epsilon_gate = 1e-05

f32 = jnp.float32
bf16 = jnp.bfloat16


def contract(left, right, left_dim=1, right_dim=0):
    return lax.dot_general(
        left, right, (((left_dim,), (right_dim,)), ((), ())), preferred_element_type=f32
    )


def lane_heads(heads):
    return lax.broadcasted_iota(jnp.int32, (1, heads * GROUP), 1) // GROUP


def packed(full, heads):
    owner = lane_heads(heads)
    result = full[:GROUP]
    for head in range(1, heads):
        result = jnp.where(owner == head, full[head * GROUP : (head + 1) * GROUP], result)
    return result


def diagonal(values, heads):
    owner = lane_heads(heads)
    low = values.astype(bf16)
    return jnp.concatenate(
        [low * jnp.where(owner == head, 1.0, 0.0).astype(bf16) for head in range(heads)], axis=0
    )


def spread(columns, heads):
    owner = lane_heads(heads)
    result = jnp.broadcast_to(columns[0], (GROUP, heads * GROUP))
    for head in range(1, heads):
        result = jnp.where(owner == head, columns[head], result)
    return result


def halves(values):
    high = values.astype(bf16)
    return high, (values - high.astype(f32)).astype(bf16)


def product3(left, right, heads):
    left_high, left_low = halves(left)
    right_high, right_low = halves(right)
    rows = left.shape[0]
    first = contract(jnp.concatenate([left_high, left_low], axis=0), diagonal(right_high, heads))
    return first[:rows] + first[rows:] + contract(left_high, diagonal(right_low, heads))


def packed_inverse(coupling, heads):
    row = lax.broadcasted_iota(jnp.int32, coupling.shape, 0)
    lane = lax.broadcasted_iota(jnp.int32, coupling.shape, 1) % GROUP
    power = -coupling
    result = jnp.where(row == lane, 1.0, 0.0) + power
    power = product3(power, power, heads)
    degree = 2
    while degree * 2 < GROUP:
        both = product3(jnp.concatenate([result, power], axis=0), power, heads)
        result = result + both[:GROUP]
        power = both[GROUP:]
        degree = degree * 2
    return result + product3(result, power, heads)


def stacked(block, heads):
    width = block.shape[1] // heads
    return jnp.concatenate([block[:, h * width : (h + 1) * width] for h in range(heads)], axis=0)


def unstacked(block, heads):
    return jnp.concatenate([block[h * GROUP : (h + 1) * GROUP] for h in range(heads)], axis=1)


def fill(ext_ref, now_ref, before_ref, rim_ref, first, keep):
    before = jnp.where(first, rim_ref[...].astype(f32), before_ref[...].astype(f32))
    ext_ref[:HALO, :] = before * keep
    ext_ref[HALO:, :] = now_ref[...].astype(f32)


def tap_sum(ext_ref, conv_ref, low, width):
    total = ext_ref[pl.ds(HALO, GROUP), pl.ds(low, width)] * conv_ref[0:1, pl.ds(low, width)]
    for tap in range(1, CONV):
        total = total + (
            ext_ref[pl.ds(HALO - tap, GROUP), pl.ds(low, width)]
            * conv_ref[tap : tap + 1, pl.ds(low, width)]
        )
    return total


def summed_rows(mask, values, pieces=3):
    parts = []
    for _ in range(pieces):
        parts.append(values.astype(bf16))
        values = values - parts[-1].astype(f32)
    width = values.shape[1]
    sums = contract(mask.astype(bf16), jnp.concatenate(parts, axis=1))
    return sum(sums[:, i * width : (i + 1) * width] for i in range(pieces))


def token_terms(scal_ref, rate_ref, heads):
    scal = scal_ref[...]
    rate = rate_ref[...]
    shifted_alpha = scal[:, :heads] + rate[1:2]
    valid = scal[:, 2 * heads : 2 * heads + 1]
    decay = -rate[0:1] * jax.nn.softplus(shifted_alpha) * valid
    beta = jax.nn.sigmoid(scal[:, heads : 2 * heads])
    row = lax.broadcasted_iota(jnp.int32, (GROUP, heads * GROUP), 0)
    lane = lax.broadcasted_iota(jnp.int32, (GROUP, heads * GROUP), 1) % GROUP
    wide = spread([decay[:, h : h + 1] for h in range(heads)], heads)
    square_row = lax.broadcasted_iota(jnp.int32, (GROUP, GROUP), 0)
    square_lane = lax.broadcasted_iota(jnp.int32, (GROUP, GROUP), 1)
    sums = summed_rows(jnp.where(square_row >= square_lane, 1.0, 0.0), wide)
    across = jnp.sum(jnp.where(row <= lane, wide, 0.0), axis=0, keepdims=True)
    lower, strict = (row >= lane, row > lane)
    ratio = jnp.where(lower, jnp.exp(jnp.where(lower, sums - across, 0.0)), 0.0)
    betas = [beta[:, h : h + 1] for h in range(heads)]
    last = sums[GROUP - 1 :]
    grown, closing = (jnp.exp(sums), jnp.exp(last - sums))
    column = lambda values: jnp.concatenate(
        [values[:, h * GROUP : h * GROUP + 1] for h in range(heads)], axis=0
    )
    fade = jnp.exp(last)
    fades = [fade[:, h * GROUP : h * GROUP + 1] for h in range(heads)]
    return dict(
        alpha=shifted_alpha,
        rate=rate[0:1],
        valid=valid,
        decay=decay,
        beta=beta,
        ratio=ratio,
        strict=strict,
        betas=spread(betas, heads),
        beta_column=jnp.concatenate(betas, axis=0),
        growth=column(grown),
        closing=column(closing),
        fades=fades,
    )


def forward_kernel(
    heads,
    groups,
    keep_ref,
    query_ref,
    key_ref,
    value_ref,
    query_before,
    key_before,
    value_before,
    query_rim,
    key_rim,
    value_rim,
    conv_query,
    conv_key,
    conv_value,
    scal_ref,
    rate_ref,
    query_out,
    key_out,
    value_out,
    wu_out,
    inverse_out,
    state_out,
    linear_out,
    local_out,
    device_out,
    state,
    ext_query,
    ext_key,
    ext_value,
):
    group = pl.program_id(0)
    first = group == 0

    @pl.when(first)
    def _():
        row = lax.broadcasted_iota(jnp.int32, (DK, WIDE), 0)
        lane = lax.broadcasted_iota(jnp.int32, (DK, WIDE), 1)
        unit = jnp.where(row == lane, 1.0, 0.0)
        for h in range(heads):
            state[pl.ds(h * DK, DK), :] = unit

    keep = keep_ref[group]
    fill(ext_query, query_ref, query_before, query_rim, first, keep)
    fill(ext_key, key_ref, key_before, key_rim, first, keep)
    fill(ext_value, value_ref, value_before, value_rim, first, keep)
    terms = token_terms(scal_ref, rate_ref, heads)
    valid = terms["valid"]
    queries, keys, values = ([], [], [])
    for h in range(heads):
        act = jax.nn.silu(tap_sum(ext_query, conv_query, h * DK, DK))
        scale = lax.rsqrt(jnp.sum(act * act, axis=1, keepdims=True) + epsilon_norm)
        queries.append((act * scale * DK ** (-0.5)).astype(bf16))
        act = jax.nn.silu(tap_sum(ext_key, conv_key, h * DK, DK))
        scale = lax.rsqrt(jnp.sum(act * act, axis=1, keepdims=True) + epsilon_norm)
        keys.append((act * scale * valid).astype(bf16))
        act = jax.nn.silu(tap_sum(ext_value, conv_value, h * DV, DV))
        values.append((act * valid).astype(bf16))
    query_out[...] = jnp.concatenate(queries, axis=1)
    key_out[...] = jnp.concatenate(keys, axis=1)
    value_out[...] = jnp.concatenate(values, axis=1)
    query = jnp.concatenate(queries, axis=0)
    key = jnp.concatenate(keys, axis=0)
    value = jnp.concatenate(values, axis=0)
    scores = contract(jnp.concatenate([query, key], axis=0), key, 1, 1)
    mix = packed(scores[: heads * GROUP], heads)
    similar = packed(scores[heads * GROUP :], heads)
    ratio, betas, strict = (terms["ratio"], terms["betas"], terms["strict"])
    mixing = diagonal(ratio * mix, heads)
    inverse = packed_inverse(jnp.where(strict, betas * ratio * similar, 0.0), heads).astype(bf16)
    inverse_out[...] = inverse
    beta, growth, closing = (terms["beta_column"], terms["growth"], terms["closing"])
    key_wide = key.astype(f32)
    right = jnp.concatenate([beta * growth * key_wide, beta * value.astype(f32)], axis=1)
    wu = contract(diagonal(inverse, heads), right.astype(bf16))
    wu_low = wu.astype(bf16)
    wu_out[0] = wu_low
    grown = (growth * query.astype(f32)).astype(bf16)
    fading = (closing * key_wide).astype(bf16)
    lane = lax.broadcasted_iota(jnp.int32, (1, WIDE), 1)
    fresh, seen = ([], [])
    for h in range(heads):
        rows = slice(h * GROUP, (h + 1) * GROUP)
        used = state[pl.ds(h * DK, DK), :] * keep
        used_low = used.astype(bf16)
        state_out[0, pl.ds(h * DK, DK), :] = used_low
        part = jnp.where(lane >= DK, wu[rows], 0.0) - contract(wu_low[rows, :DK], used_low)
        part = part.astype(bf16)
        after = terms["fades"][h] * used + contract(fading[rows], part, 0, 0)
        state[pl.ds(h * DK, DK), :] = after
        fresh.append(part)
        seen.append(contract(grown[rows], used_low))
    both = jnp.concatenate(seen, axis=0) + contract(mixing, jnp.concatenate(fresh, axis=0))
    for h in range(heads):
        rows = slice(h * GROUP, (h + 1) * GROUP)
        linear_out[:, pl.ds(h * DK, DK)] = (both[rows, :DK] * valid).astype(bf16)
        local_out[:, pl.ds(h * DV, DV)] = both[rows, DK:] * valid

    @pl.when(group == groups - 1)
    def _():
        device_out[...] = state[...]


def token_block(width, back=None):
    if back is None:
        return pl.BlockSpec((GROUP, width), lambda g: (g, 0))
    return pl.BlockSpec((GROUP, width), lambda g: (back - 1 - g, 0))


def before_block(width, back=None):
    ratio = GROUP // HALO
    if back is None:
        return pl.BlockSpec((HALO, width), lambda g: (jnp.maximum(g * ratio - 1, 0), 0))
    return pl.BlockSpec((HALO, width), lambda g: (jnp.maximum((back - 1 - g) * ratio - 1, 0), 0))


def whole(shape):
    return pl.BlockSpec(shape, lambda g: (0,) * len(shape))


def delta_forward(pres, rims, convs, scal, rate, keep):
    tokens = scal.shape[0]
    heads, groups = (rate.shape[1], tokens // GROUP)
    widths = [pre.shape[1] for pre in pres]
    smem = pl.BlockSpec(memory_space=pltpu.SMEM)
    return pl.pallas_call(
        functools.partial(forward_kernel, heads, groups),
        grid=(groups,),
        in_specs=[smem]
        + [token_block(w) for w in widths]
        + [before_block(w) for w in widths]
        + [whole((HALO, w)) for w in widths]
        + [whole((CONV, w)) for w in widths]
        + [token_block(scal.shape[1]), whole(rate.shape)],
        out_specs=[token_block(w) for w in widths]
        + [
            pl.BlockSpec((1, heads * GROUP, WIDE), lambda g: (g, 0, 0)),
            token_block(heads * GROUP),
            pl.BlockSpec((1, heads * DK, WIDE), lambda g: (g, 0, 0)),
            token_block(heads * DK),
            token_block(heads * DV),
            whole((heads * DK, WIDE)),
        ],
        out_shape=[jax.ShapeDtypeStruct((tokens, w), bf16) for w in widths]
        + [
            jax.ShapeDtypeStruct((groups, heads * GROUP, WIDE), bf16),
            jax.ShapeDtypeStruct((tokens, heads * GROUP), bf16),
            jax.ShapeDtypeStruct((groups, heads * DK, WIDE), bf16),
            jax.ShapeDtypeStruct((tokens, heads * DK), bf16),
            jax.ShapeDtypeStruct((tokens, heads * DV), f32),
            jax.ShapeDtypeStruct((heads * DK, WIDE), f32),
        ],
        scratch_shapes=[pltpu.VMEM((heads * DK, WIDE), f32)]
        + [pltpu.VMEM((HALO + GROUP, w), f32) for w in widths],
        compiler_params=pltpu.CompilerParams(vmem_limit_bytes=VMEM),
        cost_estimate=pl.CostEstimate(flops=10**6, bytes_accessed=10**4, transcendentals=0),
        name="delta_forward",
    )(keep, *pres, *pres, *rims, *convs, scal, rate)


def backward_kernel(
    heads,
    groups,
    devices,
    keep_ref,
    query_pre,
    key_pre,
    value_pre,
    query_before,
    key_before,
    value_before,
    query_rim,
    key_rim,
    value_rim,
    conv_query,
    conv_key,
    conv_value,
    scal_ref,
    rate_ref,
    query_ref,
    key_ref,
    value_ref,
    wu_ref,
    inverse_ref,
    state_ref,
    entry_ref,
    exit_ref,
    grad_ref,
    query_out,
    key_out,
    value_out,
    query_conv_out,
    key_conv_out,
    value_conv_out,
    scal_out,
    rate_out,
    tail_out,
    own_back_out,
    other_back_out,
    got_tail_out,
    got_out,
    carry,
    ext_query,
    ext_key,
    ext_value,
    dy_query,
    dy_key,
    dy_value,
    sending,
    send_sem,
    recv_sem,
    back_send,
    tail_got,
    own_got,
    other_got,
    rim_send_sem,
    rim_recv_sem,
):
    step = pl.program_id(0)
    group = groups - 1 - step
    keep = keep_ref[group]
    seq, head = (lax.axis_index("seq"), lax.axis_index("head"))
    partner = seq + 1 - 2 * (seq % 2)

    def transfer(at, block):
        return pltpu.make_async_remote_copy(
            src_ref=sending.at[at % 2],
            dst_ref=got_out.at[pl.ds(block * GROUP, GROUP), :],
            send_sem=send_sem.at[at % 2],
            recv_sem=recv_sem.at[block],
            device_id=(partner, head),
            device_id_type=pl.DeviceIdType.MESH,
        )

    def rim_transfer(kind, source, target, to):
        return pltpu.make_async_remote_copy(
            src_ref=source,
            dst_ref=target,
            send_sem=rim_send_sem.at[kind],
            recv_sem=rim_recv_sem.at[kind],
            device_id=(to, head),
            device_id_type=pl.DeviceIdType.MESH,
        )

    tail_transfer = rim_transfer(0, tail_out, tail_got, partner)
    own_transfer = rim_transfer(1, back_send, own_got, seq - 1)
    other_transfer = rim_transfer(2, back_send, other_got, seq - 2)
    even = seq % 2 == 0

    @pl.when(step == 0)
    def _():
        barrier = pltpu.get_barrier_semaphore()
        mesh = pl.DeviceIdType.MESH
        pl.semaphore_signal(barrier, inc=1, device_id=(partner, head), device_id_type=mesh)

        @pl.when(even & (seq + 2 < devices))
        def _():
            pl.semaphore_signal(barrier, inc=1, device_id=(seq + 2, head), device_id_type=mesh)

        @pl.when((seq % 2 == 1) & (seq + 1 < devices))
        def _():
            pl.semaphore_signal(barrier, inc=1, device_id=(seq + 1, head), device_id_type=mesh)

        @pl.when(even & (seq >= 2))
        def _():
            pl.semaphore_wait(barrier, 3)

        @pl.when((seq % 2 == 1) | (seq < 2))
        def _():
            pl.semaphore_wait(barrier, 1)

    @pl.when(step >= 2)
    def _():
        transfer(step, group + 2).wait_send()

    @pl.when(step == 0)
    def _():
        carry[...] = exit_ref[...]
        for ref in (dy_query, dy_key, dy_value):
            ref[...] = jnp.zeros_like(ref)
        for ref in (query_conv_out, key_conv_out, value_conv_out, rate_out):
            ref[...] = jnp.zeros_like(ref)

    terms = token_terms(scal_ref, rate_ref, heads)
    valid = terms["valid"]
    beta, growth, closing = (terms["beta_column"], terms["growth"], terms["closing"])
    query = stacked(query_ref[...], heads)
    key = stacked(key_ref[...], heads)
    value = stacked(value_ref[...], heads)
    grad = stacked(grad_ref[...], heads)
    query_wide, key_wide = (query.astype(f32), key.astype(f32))
    scores = contract(jnp.concatenate([query, key], axis=0), key, 1, 1)
    mix = packed(scores[: heads * GROUP], heads)
    similar = packed(scores[heads * GROUP :], heads)
    ratio, betas, strict = (terms["ratio"], terms["betas"], terms["strict"])
    mixing = ratio * mix
    wu = wu_ref[0]
    grown_wide = growth * query_wide
    fading_wide = closing * key_wide
    grown = grown_wide.astype(bf16)
    fading = fading_wide.astype(bf16)
    mixed_back = contract(diagonal(mixing, heads), grad, 0, 0)
    fresh, d_fresh, d_grown, d_fading, d_weights, d_fades = ([], [], [], [], [], [])
    for h in range(heads):
        rows = slice(h * GROUP, (h + 1) * GROUP)
        states = pl.ds(h * DK, DK)
        pair = state_ref[0, states, :]
        used = pair[:, DK:].astype(f32) + contract(pair[:, :DK], entry_ref[states, :])
        used_low = used.astype(bf16)
        weights = wu[rows, :DK]
        part = (wu[rows, DK:].astype(f32) - contract(weights, used_low)).astype(bf16)
        after = carry[states, :]
        after_low = after.astype(bf16)
        d_part = mixed_back[rows] + contract(fading[rows], after_low)
        d_part_low = d_part.astype(bf16)
        stack = jnp.concatenate([grad[rows], d_part_low], axis=0)
        seen = contract(stack, used_low, 1, 1)
        d_grown.append(seen[:GROUP])
        d_weights.append(-seen[GROUP:])
        d_fading.append(contract(part, after_low, 1, 1))
        fade = terms["fades"][h]
        carry[states, :] = keep * (
            fade * after
            + contract(jnp.concatenate([grown[rows], -weights], axis=0), stack, 0, 0)
        )
        d_fade = jnp.sum(after * used, axis=0, keepdims=True)
        d_fades.append(fade * jnp.sum(d_fade, axis=1, keepdims=True))
        fresh.append(part)
        d_fresh.append(d_part_low)
    d_grown = jnp.concatenate(d_grown, axis=0)
    d_fading = jnp.concatenate(d_fading, axis=0)
    d_weights = jnp.concatenate(d_weights, axis=0).astype(bf16)
    d_fresh = jnp.concatenate(d_fresh, axis=0)
    d_mixing = packed(contract(grad, jnp.concatenate(fresh, axis=0), 1, 1), heads)
    d_right = contract(
        diagonal(inverse_ref[...], heads), jnp.concatenate([d_weights, d_fresh], axis=1), 0, 0
    )
    d_coupling = -packed(contract(d_right.astype(bf16), wu, 1, 1), heads)
    d_coupling = jnp.where(strict, d_coupling, 0.0)
    ratio_grad = ratio * d_coupling
    from_similar = diagonal(betas * ratio_grad, heads)
    from_mix = diagonal(ratio * d_mixing, heads)
    plain = contract(jnp.concatenate([from_mix, from_similar], axis=0), key)
    turned = contract(
        jnp.concatenate([from_similar, from_mix], axis=0),
        jnp.concatenate([key, query], axis=0),
        0,
        0,
    )
    count = heads * GROUP
    d_scaled = d_right[:, :DK]
    d_query = growth * d_grown + plain[:count]
    d_key = beta * growth * d_scaled + closing * d_fading + plain[count:] + turned
    d_value = beta * d_right[:, DK:]
    grown_key = growth * key_wide
    ratio_similar = ratio_grad * similar
    flows = betas * ratio_similar + mixing * d_mixing
    fading_flow = d_fading * fading_wide
    sum_growth = jnp.sum(
        d_grown * grown_wide + d_scaled * (beta * grown_key) - fading_flow, axis=1, keepdims=True
    )
    sum_fading = jnp.sum(fading_flow, axis=1, keepdims=True)
    value_flow = d_right[:, DK:] * value.astype(f32)
    sum_beta = jnp.sum(
        d_scaled * grown_key + value_flow[:, :DK] + value_flow[:, DK:], axis=1, keepdims=True
    )
    flow_high, flow_low = halves(flows)
    ones = jnp.full((GROUP, 128), 1.0, bf16)
    turned_flow = contract(
        jnp.concatenate([flow_high, flow_low], axis=0),
        jnp.concatenate([ones, ones], axis=0),
        0,
        0,
    )[:, :1]
    owner = lane_heads(heads)
    lane = lax.broadcasted_iota(jnp.int32, (GROUP, 128), 1)
    d_sums = jnp.zeros((GROUP, 128), f32)
    d_beta = jnp.zeros((GROUP, 128), f32)
    d_last = jnp.zeros((1, 128), f32)
    for h in range(heads):
        rows = slice(h * GROUP, (h + 1) * GROUP)
        flow = jnp.sum(jnp.where(owner == h, flows, 0.0), axis=1, keepdims=True)
        more = jnp.sum(jnp.where(owner == h, ratio_similar, 0.0), axis=1, keepdims=True)
        d_sums = jnp.where(lane == h, sum_growth[rows] + flow - turned_flow[rows], d_sums)
        d_beta = jnp.where(lane == h, sum_beta[rows] + more, d_beta)
        total = jnp.sum(sum_fading[rows], axis=0, keepdims=True) + d_fades[h]
        d_last = jnp.where(lane[:1] == h, total, d_last)
    square_row = lax.broadcasted_iota(jnp.int32, (GROUP, GROUP), 0)
    square_lane = lax.broadcasted_iota(jnp.int32, (GROUP, GROUP), 1)
    later = jnp.where(square_row <= square_lane, 1.0, 0.0)
    d_decay = (summed_rows(later, d_sums) + d_last)[:, :heads]
    d_beta = d_beta[:, :heads]
    d_alpha = -d_decay * terms["rate"] * jax.nn.sigmoid(terms["alpha"]) * valid
    d_beta = d_beta * terms["beta"] * (1.0 - terms["beta"])
    scal_out[...] = jnp.concatenate([d_alpha, d_beta], axis=1).astype(bf16)
    rate_out[0:1, :] += jnp.sum(d_decay * terms["decay"], axis=0, keepdims=True)
    rate_out[1:2, :] += jnp.sum(d_alpha, axis=0, keepdims=True)

    first = group == 0
    after_keep = jnp.where(step == 0, 0.0, keep_ref[jnp.minimum(group + 1, groups - 1)])
    sections = (
        (query_pre, query_before, query_rim, conv_query, ext_query, dy_query, DK, d_query),
        (key_pre, key_before, key_rim, conv_key, ext_key, dy_key, DK, d_key),
        (value_pre, value_before, value_rim, conv_value, ext_value, dy_value, DV, d_value),
    )
    outs = (
        (query_out, query_conv_out),
        (key_out, key_conv_out),
        (value_out, value_conv_out),
    )
    for kind, (section, out) in enumerate(zip(sections, outs)):
        now_ref, before_ref, rim_ref, conv_ref, ext_ref, dy_ref, width, cotangent = section
        pre_out, conv_out = out
        first_lane = kind * heads * DK
        fill(ext_ref, now_ref, before_ref, rim_ref, first, keep)
        dy_ref[8 + GROUP :, :] = dy_ref[8:16, :] * after_keep
        for h in range(heads):
            lanes = pl.ds(h * width, width)
            rows = slice(h * GROUP, (h + 1) * GROUP)
            total = tap_sum(ext_ref, conv_ref, h * width, width)
            sigmoid = jax.nn.sigmoid(total)
            act = total * sigmoid
            d_act = cotangent[rows]
            if kind > 0:
                d_act = d_act * valid
            if kind < 2:
                scale = lax.rsqrt(jnp.sum(act * act, axis=1, keepdims=True) + epsilon_norm)
                inner = jnp.sum(act * d_act, axis=1, keepdims=True)
                d_act = scale * (d_act - act * (scale * scale * inner))
            if kind == 0:
                d_act = d_act * DK ** (-0.5)
            d_total = d_act * (sigmoid * (1.0 + total * (1.0 - sigmoid)))
            dy_ref[pl.ds(8, GROUP), lanes] = d_total
            for tap in range(CONV):
                product = d_total * ext_ref[pl.ds(HALO - tap, GROUP), lanes]
                conv_out[pl.ds(tap * 8, 8), lanes] += jnp.sum(
                    product.reshape(GROUP // 8, 8, width), axis=0
                )
            d_pre = d_total * conv_ref[0:1, lanes]
            for tap in range(1, CONV):
                d_pre = d_pre + dy_ref[pl.ds(8 + tap, GROUP), lanes] * conv_ref[tap : tap + 1, lanes]
            pre_out[:, lanes] = d_pre.astype(bf16)
            sending[step % 2, :, pl.ds(first_lane + h * width, width)] = d_pre.astype(bf16)

            @pl.when(step == 0)
            def _():
                tail_out[:, pl.ds(first_lane + h * width, width)] = d_pre[GROUP - 8 :]

            @pl.when(first)
            def _():
                d_back = dy_ref[pl.ds(1, 8), lanes] * conv_ref[1:2, lanes]
                for tap in range(2, CONV):
                    d_back = d_back + dy_ref[pl.ds(tap, 8), lanes] * conv_ref[tap : tap + 1, lanes]
                back_send[:, pl.ds(first_lane + h * width, width)] = d_back * keep

    transfer(step, group).start()

    @pl.when(step == 0)
    def _():
        tail_transfer.start()

    @pl.when(step == groups - 1)
    def _():
        @pl.when(seq >= 1)
        def _():
            own_transfer.start()

        @pl.when(even & (seq >= 2))
        def _():
            other_transfer.start()

        tail_transfer.wait_send()
        tail_transfer.wait_recv()
        got_tail_out[...] = tail_got[...]

        @pl.when(seq >= 1)
        def _():
            own_transfer.wait_send()

        @pl.when(even & (seq >= 2))
        def _():
            other_transfer.wait_send()

        @pl.when(seq + 1 < devices)
        def _():
            own_transfer.wait_recv()
            own_back_out[...] = own_got[...]

        @pl.when(seq + 1 >= devices)
        def _():
            own_back_out[...] = jnp.zeros_like(own_back_out)

        @pl.when(even & (seq + 2 < devices))
        def _():
            other_transfer.wait_recv()
            other_back_out[...] = other_got[...]

        @pl.when(even & (seq + 2 >= devices))
        def _():
            other_back_out[...] = jnp.zeros_like(other_back_out)

        @pl.when(seq % 2 == 1)
        def _():
            other_back_out[...] = back_send[...]

        transfer(step - 1, group + 1).wait_send()
        transfer(step, group).wait_send()
        for block in range(groups):
            transfer(step, block).wait_recv()


def delta_backward(pres, rims, convs, scal, rate, keep, made, entry, exit_grad, grad):
    tokens = scal.shape[0]
    heads, groups = (rate.shape[1], tokens // GROUP)
    widths = [pre.shape[1] for pre in pres]
    smem = pl.BlockSpec(memory_space=pltpu.SMEM)
    turn = lambda *shape: pl.BlockSpec(shape, lambda g: (groups - 1 - g, 0, 0))
    columns = 2 * heads
    return pl.pallas_call(
        functools.partial(backward_kernel, heads, groups, lax.axis_size("seq")),
        grid=(groups,),
        in_specs=[smem]
        + [token_block(w, groups) for w in widths]
        + [before_block(w, groups) for w in widths]
        + [whole((HALO, w)) for w in widths]
        + [whole((CONV, w)) for w in widths]
        + [token_block(scal.shape[1], groups), whole(rate.shape)]
        + [token_block(w, groups) for w in widths]
        + [
            turn(1, heads * GROUP, WIDE),
            token_block(heads * GROUP, groups),
            turn(1, heads * DK, WIDE),
            whole((heads * DK, DV)),
            whole((heads * DK, DV)),
            token_block(heads * DV, groups),
        ],
        out_specs=[token_block(w, groups) for w in widths]
        + [whole((CONV * 8, w)) for w in widths]
        + [token_block(columns, groups), whole((8, heads))]
        + [pl.BlockSpec(memory_space=pltpu.VMEM)]
        + [whole((8, sum(widths)))] * 3
        + [pl.BlockSpec(memory_space=pl.ANY)],
        out_shape=[jax.ShapeDtypeStruct((tokens, w), bf16) for w in widths]
        + [jax.ShapeDtypeStruct((CONV * 8, w), f32) for w in widths]
        + [
            jax.ShapeDtypeStruct((tokens, columns), bf16),
            jax.ShapeDtypeStruct((8, heads), f32),
            *[jax.ShapeDtypeStruct((8, sum(widths)), f32)] * 4,
            jax.ShapeDtypeStruct((tokens, sum(widths)), bf16),
        ],
        scratch_shapes=[pltpu.VMEM((heads * DK, DV), f32)]
        + [pltpu.VMEM((HALO + GROUP, w), f32) for w in widths]
        + [pltpu.VMEM((16 + GROUP, w), f32) for w in widths]
        + [
            pltpu.VMEM((2, GROUP, sum(widths)), bf16),
            pltpu.SemaphoreType.DMA((2,)),
            pltpu.SemaphoreType.DMA((groups,)),
            *[pltpu.VMEM((8, sum(widths)), f32)] * 4,
            pltpu.SemaphoreType.DMA((3,)),
            pltpu.SemaphoreType.DMA((3,)),
        ],
        compiler_params=pltpu.CompilerParams(
            vmem_limit_bytes=VMEM, collective_id=1, has_side_effects=True
        ),
        cost_estimate=pl.CostEstimate(flops=10**6, bytes_accessed=10**4, transcendentals=0),
        name="delta_backward",
    )(keep, *pres, *pres, *rims, *convs, scal, rate, *made, entry, exit_grad, grad)


def gated_forward_kernel(heads, linear_ref, local_ref, gate_ref, entry_ref, gain_ref, gated_out):
    for h in range(heads):
        wide = pl.ds(h * DV, DV)
        out = local_ref[:, wide] + contract(
            linear_ref[:, pl.ds(h * DK, DK)], entry_ref[pl.ds(h * DK, DK), :]
        )
        scale = lax.rsqrt(jnp.mean(out * out, axis=1, keepdims=True) + epsilon_gate)
        gate = gate_ref[:, wide]
        gated_out[:, wide] = (out * scale * gain_ref[...] * jax.nn.silu(gate)).astype(bf16)


def row_block(rows, width):
    return pl.BlockSpec((rows, width), lambda g: (g, 0))


def gated_forward(linear, local, gate, entry, gain):
    tokens, heads = (local.shape[0], local.shape[1] // DV)
    rows = 2 * GROUP
    return pl.pallas_call(
        functools.partial(gated_forward_kernel, heads),
        grid=(tokens // rows,),
        in_specs=[
            row_block(rows, heads * DK),
            row_block(rows, heads * DV),
            row_block(rows, heads * DV),
            whole((heads * DK, DV)),
            whole((1, DV)),
        ],
        out_specs=row_block(rows, heads * DV),
        out_shape=jax.ShapeDtypeStruct((tokens, heads * DV), bf16),
        compiler_params=pltpu.CompilerParams(vmem_limit_bytes=SMALL),
        cost_estimate=pl.CostEstimate(flops=10**9, bytes_accessed=10**7, transcendentals=0),
        name="gated_forward",
    )(linear, local, gate, entry, gain[None, :])


def gated_backward_kernel(
    heads,
    linear_ref,
    local_ref,
    gate_ref,
    entry_ref,
    gain_ref,
    grad_ref,
    valid_ref,
    delta_out,
    gate_out,
    gain_out,
    entry_out,
):
    @pl.when(pl.program_id(0) == 0)
    def _():
        gain_out[...] = jnp.zeros_like(gain_out)
        entry_out[...] = jnp.zeros_like(entry_out)

    rows = local_ref.shape[0]
    for h in range(heads):
        wide = pl.ds(h * DV, DV)
        linear = linear_ref[:, pl.ds(h * DK, DK)]
        out = local_ref[:, wide] + contract(linear, entry_ref[pl.ds(h * DK, DK), :])
        scale = lax.rsqrt(jnp.mean(out * out, axis=1, keepdims=True) + epsilon_gate)
        unit = out * scale
        gate = gate_ref[:, wide]
        sigmoid = jax.nn.sigmoid(gate)
        grad = grad_ref[:, wide]
        silu = gate * sigmoid
        product = grad * unit
        gain_out[...] += jnp.sum((product * silu).reshape(rows // 8, 8, DV), axis=0)
        gate_out[:, wide] = (
            product * gain_ref[...] * (sigmoid * (1.0 + gate * (1.0 - sigmoid)))
        ).astype(bf16)
        d_unit = grad * gain_ref[...] * silu
        inner = jnp.mean(d_unit * unit, axis=1, keepdims=True)
        delta = (scale * (d_unit - unit * inner) * valid_ref[...]).astype(bf16)
        delta_out[:, wide] = delta
        entry_out[pl.ds(h * DK, DK), :] += contract(linear, delta, 0, 0)


def gated_backward(linear, local, gate, entry, gain, grad, valid):
    tokens, heads = (local.shape[0], local.shape[1] // DV)
    rows = 2 * GROUP
    return pl.pallas_call(
        functools.partial(gated_backward_kernel, heads),
        grid=(tokens // rows,),
        in_specs=[
            row_block(rows, heads * DK),
            row_block(rows, heads * DV),
            row_block(rows, heads * DV),
            whole((heads * DK, DV)),
            whole((1, DV)),
            row_block(rows, heads * DV),
            row_block(rows, 1),
        ],
        out_specs=[
            row_block(rows, heads * DV),
            row_block(rows, heads * DV),
            whole((8, DV)),
            whole((heads * DK, DV)),
        ],
        out_shape=[
            jax.ShapeDtypeStruct((tokens, heads * DV), bf16),
            jax.ShapeDtypeStruct((tokens, heads * DV), bf16),
            jax.ShapeDtypeStruct((8, DV), f32),
            jax.ShapeDtypeStruct((heads * DK, DV), f32),
        ],
        compiler_params=pltpu.CompilerParams(vmem_limit_bytes=SMALL),
        cost_estimate=pl.CostEstimate(flops=10**6, bytes_accessed=10**4, transcendentals=0),
        name="gated_backward",
    )(linear, local, gate, entry, gain[None, :], grad, valid[:, None])


def column_place(tile, tiles, place):
    block, inner = (tile // (tiles // 4), tile % (tiles // 4))
    core = jnp.where(block < 2, 1 - place % 2, place % 2)
    chip = jnp.where(block % 2 == 0, 1 - place // 2, place // 2)
    return (chip * 2 + core) * (tiles // 4) + inner


def plain_dense_kernel(place_ref, left_ref, right_ref, out_ref):
    left = left_ref[:, : right_ref.shape[0]]
    out_ref[...] = contract(left, right_ref[...]).astype(bf16)


def plain_dense(left, right, place, tile=256):
    rows, cols = (left.shape[0], right.shape[1])
    tiles = cols // tile
    return pl.pallas_call(
        plain_dense_kernel,
        grid_spec=pltpu.PrefetchScalarGridSpec(
            num_scalar_prefetch=1,
            grid=(tiles,),
            in_specs=[
                pl.BlockSpec(left.shape, lambda i, place: (0, 0)),
                pl.BlockSpec(
                    (right.shape[0], tile), lambda i, place: (0, column_place(i, tiles, place[0]))
                ),
            ],
            out_specs=pl.BlockSpec((rows, tile), lambda i, place: (0, i)),
        ),
        out_shape=jax.ShapeDtypeStruct((rows, cols), bf16),
        compiler_params=pltpu.CompilerParams(vmem_limit_bytes=SMALL),
        cost_estimate=pl.CostEstimate(
            flops=2 * rows * cols * left.shape[1], bytes_accessed=10**7, transcendentals=0
        ),
        name="plain_dense",
    )(place, left, right)


def norm_dense_kernel(sides, place_ref, *refs):
    count = len(sides)
    lefts, rights = (refs[:count], refs[count : 2 * count])
    rows_ref, scale_ref, gain_ref, out_ref, gain_out, dots_out = refs[2 * count :]
    total = 0.0
    for left, right, side in zip(lefts, rights, sides):
        total = total + contract(left[:, : right.shape[side]], right[...], 1, side)
    out_ref[...] = total.astype(bf16)
    weighted = total * (rows_ref[...].astype(f32) * scale_ref[...])
    gain_out[...] = jnp.sum(weighted, axis=0, keepdims=True)
    dots = jnp.sum(weighted * gain_ref[...], axis=1, keepdims=True)

    @pl.when(pl.program_id(0) == 0)
    def _():
        dots_out[...] = dots

    @pl.when(pl.program_id(0) > 0)
    def _():
        dots_out[...] += dots


def norm_dense(pairs, rows, scale, gain, place, tile=256):
    tokens, cols = rows.shape
    tiles = cols // tile
    lefts, rights = ([left for left, _ in pairs], [right for _, right in pairs])
    placed = lambda i, place: (0, column_place(i, tiles, place[0]))
    upright = lambda i, place: (column_place(i, tiles, place[0]), 0)
    sides = [1 if right.shape[0] == cols else 0 for right in rights]
    return pl.pallas_call(
        functools.partial(norm_dense_kernel, sides),
        grid_spec=pltpu.PrefetchScalarGridSpec(
            num_scalar_prefetch=1,
            grid=(tiles,),
            in_specs=[pl.BlockSpec(left.shape, lambda i, place: (0, 0)) for left in lefts]
            + [
                pl.BlockSpec((tile, right.shape[1]), upright)
                if side
                else pl.BlockSpec((right.shape[0], tile), placed)
                for right, side in zip(rights, sides)
            ]
            + [
                pl.BlockSpec((tokens, tile), placed),
                pl.BlockSpec((tokens, 1), lambda i, place: (0, 0)),
                pl.BlockSpec((1, tile), placed),
            ],
            out_specs=[
                pl.BlockSpec((tokens, tile), lambda i, place: (0, i)),
                pl.BlockSpec((1, tile), placed),
                pl.BlockSpec((tokens, 1), lambda i, place: (0, 0)),
            ],
        ),
        out_shape=[
            jax.ShapeDtypeStruct((tokens, cols), bf16),
            jax.ShapeDtypeStruct((1, cols), f32),
            jax.ShapeDtypeStruct((tokens, 1), f32),
        ],
        compiler_params=pltpu.CompilerParams(vmem_limit_bytes=VMEM),
        cost_estimate=pl.CostEstimate(
            flops=2 * tokens * cols * sum(left.shape[1] for left in lefts),
            bytes_accessed=2 * 10**7,
            transcendentals=0,
        ),
        name="norm_dense",
    )(place, *lefts, *rights, rows, scale, gain[None, :])


def shifted(block, axis, distance):
    devices = range(lax.axis_size(axis))
    route = [(i - distance, i) for i in devices if i - distance in devices]
    return lax.ppermute(block, axis, route)


def exchanged(block, axis, bit):
    route = [(i, i ^ bit) for i in range(lax.axis_size(axis))]
    return lax.ppermute(block, axis, route)


def half(block, axis, at, count):
    width = block.shape[axis] // count
    return lax.dynamic_slice_in_dim(block, at * width, width, axis)


def weight_grad_kernel(turned, place_ref, rows_ref, got_rows_ref, cols_ref, got_cols_ref, out_ref):
    if turned:
        total = contract(cols_ref[...], rows_ref[...], 0, 0)
        total = total + contract(got_cols_ref[...], got_rows_ref[...], 0, 0)
        total = total[: out_ref.shape[0]]
    else:
        total = contract(rows_ref[...], cols_ref[...], 0, 0)
        total = total + contract(got_rows_ref[...], got_cols_ref[...], 0, 0)
    out_ref[...] = total.astype(bf16)


def pair_grad(rows, got_rows, cols, got_cols, turned, kept=None, spot=0):
    odd = lax.axis_index("seq").astype(jnp.int32) % 2
    devices = lax.axis_size("seq")
    tokens, padded = cols.shape
    count = padded if kept is None else kept
    width = rows.shape[1] // devices
    if width % 128:
        part = jnp.concatenate([own_half(rows, odd, width), got_rows], axis=0)
        got_cols = lax.slice_in_dim(got_cols, spot * padded, (spot + 1) * padded, axis=1)
        cols = jnp.concatenate([cols, got_cols], axis=0)[:, :count]
        if turned:
            part = part.reshape(2 * tokens, devices // 2, width)
            total = jnp.einsum("tn,tcw->cnw", cols, part, preferred_element_type=f32)
            return total.reshape(devices // 2 * count, width).astype(bf16)
        return dense(part.T, cols).astype(bf16)
    block = (count, width) if turned else (width, count)
    still = pl.BlockSpec((tokens, padded), lambda i, place: (0, 0))
    return pl.pallas_call(
        functools.partial(weight_grad_kernel, turned),
        grid_spec=pltpu.PrefetchScalarGridSpec(
            num_scalar_prefetch=1,
            grid=(devices // 2,),
            in_specs=[
                pl.BlockSpec((tokens, width), lambda i, place: (0, 2 * i + place[0])),
                pl.BlockSpec((tokens, width), lambda i, place: (0, i)),
                still,
                pl.BlockSpec((tokens, padded), lambda i, place: (0, spot)),
            ],
            out_specs=pl.BlockSpec(block, lambda i, place: (i, 0)),
        ),
        out_shape=jax.ShapeDtypeStruct((devices // 2 * block[0], block[1]), bf16),
        compiler_params=pltpu.CompilerParams(vmem_limit_bytes=SMALL),
        cost_estimate=pl.CostEstimate(flops=10**6, bytes_accessed=10**4, transcendentals=0),
        name="weight_grad",
    )(odd[None], rows, got_rows, cols, got_cols)


def triple_grad_kernel(
    place_ref, rows_ref, got_rows_ref, first_ref, second_ref, third_ref, got_ref, out_ref
):
    rows, got_rows = (rows_ref[...], got_rows_ref[...])
    start = 0
    for ref in (first_ref, second_ref, third_ref):
        spot = pl.ds(start, ref.shape[1])
        total = contract(rows, ref[...], 0, 0) + contract(got_rows, got_ref[:, spot], 0, 0)
        out_ref[:, spot] = total.astype(bf16)
        start += ref.shape[1]


def triple_grad(rows, got_rows, parts, got_all):
    odd = lax.axis_index("seq").astype(jnp.int32) % 2
    devices = lax.axis_size("seq")
    tokens, total = got_all.shape
    width = rows.shape[1] // devices
    if width % 128:
        part = jnp.concatenate([own_half(rows, odd, width), got_rows], axis=0)
        cols = jnp.concatenate([jnp.concatenate(parts, axis=1), got_all], axis=0)
        return dense(part.T, cols).astype(bf16)
    still = lambda cols: pl.BlockSpec((tokens, cols), lambda i, place: (0, 0))
    return pl.pallas_call(
        triple_grad_kernel,
        grid_spec=pltpu.PrefetchScalarGridSpec(
            num_scalar_prefetch=1,
            grid=(devices // 2,),
            in_specs=[
                pl.BlockSpec((tokens, width), lambda i, place: (0, 2 * i + place[0])),
                pl.BlockSpec((tokens, width), lambda i, place: (0, i)),
                *[still(part.shape[1]) for part in parts],
                still(total),
            ],
            out_specs=pl.BlockSpec((width, total), lambda i, place: (i, 0)),
        ),
        out_shape=jax.ShapeDtypeStruct((devices // 2 * width, total), bf16),
        compiler_params=pltpu.CompilerParams(vmem_limit_bytes=SMALL),
        cost_estimate=pl.CostEstimate(flops=10**6, bytes_accessed=10**4, transcendentals=0),
        name="triple_grad",
    )(odd[None], rows, got_rows, *parts, got_all)


def line_kernel(
    planes,
    kept_ref,
    across_ref,
    out_ref,
    across_out,
    up_send,
    up_got,
    down_send,
    down_got,
    send_sem,
    recv_sem,
    across_sem,
):
    seq, head = (lax.axis_index("seq"), lax.axis_index("head"))
    plane = seq // 2
    mesh = pl.DeviceIdType.MESH
    lower, upper = (plane > 0, plane < planes - 1)
    beside = head + 2 - 4 * (head // 2)
    barrier = pltpu.get_barrier_semaphore()
    pl.semaphore_signal(barrier, inc=1, device_id=(seq, beside), device_id_type=mesh)

    @pl.when(lower)
    def _():
        pl.semaphore_signal(barrier, inc=1, device_id=(seq - 2, head), device_id_type=mesh)

    @pl.when(upper)
    def _():
        pl.semaphore_signal(barrier, inc=1, device_id=(seq + 2, head), device_id_type=mesh)

    @pl.when(lower & upper)
    def _():
        pl.semaphore_wait(barrier, 3)

    @pl.when((plane == 0) | (plane == planes - 1))
    def _():
        pl.semaphore_wait(barrier, 2)

    crossing = pltpu.make_async_remote_copy(
        src_ref=across_ref,
        dst_ref=across_out,
        send_sem=across_sem.at[0],
        recv_sem=across_sem.at[1],
        device_id=(seq, beside),
        device_id_type=mesh,
    )
    crossing.start()
    ways = ((up_send, up_got, 2, 0), (down_send, down_got, -2, 1))

    def transfer(way, step):
        send, got, hop, side = ways[way]
        return pltpu.make_async_remote_copy(
            src_ref=send.at[step - 1],
            dst_ref=got.at[step - 1],
            send_sem=send_sem.at[side, step - 1],
            recv_sem=recv_sem.at[side, step - 1],
            device_id=(seq + hop, head),
            device_id_type=mesh,
        )

    rows = out_ref.shape[0]
    slab = 2 * HALO

    def each(body):
        def run(i, carry):
            body(pl.ds(pl.multiple_of(i * slab, slab), slab))
            return carry

        lax.fori_loop(0, rows // slab, run, 0)

    for step in range(1, planes):
        for way in range(2):
            send, got, hop, side = ways[way]
            rank = plane if way == 0 else planes - 1 - plane
            at = plane + planes - step if way == 0 else plane - planes + step

            @pl.when((rank < step) & (rank == 0))
            def _(send=send, at=at, way=way, step=step):
                def body(span):
                    send[step - 1, span, :] = kept_ref[at, span, :]

                each(body)
                transfer(way, step).start()

            if step > 1:

                @pl.when((rank < step) & (rank > 0) & (rank < planes - 1))
                def _(send=send, got=got, at=at, way=way, step=step):
                    transfer(way, step - 1).wait_recv()

                    def body(span):
                        total = kept_ref[at, span, :].astype(f32)
                        total = total + got[step - 2, span, :].astype(f32)
                        send[step - 1, span, :] = total.astype(bf16)

                    each(body)
                    transfer(way, step).start()

    def own(span):
        out_ref[span, :] = kept_ref[plane, span, :].astype(f32)

    each(own)
    for way in range(2):
        got = ways[way][1]

        @pl.when(lower if way == 0 else upper)
        def _(got=got, way=way):
            transfer(way, planes - 1).wait_recv()

            def body(span):
                out_ref[span, :] += got[planes - 2, span, :].astype(f32)

            each(body)

    for step in range(1, planes):
        for way in range(2):
            rank = plane if way == 0 else planes - 1 - plane

            @pl.when((rank < step) & (rank < planes - 1))
            def _(way=way, step=step):
                transfer(way, step).wait_send()

    crossing.wait()


def line_summed(kept, across):
    planes = lax.axis_size("seq") // 2
    rows, cols = (kept.shape[0] // planes, kept.shape[1])
    if planes > 4 or rows % (2 * HALO):
        return seq_scattered(kept), exchanged(across, "head", 2)
    slots = pltpu.VMEM((planes - 1, rows, cols), bf16)
    return pl.pallas_call(
        functools.partial(line_kernel, planes),
        in_specs=[pl.BlockSpec(memory_space=pltpu.VMEM)] * 2,
        out_specs=[pl.BlockSpec(memory_space=pltpu.VMEM)] * 2,
        out_shape=[
            jax.ShapeDtypeStruct((rows, cols), f32),
            jax.ShapeDtypeStruct(across.shape, bf16),
        ],
        scratch_shapes=[slots] * 4
        + [pltpu.SemaphoreType.DMA((2, planes - 1))] * 2
        + [pltpu.SemaphoreType.DMA((2,))],
        compiler_params=pltpu.CompilerParams(
            vmem_limit_bytes=VMEM, collective_id=2, has_side_effects=True
        ),
        cost_estimate=pl.CostEstimate(flops=9 * 10**10, bytes_accessed=10**7, transcendentals=0),
        name="line_sum",
    )(kept.reshape(planes, rows, cols), across)


def partner_rows(block):
    width = block.shape[1] * 4 // lax.axis_size("seq")
    odd = lax.axis_index("seq") % 2
    if block.shape[1] == 2 * width:
        part = half(block, 1, 1 - odd, 2)
    else:
        part = own_half(block, 1 - odd, width)
    return exchanged(part, "seq", 1)


def gather_kernel(norm, place_ref, *refs):
    blocks = [ref[...] for ref in refs[:4]]
    width = blocks[0].shape[1]
    place = place_ref[0]
    out_ref = refs[5] if norm else refs[4]
    spots = [pl.ds(pl.multiple_of((place ^ at) * width, 128), width) for at in range(4)]
    for block, spot in zip(blocks, spots):
        out_ref[:, spot] = block
    if norm:
        gain_ref, normed_out, scale_out = (refs[4], refs[6], refs[7])
        wides = [block.astype(f32) for block in blocks]
        total = sum(jnp.sum(wide * wide, axis=1, keepdims=True) for wide in wides)
        scale = lax.rsqrt(total / (4 * width) + epsilon_norm)
        scale_out[...] = scale
        for wide, spot in zip(wides, spots):
            normed_out[:, spot] = (wide * scale * gain_ref[:, spot]).astype(bf16)


def head_gathered(block, gain=None):
    place = lax.axis_index("head").astype(jnp.int32)
    tokens, width = block.shape
    across = exchanged(block, "head", 2)
    beside = exchanged(block, "head", 1)
    corner = exchanged(across, "head", 1)
    rows = 4 * GROUP
    norm = gain is not None
    spec = lambda cols: pl.BlockSpec((rows, cols), lambda i, place: (i, 0))
    whole_shape = jax.ShapeDtypeStruct((tokens, 4 * width), bf16)
    out_specs, out_shape = (spec(4 * width), whole_shape)
    if norm:
        out_specs = [out_specs, spec(4 * width), spec(1)]
        out_shape = [whole_shape, whole_shape, jax.ShapeDtypeStruct((tokens, 1), f32)]
    gain_spec = pl.BlockSpec((1, 4 * width), lambda i, place: (0, 0))
    return pl.pallas_call(
        functools.partial(gather_kernel, norm),
        grid_spec=pltpu.PrefetchScalarGridSpec(
            num_scalar_prefetch=1,
            grid=(tokens // rows,),
            in_specs=[spec(width)] * 4 + ([gain_spec] if norm else []),
            out_specs=out_specs,
        ),
        out_shape=out_shape,
        compiler_params=pltpu.CompilerParams(vmem_limit_bytes=SMALL),
        cost_estimate=pl.CostEstimate(flops=10**6, bytes_accessed=6 * 10**6, transcendentals=0),
        name="gather",
    )(place[None], block, beside, across, corner, *([gain[None, :]] if norm else []))


def rows_dense_kernel(left_ref, right_ref, out_ref):
    out_ref[...] = contract(left_ref[...], right_ref[...], 1, 1)


def rows_dense(left, right):
    tokens, rows = (left.shape[0], 4 * GROUP)
    return pl.pallas_call(
        rows_dense_kernel,
        grid=(tokens // rows,),
        in_specs=[row_block(rows, left.shape[1]), whole(right.shape)],
        out_specs=row_block(rows, right.shape[0]),
        out_shape=jax.ShapeDtypeStruct((tokens, right.shape[0]), f32),
        compiler_params=pltpu.CompilerParams(vmem_limit_bytes=SMALL),
        cost_estimate=pl.CostEstimate(
            flops=2 * left.size * right.shape[0], bytes_accessed=10**7, transcendentals=0
        ),
        name="rows_dense",
    )(left, right)


def ffn_kernel(normed_ref, gate_ref, up_ref, grad_ref, inner_out, d_gate_out, d_up_out):
    normed = normed_ref[...]
    gate = contract(normed, gate_ref[...], 1, 1)
    up = contract(normed, up_ref[...], 1, 1)
    sigmoid = jax.nn.sigmoid(gate)
    silu = gate * sigmoid
    grad = grad_ref[...]
    padding = inner_out.shape[1] - gate.shape[1]
    for ref, values in (
        (inner_out, silu * up),
        (d_gate_out, grad * up * (sigmoid * (1.0 + gate * (1.0 - sigmoid)))),
        (d_up_out, grad * silu),
    ):
        values = values.astype(bf16)
        if padding:
            values = jnp.pad(values, ((0, 0), (0, padding)))
        ref[...] = values


def ffn(normed, w_gate, w_up, grad):
    tokens, count = grad.shape
    rows, padded = (4 * GROUP, -(-count // 128) * 128)
    return pl.pallas_call(
        ffn_kernel,
        grid=(tokens // rows,),
        in_specs=[row_block(rows, normed.shape[1])]
        + [whole(w_gate.shape)] * 2
        + [row_block(rows, count)],
        out_specs=[row_block(rows, padded)] * 3,
        out_shape=[jax.ShapeDtypeStruct((tokens, padded), bf16)] * 3,
        compiler_params=pltpu.CompilerParams(vmem_limit_bytes=VMEM),
        cost_estimate=pl.CostEstimate(
            flops=4 * normed.size * count, bytes_accessed=2 * 10**7, transcendentals=0
        ),
        name="ffn",
    )(normed, w_gate, w_up, grad)


def tied(*values):
    return lax.optimization_barrier(values)


def head_scattered(partial):
    width = partial.shape[1] // 2
    mine = partial[:, width:].astype(f32) + exchanged(partial[:, :width], "head", 1).astype(f32)
    width = width // 2
    return mine[:, width:] + exchanged(mine[:, :width].astype(bf16), "head", 2).astype(f32)


def head_summed(values):
    bit = 1
    while bit < lax.axis_size("head"):
        values = values + exchanged(values, "head", bit)
        bit = bit * 2
    return values


def own_half(rows, odd, width):
    tokens, total = rows.shape
    parts = rows.reshape(tokens, total // (2 * width), 2, width)
    return lax.dynamic_index_in_dim(parts, odd, 2, False).reshape(tokens, total // 2)


def seq_scattered(mine):
    devices = lax.axis_size("seq")
    groups = [list(range(first, devices, 2)) for first in range(2)]
    return lax.psum_scatter(
        mine.astype(bf16), "seq", scatter_dimension=0, axis_index_groups=groups, tiled=True
    ).astype(f32)


def composed(later, before):
    moved = jnp.einsum(
        "hij,hjk->hik", later[:, :, :DK].astype(bf16), before, preferred_element_type=f32
    )
    linear = moved.shape[2] - DV
    offset = later[:, :, DK:] + moved[:, :, linear:]
    return jnp.concatenate([moved[:, :, :linear], offset], axis=2)


def prefix(pair, got, direction):
    odd = lax.axis_index("seq") % 2
    front = odd == 1 if direction == 1 else odd == 0
    wide = got.astype(f32)
    low = pair.astype(bf16)
    closed = composed(jnp.where(front, pair, wide), jnp.where(front, got, low))
    distance = 2
    before = shifted(closed.astype(bf16), "seq", direction * distance)
    opened = before.astype(f32)
    while True:
        closed = composed(closed, before)
        distance = distance * 2
        last = distance * 2 >= lax.axis_size("seq")
        sent = closed[:, :, DK:] if last else closed
        before = shifted(sent.astype(bf16), "seq", direction * distance)
        opened = composed(opened, before)
        if last:
            break
    opened = opened[:, :, -DV:]
    moved = composed(wide, opened.astype(bf16))[:, :, -DV:]
    return jnp.where(front, moved, opened)


def layout(lengths, positions):
    padded = (lengths + (GROUP - 1)) // GROUP * GROUP
    seq_ends = jnp.cumsum(padded)
    begins = seq_ends - padded
    offset = positions[:, None] - begins[None, :]
    inside = (offset >= 0) & (positions[:, None] < seq_ends[None, :])
    valid_mask = jnp.any(inside & (offset < lengths[None, :]), axis=1).astype(jnp.float32)
    starts = jnp.any(offset == 0, axis=1).astype(jnp.float32)
    return (valid_mask, starts)


def dense(left, right):
    return jnp.dot(left, right, preferred_element_type=jnp.float32)


def shards(
    hidden_in,
    lengths,
    attn_gain,
    w_query,
    w_key,
    w_value,
    w_gate,
    w_alpha,
    w_beta,
    conv_query,
    conv_key,
    conv_value,
    decay_log,
    decay_bias,
    out_gain,
    w_out,
    ffn_gain,
    w_ffn_gate,
    w_ffn_up,
    w_ffn_down,
    grad_out,
):
    token_rows = hidden_in.shape[0]
    head_count = w_alpha.shape[1]
    col_width = grad_out.shape[1]
    devices = lax.axis_size("seq")
    positions = lax.axis_index("seq") * token_rows + jnp.arange(token_rows, dtype=jnp.int32)
    valid_mask, starts = layout(lengths, positions)
    keep_flags = 1.0 - starts[::GROUP]
    head_place = lax.axis_index("head")
    place = head_place[None].astype(jnp.int32)
    head_first = head_place * head_count
    col_first = head_place * col_width
    cols = lambda rows: lax.dynamic_slice_in_dim(rows, col_first, col_width, rows.ndim - 1)
    local_log = lax.dynamic_slice_in_dim(decay_log, head_first, head_count)
    local_bias = lax.dynamic_slice_in_dim(decay_bias, head_first, head_count)

    inputs32 = hidden_in.astype(f32)
    attn_scale = lax.rsqrt(jnp.mean(inputs32 * inputs32, axis=-1, keepdims=True) + epsilon_norm)
    normed = (inputs32 * attn_scale * attn_gain).astype(bf16)
    pres = [dense(normed, weight).astype(bf16) for weight in (w_query, w_key, w_value)]
    widths = [pre.shape[1] for pre in pres]
    edges = [0, widths[0], widths[0] + widths[1], sum(widths)]
    split = lambda rows: [rows[:, a:b] for a, b in zip(edges[:-1], edges[1:])]
    tail_first = token_rows - (CONV - 1)
    rims = shifted(jnp.concatenate([pre[tail_first:] for pre in pres], 1), "seq", 1)
    rims, grad_cols, normed_cols = tied(rims, grad_out, cols(normed))
    got_grad_rows = head_gathered(partner_rows(grad_cols))
    got_normed = head_gathered(partner_rows(normed_cols))
    rims = split(jnp.pad(rims, ((HALO - (CONV - 1), 0), (0, 0))))
    w_scal = jnp.concatenate([w_alpha, w_beta], axis=1)
    scal = jnp.concatenate([dense(normed, w_scal), valid_mask[:, None]], axis=1)
    rate = jnp.stack([jnp.exp(local_log), local_bias])
    convs = [conv_query, conv_key, conv_value]
    *made, linear, local, device_pair = delta_forward(
        pres, rims, convs, scal, rate, keep_flags
    )
    grad_rows = head_gathered(grad_out)
    device_pair, grad_rows = tied(device_pair, grad_rows)
    device_pair = device_pair.reshape(head_count, DK, WIDE)
    got_pair = exchanged(device_pair.astype(bf16), "seq", 1)
    entry = prefix(device_pair, got_pair, 1).astype(bf16).reshape(head_count * DK, DV)
    gate_pre = dense(normed, w_gate)
    d_inner = rows_dense(grad_rows, w_ffn_down)
    entry, d_inner, gate_pre, got_grad_rows, got_normed = tied(
        entry, d_inner, gate_pre, got_grad_rows, got_normed
    )
    gated = gated_forward(linear, local, gate_pre, entry, out_gain)
    mixed = head_scattered(plain_dense(gated, w_out, place))
    middle = cols(hidden_in).astype(f32) + mixed
    sent, normed_ffn, ffn_scale = head_gathered(middle.astype(bf16), ffn_gain)
    got_gated = exchanged(gated, "seq", 1)
    d_inner, got_gated = tied(d_inner, got_gated)
    inner_act, d_ffn_gate, d_ffn_up = ffn(normed_ffn, w_ffn_gate.T, w_ffn_up.T, d_inner)
    units = w_ffn_gate.shape[1]
    got_ffn_cols = partner_rows(cols(normed_ffn))
    inner_sent, d_ffn_gate, got_ffn_cols = tied(inner_act, d_ffn_gate, got_ffn_cols)
    got_inner = exchanged(inner_sent, "seq", 1)
    d_normed_ffn, grad_ffn_gain, ffn_dots = norm_dense(
        [(d_ffn_gate, w_ffn_gate.T), (d_ffn_up, w_ffn_up.T)], sent, ffn_scale, ffn_gain, place
    )
    ffn_dots = head_summed(ffn_dots[:, 0])[:, None] / sent.shape[1]
    d_sent_cols = ffn_scale * (
        cols(ffn_gain) * head_scattered(d_normed_ffn)
        - cols(sent).astype(f32) * ffn_scale * ffn_dots
    )
    d_middle = grad_out.astype(f32) + d_sent_cols
    got_normed_ffn = head_gathered(got_ffn_cols)
    middle_cols, got_normed_ffn = tied(d_middle.astype(bf16), got_normed_ffn)
    d_mixed = head_gathered(middle_cols)
    d_gated = dense(d_mixed, w_out.T)
    got_mixed_cols = partner_rows(middle_cols)
    d_gate_sent, got_inner, got_mixed_cols = tied(d_ffn_gate, got_inner, got_mixed_cols)
    got_d_gate = exchanged(d_gate_sent, "seq", 1)
    kept_down = pair_grad(grad_rows, got_grad_rows, inner_act, got_inner, True, units)
    grad_w_ffn_down = seq_scattered(kept_down)
    d_gated, kept_down = tied(d_gated, kept_down)
    d_delta, d_gate_pre, gain_part, entry_grad = gated_backward(
        linear, local, gate_pre, entry, out_gain, d_gated, valid_mask
    )
    back_pair = jnp.concatenate(
        [
            jnp.swapaxes(device_pair[:, :, :DK], 1, 2),
            entry_grad.reshape(head_count, DK, DV),
        ],
        axis=2,
    )
    back_pair, got_d_gate = tied(back_pair, got_d_gate)
    got_back = exchanged(back_pair.astype(bf16), "seq", 1)
    d_up_sent, got_mixed_cols, inner_late, got_back = tied(
        d_ffn_up, got_mixed_cols, inner_act, got_back
    )
    got_d_up = exchanged(d_up_sent, "seq", 1)
    kept_gate = pair_grad(normed_ffn, got_normed_ffn, d_ffn_gate, got_d_gate, True, units)
    got_d_mixed = head_gathered(got_mixed_cols)
    kept_out = pair_grad(d_mixed, got_d_mixed, gated, got_gated, True)
    ffn_out = head_scattered(plain_dense(inner_late, w_ffn_down, place))
    hidden_out = (middle + ffn_out).astype(bf16)
    exit_grad = prefix(back_pair, got_back, -1).reshape(head_count * DK, DV)
    exit_grad, kept_gate, kept_out, grad_w_ffn_down, hidden_out, got_d_up = tied(
        exit_grad, kept_gate, kept_out, grad_w_ffn_down, hidden_out, got_d_up
    )
    grad_w_ffn_gate = seq_scattered(kept_gate)
    grad_w_out = seq_scattered(kept_out)
    results = delta_backward(
        pres, rims, convs, scal, rate, keep_flags, made, entry, exit_grad, d_delta
    )
    d_pres, conv_parts = (results[:3], results[3:6])
    d_scal, d_rate, tails, own_back, other_back, got_tails, got_all = results[6:]
    d_scal, gate_sent, d_up_late = tied(d_scal, d_gate_pre, d_ffn_up)
    gate_middle = gate_sent.shape[1] // 2
    got_gate_low = exchanged(gate_sent[:, :gate_middle], "seq", 1)
    got_gate_high = exchanged(gate_sent[:, gate_middle:], "seq", 1)
    kept_up = pair_grad(normed_ffn, got_normed_ffn, d_up_late, got_d_up, True, units)
    grad_w_ffn_up = seq_scattered(kept_up)
    got_all = lax.dynamic_update_slice(
        got_all, (got_tails + other_back).astype(bf16), (token_rows - 8, 0)
    )
    d_query_pre, d_key_pre, d_value_pre = [
        lax.dynamic_update_slice(d_pre, tail.astype(bf16), (token_rows - 8, 0))
        for d_pre, tail in zip(d_pres, split(tails + own_back))
    ]
    kept_last = triple_grad(
        normed, got_normed, [d_query_pre, d_key_pre, d_value_pre], got_all
    )
    d_scal, kept_last, grad_w_ffn_gate, kept_up, got_gate_low = tied(
        d_scal, kept_last, grad_w_ffn_gate, kept_up, got_gate_low
    )
    gain_count = out_gain.shape[0]
    full_log, full_bias = [
        lax.dynamic_update_slice_in_dim(
            jnp.zeros(decay_log.shape, f32), d_rate[i], head_first, 0
        )
        for i in range(2)
    ]
    d_normed, grad_attn_gain, attn_dots = norm_dense(
        [
            (d_query_pre, w_query),
            (d_key_pre, w_key),
            (d_value_pre, w_value),
            (d_gate_pre, w_gate),
            (d_scal, w_scal),
        ],
        hidden_in,
        attn_scale,
        attn_gain,
        place,
    )
    d_normed, got_gate_high = tied(d_normed, got_gate_high)
    got_d_gate_pre = jnp.concatenate([got_gate_low, got_gate_high], axis=1)
    kept_w_gate = pair_grad(normed, got_normed, d_gate_pre, got_d_gate_pre, False)
    grad_w_gate = seq_scattered(kept_w_gate)
    attn_dots, kept_w_gate = tied(attn_dots, kept_w_gate)
    wide = d_normed.shape[1] // 2
    mine = d_normed[:, wide:].astype(f32) + exchanged(d_normed[:, :wide], "head", 1).astype(f32)
    across = mine[:, : wide // 2].astype(bf16)
    model = attn_gain.shape[0]
    packed_sums = head_summed(
        jnp.concatenate(
            [
                attn_dots[:, 0],
                grad_attn_gain[0],
                grad_ffn_gain[0],
                jnp.sum(gain_part, 0),
                full_log,
                full_bias,
            ]
        )
    )
    packed_sums, across = tied(packed_sums, across)
    attn_dots = packed_sums[:token_rows, None] / hidden_in.shape[1]
    small = dense(d_scal.T, normed)
    small = [jnp.swapaxes(small.reshape(2 * head_count, devices, -1), 0, 1).reshape(devices, -1)]
    for part in conv_parts:
        part = jnp.sum(part.reshape(CONV, 8, -1), axis=1).reshape(CONV, devices, -1)
        small.append(jnp.swapaxes(part, 0, 1).reshape(devices, -1))
    sums = packed_sums[token_rows + 2 * model :]
    for first in (token_rows, token_rows + model):
        small.append(packed_sums[first : first + model].reshape(devices, -1))
    small.append(jnp.broadcast_to(sums, (devices, sums.shape[0])))
    small = jnp.concatenate(small, axis=1)
    small = jnp.pad(small, ((0, 0), (0, -small.shape[1] % 2048)))
    small_width = small.shape[1]
    odd = lax.axis_index("seq") % 2
    small = small.reshape(devices // 2, 2, small_width // 128, 128)
    got = exchanged(lax.dynamic_index_in_dim(small, 1 - odd, 1, False), "seq", 1)
    small = lax.dynamic_index_in_dim(small, odd, 1, False) + got
    small = small.reshape(devices * small_width // 256, 128)
    small_sum = lax.psum_scatter(
        small,
        "seq",
        scatter_dimension=0,
        axis_index_groups=[list(range(first, devices, 2)) for first in range(2)],
        tiled=True,
    )
    kept_last, across, small, grad_w_out, kept_w_gate = tied(
        kept_last, across, small, grad_w_out, kept_w_gate
    )
    last_grads, across = line_summed(kept_last, across)
    grad_w_query, grad_w_key, grad_w_value = split(last_grads)
    small = small_sum.reshape(small_width)
    small_pieces = []
    for rows, width in [(head_count, model // devices)] * 2 + [
        (CONV, width // devices) for width in widths
    ]:
        piece = small[: rows * width].reshape(rows, width)
        small_pieces.append(piece.T if len(small_pieces) < 2 else piece)
        small = small[rows * width :]
    grad_attn_rows, grad_ffn_rows = (
        small[: model // devices],
        small[model // devices : 2 * (model // devices)],
    )
    sums = small[2 * (model // devices) :]
    grad_in = d_middle + attn_scale * (
        cols(attn_gain) * (mine[:, wide // 2 :] + across.astype(f32))
        - cols(hidden_in).astype(f32) * attn_scale * attn_dots
    )
    log_first = gain_count
    bias_first = log_first + decay_log.shape[0]
    return (
        hidden_out,
        grad_in,
        grad_attn_rows,
        grad_w_query,
        grad_w_key,
        grad_w_value,
        grad_w_gate,
        *small_pieces,
        sums[log_first:bias_first],
        sums[bias_first : bias_first + decay_bias.shape[0]],
        sums[:gain_count],
        grad_w_out,
        grad_ffn_rows,
        grad_w_ffn_gate.T,
        grad_w_ffn_up.T,
        grad_w_ffn_down,
    )


def solution(mesh):
    return jax.shard_map(
        shards,
        mesh=mesh,
        in_specs=(
            P("seq", None),
            P(),
            P(),
            P(None, "head"),
            P(None, "head"),
            P(None, "head"),
            P(None, "head"),
            P(None, "head"),
            P(None, "head"),
            P(None, "head"),
            P(None, "head"),
            P(None, "head"),
            P(),
            P(),
            P(),
            P("head", None),
            P(),
            P(None, "head"),
            P(None, "head"),
            P("head", None),
            P("seq", "head"),
        ),
        out_specs=(
            P("seq", "head"),
            P("seq", "head"),
            P("seq"),
            P("seq", "head"),
            P("seq", "head"),
            P("seq", "head"),
            P("seq", "head"),
            P("seq", "head"),
            P("seq", "head"),
            P(None, ("head", "seq")),
            P(None, ("head", "seq")),
            P(None, ("head", "seq")),
            P(),
            P(),
            P(),
            P("head", "seq"),
            P("seq"),
            P("seq", "head"),
            P("seq", "head"),
            P("head", "seq"),
        ),
        check_vma=False,
    )
```

```python
import functools

import jax
import jax.numpy as jnp
from jax import lax
from jax.experimental import pallas as pl
from jax.experimental.pallas import tpu as pltpu
from jax.sharding import PartitionSpec as P

DK = 128
DV = 256
GROUP = 64
CONV = 4
HALO = 16
WIDE = DK + DV
VMEM = 60 * 2**20
SMALL = 30 * 2**20

epsilon_norm = 1e-06
epsilon_gate = 1e-05

f32 = jnp.float32
bf16 = jnp.bfloat16


def contract(left, right, left_dim=1, right_dim=0):
    return lax.dot_general(
        left, right, (((left_dim,), (right_dim,)), ((), ())), preferred_element_type=f32
    )


def lane_heads(heads):
    return lax.broadcasted_iota(jnp.int32, (1, heads * GROUP), 1) // GROUP


def packed(full, heads):
    owner = lane_heads(heads)
    result = full[:GROUP]
    for head in range(1, heads):
        result = jnp.where(owner == head, full[head * GROUP : (head + 1) * GROUP], result)
    return result


def diagonal(values, heads):
    owner = lane_heads(heads)
    low = values.astype(bf16)
    return jnp.concatenate(
        [low * jnp.where(owner == head, 1.0, 0.0).astype(bf16) for head in range(heads)], axis=0
    )


def spread(columns, heads):
    owner = lane_heads(heads)
    result = jnp.broadcast_to(columns[0], (GROUP, heads * GROUP))
    for head in range(1, heads):
        result = jnp.where(owner == head, columns[head], result)
    return result


def halves(values):
    high = values.astype(bf16)
    return high, (values - high.astype(f32)).astype(bf16)


def product3(left, right, heads):
    left_high, left_low = halves(left)
    right_high, right_low = halves(right)
    rows = left.shape[0]
    first = contract(jnp.concatenate([left_high, left_low], axis=0), diagonal(right_high, heads))
    return first[:rows] + first[rows:] + contract(left_high, diagonal(right_low, heads))


def packed_inverse(coupling, heads):
    row = lax.broadcasted_iota(jnp.int32, coupling.shape, 0)
    lane = lax.broadcasted_iota(jnp.int32, coupling.shape, 1) % GROUP
    power = -coupling
    result = jnp.where(row == lane, 1.0, 0.0) + power
    power = product3(power, power, heads)
    degree = 2
    while degree * 2 < GROUP:
        both = product3(jnp.concatenate([result, power], axis=0), power, heads)
        result = result + both[:GROUP]
        power = both[GROUP:]
        degree = degree * 2
    return result + product3(result, power, heads)


def stacked(block, heads):
    width = block.shape[1] // heads
    return jnp.concatenate([block[:, h * width : (h + 1) * width] for h in range(heads)], axis=0)


def unstacked(block, heads):
    return jnp.concatenate([block[h * GROUP : (h + 1) * GROUP] for h in range(heads)], axis=1)


def fill(ext_ref, now_ref, before_ref, rim_ref, first, keep):
    before = jnp.where(first, rim_ref[...].astype(f32), before_ref[...].astype(f32))
    ext_ref[:HALO, :] = before * keep
    ext_ref[HALO:, :] = now_ref[...].astype(f32)


def tap_sum(ext_ref, conv_ref, low, width):
    total = ext_ref[pl.ds(HALO, GROUP), pl.ds(low, width)] * conv_ref[0:1, pl.ds(low, width)]
    for tap in range(1, CONV):
        total = total + (
            ext_ref[pl.ds(HALO - tap, GROUP), pl.ds(low, width)]
            * conv_ref[tap : tap + 1, pl.ds(low, width)]
        )
    return total


def summed_rows(mask, values, pieces=3):
    parts = []
    for _ in range(pieces):
        parts.append(values.astype(bf16))
        values = values - parts[-1].astype(f32)
    width = values.shape[1]
    sums = contract(mask.astype(bf16), jnp.concatenate(parts, axis=1))
    return sum(sums[:, i * width : (i + 1) * width] for i in range(pieces))


def token_terms(scal_ref, rate_ref, heads):
    scal = scal_ref[...]
    rate = rate_ref[...]
    shifted_alpha = scal[:, :heads] + rate[1:2]
    valid = scal[:, 2 * heads : 2 * heads + 1]
    decay = -rate[0:1] * jax.nn.softplus(shifted_alpha) * valid
    beta = jax.nn.sigmoid(scal[:, heads : 2 * heads])
    row = lax.broadcasted_iota(jnp.int32, (GROUP, heads * GROUP), 0)
    lane = lax.broadcasted_iota(jnp.int32, (GROUP, heads * GROUP), 1) % GROUP
    wide = spread([decay[:, h : h + 1] for h in range(heads)], heads)
    square_row = lax.broadcasted_iota(jnp.int32, (GROUP, GROUP), 0)
    square_lane = lax.broadcasted_iota(jnp.int32, (GROUP, GROUP), 1)
    sums = summed_rows(jnp.where(square_row >= square_lane, 1.0, 0.0), wide)
    across = jnp.sum(jnp.where(row <= lane, wide, 0.0), axis=0, keepdims=True)
    lower, strict = (row >= lane, row > lane)
    ratio = jnp.where(lower, jnp.exp(jnp.where(lower, sums - across, 0.0)), 0.0)
    betas = [beta[:, h : h + 1] for h in range(heads)]
    last = sums[GROUP - 1 :]
    grown, closing = (jnp.exp(sums), jnp.exp(last - sums))
    column = lambda values: jnp.concatenate(
        [values[:, h * GROUP : h * GROUP + 1] for h in range(heads)], axis=0
    )
    fade = jnp.exp(last)
    fades = [fade[:, h * GROUP : h * GROUP + 1] for h in range(heads)]
    return dict(
        alpha=shifted_alpha,
        rate=rate[0:1],
        valid=valid,
        decay=decay,
        beta=beta,
        ratio=ratio,
        strict=strict,
        betas=spread(betas, heads),
        beta_column=jnp.concatenate(betas, axis=0),
        growth=column(grown),
        closing=column(closing),
        fades=fades,
    )


def forward_kernel(
    heads,
    groups,
    keep_ref,
    query_ref,
    key_ref,
    value_ref,
    query_before,
    key_before,
    value_before,
    query_rim,
    key_rim,
    value_rim,
    conv_query,
    conv_key,
    conv_value,
    scal_ref,
    rate_ref,
    query_out,
    key_out,
    value_out,
    wu_out,
    inverse_out,
    state_out,
    linear_out,
    local_out,
    device_out,
    state,
    ext_query,
    ext_key,
    ext_value,
):
    group = pl.program_id(0)
    first = group == 0

    @pl.when(first)
    def _():
        row = lax.broadcasted_iota(jnp.int32, (DK, WIDE), 0)
        lane = lax.broadcasted_iota(jnp.int32, (DK, WIDE), 1)
        unit = jnp.where(row == lane, 1.0, 0.0)
        for h in range(heads):
            state[pl.ds(h * DK, DK), :] = unit

    keep = keep_ref[group]
    fill(ext_query, query_ref, query_before, query_rim, first, keep)
    fill(ext_key, key_ref, key_before, key_rim, first, keep)
    fill(ext_value, value_ref, value_before, value_rim, first, keep)
    terms = token_terms(scal_ref, rate_ref, heads)
    valid = terms["valid"]
    queries, keys, values = ([], [], [])
    for h in range(heads):
        act = jax.nn.silu(tap_sum(ext_query, conv_query, h * DK, DK))
        scale = lax.rsqrt(jnp.sum(act * act, axis=1, keepdims=True) + epsilon_norm)
        queries.append((act * scale * DK ** (-0.5)).astype(bf16))
        act = jax.nn.silu(tap_sum(ext_key, conv_key, h * DK, DK))
        scale = lax.rsqrt(jnp.sum(act * act, axis=1, keepdims=True) + epsilon_norm)
        keys.append((act * scale * valid).astype(bf16))
        act = jax.nn.silu(tap_sum(ext_value, conv_value, h * DV, DV))
        values.append((act * valid).astype(bf16))
    query_out[...] = jnp.concatenate(queries, axis=1)
    key_out[...] = jnp.concatenate(keys, axis=1)
    value_out[...] = jnp.concatenate(values, axis=1)
    query = jnp.concatenate(queries, axis=0)
    key = jnp.concatenate(keys, axis=0)
    value = jnp.concatenate(values, axis=0)
    scores = contract(jnp.concatenate([query, key], axis=0), key, 1, 1)
    mix = packed(scores[: heads * GROUP], heads)
    similar = packed(scores[heads * GROUP :], heads)
    ratio, betas, strict = (terms["ratio"], terms["betas"], terms["strict"])
    mixing = diagonal(ratio * mix, heads)
    inverse = packed_inverse(jnp.where(strict, betas * ratio * similar, 0.0), heads).astype(bf16)
    inverse_out[...] = inverse
    beta, growth, closing = (terms["beta_column"], terms["growth"], terms["closing"])
    key_wide = key.astype(f32)
    right = jnp.concatenate([beta * growth * key_wide, beta * value.astype(f32)], axis=1)
    wu = contract(diagonal(inverse, heads), right.astype(bf16))
    wu_low = wu.astype(bf16)
    wu_out[0] = wu_low
    grown = (growth * query.astype(f32)).astype(bf16)
    fading = (closing * key_wide).astype(bf16)
    lane = lax.broadcasted_iota(jnp.int32, (1, WIDE), 1)
    fresh, seen = ([], [])
    for h in range(heads):
        rows = slice(h * GROUP, (h + 1) * GROUP)
        used = state[pl.ds(h * DK, DK), :] * keep
        used_low = used.astype(bf16)
        state_out[0, pl.ds(h * DK, DK), :] = used_low
        part = jnp.where(lane >= DK, wu[rows], 0.0) - contract(wu_low[rows, :DK], used_low)
        part = part.astype(bf16)
        after = terms["fades"][h] * used + contract(fading[rows], part, 0, 0)
        state[pl.ds(h * DK, DK), :] = after
        fresh.append(part)
        seen.append(contract(grown[rows], used_low))
    both = jnp.concatenate(seen, axis=0) + contract(mixing, jnp.concatenate(fresh, axis=0))
    for h in range(heads):
        rows = slice(h * GROUP, (h + 1) * GROUP)
        linear_out[:, pl.ds(h * DK, DK)] = (both[rows, :DK] * valid).astype(bf16)
        local_out[:, pl.ds(h * DV, DV)] = both[rows, DK:] * valid

    @pl.when(group == groups - 1)
    def _():
        device_out[...] = state[...]


def token_block(width, back=None):
    if back is None:
        return pl.BlockSpec((GROUP, width), lambda g: (g, 0))
    return pl.BlockSpec((GROUP, width), lambda g: (back - 1 - g, 0))


def before_block(width, back=None):
    ratio = GROUP // HALO
    if back is None:
        return pl.BlockSpec((HALO, width), lambda g: (jnp.maximum(g * ratio - 1, 0), 0))
    return pl.BlockSpec((HALO, width), lambda g: (jnp.maximum((back - 1 - g) * ratio - 1, 0), 0))


def whole(shape):
    return pl.BlockSpec(shape, lambda g: (0,) * len(shape))


def delta_forward(pres, rims, convs, scal, rate, keep):
    tokens = scal.shape[0]
    heads, groups = (rate.shape[1], tokens // GROUP)
    widths = [pre.shape[1] for pre in pres]
    smem = pl.BlockSpec(memory_space=pltpu.SMEM)
    return pl.pallas_call(
        functools.partial(forward_kernel, heads, groups),
        grid=(groups,),
        in_specs=[smem]
        + [token_block(w) for w in widths]
        + [before_block(w) for w in widths]
        + [whole((HALO, w)) for w in widths]
        + [whole((CONV, w)) for w in widths]
        + [token_block(scal.shape[1]), whole(rate.shape)],
        out_specs=[token_block(w) for w in widths]
        + [
            pl.BlockSpec((1, heads * GROUP, WIDE), lambda g: (g, 0, 0)),
            token_block(heads * GROUP),
            pl.BlockSpec((1, heads * DK, WIDE), lambda g: (g, 0, 0)),
            token_block(heads * DK),
            token_block(heads * DV),
            whole((heads * DK, WIDE)),
        ],
        out_shape=[jax.ShapeDtypeStruct((tokens, w), bf16) for w in widths]
        + [
            jax.ShapeDtypeStruct((groups, heads * GROUP, WIDE), bf16),
            jax.ShapeDtypeStruct((tokens, heads * GROUP), bf16),
            jax.ShapeDtypeStruct((groups, heads * DK, WIDE), bf16),
            jax.ShapeDtypeStruct((tokens, heads * DK), bf16),
            jax.ShapeDtypeStruct((tokens, heads * DV), f32),
            jax.ShapeDtypeStruct((heads * DK, WIDE), f32),
        ],
        scratch_shapes=[pltpu.VMEM((heads * DK, WIDE), f32)]
        + [pltpu.VMEM((HALO + GROUP, w), f32) for w in widths],
        compiler_params=pltpu.CompilerParams(vmem_limit_bytes=VMEM),
        cost_estimate=pl.CostEstimate(flops=10**6, bytes_accessed=10**4, transcendentals=0),
        name="delta_forward",
    )(keep, *pres, *pres, *rims, *convs, scal, rate)


def backward_kernel(
    heads,
    groups,
    devices,
    keep_ref,
    query_pre,
    key_pre,
    value_pre,
    query_before,
    key_before,
    value_before,
    query_rim,
    key_rim,
    value_rim,
    conv_query,
    conv_key,
    conv_value,
    scal_ref,
    rate_ref,
    query_ref,
    key_ref,
    value_ref,
    wu_ref,
    inverse_ref,
    state_ref,
    entry_ref,
    exit_ref,
    grad_ref,
    query_out,
    key_out,
    value_out,
    query_conv_out,
    key_conv_out,
    value_conv_out,
    scal_out,
    rate_out,
    tail_out,
    own_back_out,
    other_back_out,
    got_tail_out,
    got_out,
    carry,
    ext_query,
    ext_key,
    ext_value,
    dy_query,
    dy_key,
    dy_value,
    sending,
    send_sem,
    recv_sem,
    back_send,
    tail_got,
    own_got,
    other_got,
    rim_send_sem,
    rim_recv_sem,
):
    step = pl.program_id(0)
    group = groups - 1 - step
    keep = keep_ref[group]
    seq, head = (lax.axis_index("seq"), lax.axis_index("head"))
    partner = seq + 1 - 2 * (seq % 2)

    def transfer(at, block):
        return pltpu.make_async_remote_copy(
            src_ref=sending.at[at % 2],
            dst_ref=got_out.at[pl.ds(block * GROUP, GROUP), :],
            send_sem=send_sem.at[at % 2],
            recv_sem=recv_sem.at[block],
            device_id=(partner, head),
            device_id_type=pl.DeviceIdType.MESH,
        )

    def rim_transfer(kind, source, target, to):
        return pltpu.make_async_remote_copy(
            src_ref=source,
            dst_ref=target,
            send_sem=rim_send_sem.at[kind],
            recv_sem=rim_recv_sem.at[kind],
            device_id=(to, head),
            device_id_type=pl.DeviceIdType.MESH,
        )

    tail_transfer = rim_transfer(0, tail_out, tail_got, partner)
    own_transfer = rim_transfer(1, back_send, own_got, seq - 1)
    other_transfer = rim_transfer(2, back_send, other_got, seq - 2)
    even = seq % 2 == 0

    @pl.when(step == 0)
    def _():
        barrier = pltpu.get_barrier_semaphore()
        mesh = pl.DeviceIdType.MESH
        pl.semaphore_signal(barrier, inc=1, device_id=(partner, head), device_id_type=mesh)

        @pl.when(even & (seq + 2 < devices))
        def _():
            pl.semaphore_signal(barrier, inc=1, device_id=(seq + 2, head), device_id_type=mesh)

        @pl.when((seq % 2 == 1) & (seq + 1 < devices))
        def _():
            pl.semaphore_signal(barrier, inc=1, device_id=(seq + 1, head), device_id_type=mesh)

        @pl.when(even & (seq >= 2))
        def _():
            pl.semaphore_wait(barrier, 3)

        @pl.when((seq % 2 == 1) | (seq < 2))
        def _():
            pl.semaphore_wait(barrier, 1)

    @pl.when(step >= 2)
    def _():
        transfer(step, group + 2).wait_send()

    @pl.when(step == 0)
    def _():
        carry[...] = exit_ref[...]
        for ref in (dy_query, dy_key, dy_value):
            ref[...] = jnp.zeros_like(ref)
        for ref in (query_conv_out, key_conv_out, value_conv_out, rate_out):
            ref[...] = jnp.zeros_like(ref)

    terms = token_terms(scal_ref, rate_ref, heads)
    valid = terms["valid"]
    beta, growth, closing = (terms["beta_column"], terms["growth"], terms["closing"])
    query = stacked(query_ref[...], heads)
    key = stacked(key_ref[...], heads)
    value = stacked(value_ref[...], heads)
    grad = stacked(grad_ref[...], heads)
    query_wide, key_wide = (query.astype(f32), key.astype(f32))
    scores = contract(jnp.concatenate([query, key], axis=0), key, 1, 1)
    mix = packed(scores[: heads * GROUP], heads)
    similar = packed(scores[heads * GROUP :], heads)
    ratio, betas, strict = (terms["ratio"], terms["betas"], terms["strict"])
    mixing = ratio * mix
    wu = wu_ref[0]
    grown_wide = growth * query_wide
    fading_wide = closing * key_wide
    grown = grown_wide.astype(bf16)
    fading = fading_wide.astype(bf16)
    mixed_back = contract(diagonal(mixing, heads), grad, 0, 0)
    fresh, d_fresh, d_grown, d_fading, d_weights, d_fades = ([], [], [], [], [], [])
    for h in range(heads):
        rows = slice(h * GROUP, (h + 1) * GROUP)
        states = pl.ds(h * DK, DK)
        pair = state_ref[0, states, :]
        used = pair[:, DK:].astype(f32) + contract(pair[:, :DK], entry_ref[states, :])
        used_low = used.astype(bf16)
        weights = wu[rows, :DK]
        part = (wu[rows, DK:].astype(f32) - contract(weights, used_low)).astype(bf16)
        after = carry[states, :]
        after_low = after.astype(bf16)
        d_part = mixed_back[rows] + contract(fading[rows], after_low)
        d_part_low = d_part.astype(bf16)
        stack = jnp.concatenate([grad[rows], d_part_low], axis=0)
        seen = contract(stack, used_low, 1, 1)
        d_grown.append(seen[:GROUP])
        d_weights.append(-seen[GROUP:])
        d_fading.append(contract(part, after_low, 1, 1))
        fade = terms["fades"][h]
        carry[states, :] = keep * (
            fade * after
            + contract(jnp.concatenate([grown[rows], -weights], axis=0), stack, 0, 0)
        )
        d_fade = jnp.sum(after * used, axis=0, keepdims=True)
        d_fades.append(fade * jnp.sum(d_fade, axis=1, keepdims=True))
        fresh.append(part)
        d_fresh.append(d_part_low)
    d_grown = jnp.concatenate(d_grown, axis=0)
    d_fading = jnp.concatenate(d_fading, axis=0)
    d_weights = jnp.concatenate(d_weights, axis=0).astype(bf16)
    d_fresh = jnp.concatenate(d_fresh, axis=0)
    d_mixing = packed(contract(grad, jnp.concatenate(fresh, axis=0), 1, 1), heads)
    d_right = contract(
        diagonal(inverse_ref[...], heads), jnp.concatenate([d_weights, d_fresh], axis=1), 0, 0
    )
    d_coupling = -packed(contract(d_right.astype(bf16), wu, 1, 1), heads)
    d_coupling = jnp.where(strict, d_coupling, 0.0)
    ratio_grad = ratio * d_coupling
    from_similar = diagonal(betas * ratio_grad, heads)
    from_mix = diagonal(ratio * d_mixing, heads)
    plain = contract(jnp.concatenate([from_mix, from_similar], axis=0), key)
    turned = contract(
        jnp.concatenate([from_similar, from_mix], axis=0),
        jnp.concatenate([key, query], axis=0),
        0,
        0,
    )
    count = heads * GROUP
    d_scaled = d_right[:, :DK]
    d_query = growth * d_grown + plain[:count]
    d_key = beta * growth * d_scaled + closing * d_fading + plain[count:] + turned
    d_value = beta * d_right[:, DK:]
    grown_key = growth * key_wide
    ratio_similar = ratio_grad * similar
    flows = betas * ratio_similar + mixing * d_mixing
    fading_flow = d_fading * fading_wide
    sum_growth = jnp.sum(
        d_grown * grown_wide + d_scaled * (beta * grown_key) - fading_flow, axis=1, keepdims=True
    )
    sum_fading = jnp.sum(fading_flow, axis=1, keepdims=True)
    value_flow = d_right[:, DK:] * value.astype(f32)
    sum_beta = jnp.sum(
        d_scaled * grown_key + value_flow[:, :DK] + value_flow[:, DK:], axis=1, keepdims=True
    )
    flow_high, flow_low = halves(flows)
    ones = jnp.full((GROUP, 128), 1.0, bf16)
    turned_flow = contract(
        jnp.concatenate([flow_high, flow_low], axis=0),
        jnp.concatenate([ones, ones], axis=0),
        0,
        0,
    )[:, :1]
    owner = lane_heads(heads)
    lane = lax.broadcasted_iota(jnp.int32, (GROUP, 128), 1)
    d_sums = jnp.zeros((GROUP, 128), f32)
    d_beta = jnp.zeros((GROUP, 128), f32)
    d_last = jnp.zeros((1, 128), f32)
    for h in range(heads):
        rows = slice(h * GROUP, (h + 1) * GROUP)
        flow = jnp.sum(jnp.where(owner == h, flows, 0.0), axis=1, keepdims=True)
        more = jnp.sum(jnp.where(owner == h, ratio_similar, 0.0), axis=1, keepdims=True)
        d_sums = jnp.where(lane == h, sum_growth[rows] + flow - turned_flow[rows], d_sums)
        d_beta = jnp.where(lane == h, sum_beta[rows] + more, d_beta)
        total = jnp.sum(sum_fading[rows], axis=0, keepdims=True) + d_fades[h]
        d_last = jnp.where(lane[:1] == h, total, d_last)
    square_row = lax.broadcasted_iota(jnp.int32, (GROUP, GROUP), 0)
    square_lane = lax.broadcasted_iota(jnp.int32, (GROUP, GROUP), 1)
    later = jnp.where(square_row <= square_lane, 1.0, 0.0)
    d_decay = (summed_rows(later, d_sums) + d_last)[:, :heads]
    d_beta = d_beta[:, :heads]
    d_alpha = -d_decay * terms["rate"] * jax.nn.sigmoid(terms["alpha"]) * valid
    d_beta = d_beta * terms["beta"] * (1.0 - terms["beta"])
    scal_out[...] = jnp.concatenate([d_alpha, d_beta], axis=1).astype(bf16)
    rate_out[0:1, :] += jnp.sum(d_decay * terms["decay"], axis=0, keepdims=True)
    rate_out[1:2, :] += jnp.sum(d_alpha, axis=0, keepdims=True)

    first = group == 0
    after_keep = jnp.where(step == 0, 0.0, keep_ref[jnp.minimum(group + 1, groups - 1)])
    sections = (
        (query_pre, query_before, query_rim, conv_query, ext_query, dy_query, DK, d_query),
        (key_pre, key_before, key_rim, conv_key, ext_key, dy_key, DK, d_key),
        (value_pre, value_before, value_rim, conv_value, ext_value, dy_value, DV, d_value),
    )
    outs = (
        (query_out, query_conv_out),
        (key_out, key_conv_out),
        (value_out, value_conv_out),
    )
    for kind, (section, out) in enumerate(zip(sections, outs)):
        now_ref, before_ref, rim_ref, conv_ref, ext_ref, dy_ref, width, cotangent = section
        pre_out, conv_out = out
        first_lane = kind * heads * DK
        fill(ext_ref, now_ref, before_ref, rim_ref, first, keep)
        dy_ref[8 + GROUP :, :] = dy_ref[8:16, :] * after_keep
        for h in range(heads):
            lanes = pl.ds(h * width, width)
            rows = slice(h * GROUP, (h + 1) * GROUP)
            total = tap_sum(ext_ref, conv_ref, h * width, width)
            sigmoid = jax.nn.sigmoid(total)
            act = total * sigmoid
            d_act = cotangent[rows]
            if kind > 0:
                d_act = d_act * valid
            if kind < 2:
                scale = lax.rsqrt(jnp.sum(act * act, axis=1, keepdims=True) + epsilon_norm)
                inner = jnp.sum(act * d_act, axis=1, keepdims=True)
                d_act = scale * (d_act - act * (scale * scale * inner))
            if kind == 0:
                d_act = d_act * DK ** (-0.5)
            d_total = d_act * (sigmoid * (1.0 + total * (1.0 - sigmoid)))
            dy_ref[pl.ds(8, GROUP), lanes] = d_total
            for tap in range(CONV):
                product = d_total * ext_ref[pl.ds(HALO - tap, GROUP), lanes]
                conv_out[pl.ds(tap * 8, 8), lanes] += jnp.sum(
                    product.reshape(GROUP // 8, 8, width), axis=0
                )
            d_pre = d_total * conv_ref[0:1, lanes]
            for tap in range(1, CONV):
                d_pre = d_pre + dy_ref[pl.ds(8 + tap, GROUP), lanes] * conv_ref[tap : tap + 1, lanes]
            pre_out[:, lanes] = d_pre.astype(bf16)
            sending[step % 2, :, pl.ds(first_lane + h * width, width)] = d_pre.astype(bf16)

            @pl.when(step == 0)
            def _():
                tail_out[:, pl.ds(first_lane + h * width, width)] = d_pre[GROUP - 8 :]

            @pl.when(first)
            def _():
                d_back = dy_ref[pl.ds(1, 8), lanes] * conv_ref[1:2, lanes]
                for tap in range(2, CONV):
                    d_back = d_back + dy_ref[pl.ds(tap, 8), lanes] * conv_ref[tap : tap + 1, lanes]
                back_send[:, pl.ds(first_lane + h * width, width)] = d_back * keep

    transfer(step, group).start()

    @pl.when(step == 0)
    def _():
        tail_transfer.start()

    @pl.when(step == groups - 1)
    def _():
        @pl.when(seq >= 1)
        def _():
            own_transfer.start()

        @pl.when(even & (seq >= 2))
        def _():
            other_transfer.start()

        tail_transfer.wait_send()
        tail_transfer.wait_recv()
        got_tail_out[...] = tail_got[...]

        @pl.when(seq >= 1)
        def _():
            own_transfer.wait_send()

        @pl.when(even & (seq >= 2))
        def _():
            other_transfer.wait_send()

        @pl.when(seq + 1 < devices)
        def _():
            own_transfer.wait_recv()
            own_back_out[...] = own_got[...]

        @pl.when(seq + 1 >= devices)
        def _():
            own_back_out[...] = jnp.zeros_like(own_back_out)

        @pl.when(even & (seq + 2 < devices))
        def _():
            other_transfer.wait_recv()
            other_back_out[...] = other_got[...]

        @pl.when(even & (seq + 2 >= devices))
        def _():
            other_back_out[...] = jnp.zeros_like(other_back_out)

        @pl.when(seq % 2 == 1)
        def _():
            other_back_out[...] = back_send[...]

        transfer(step - 1, group + 1).wait_send()
        transfer(step, group).wait_send()
        for block in range(groups):
            transfer(step, block).wait_recv()


def delta_backward(pres, rims, convs, scal, rate, keep, made, entry, exit_grad, grad):
    tokens = scal.shape[0]
    heads, groups = (rate.shape[1], tokens // GROUP)
    widths = [pre.shape[1] for pre in pres]
    smem = pl.BlockSpec(memory_space=pltpu.SMEM)
    turn = lambda *shape: pl.BlockSpec(shape, lambda g: (groups - 1 - g, 0, 0))
    columns = 2 * heads
    return pl.pallas_call(
        functools.partial(backward_kernel, heads, groups, lax.axis_size("seq")),
        grid=(groups,),
        in_specs=[smem]
        + [token_block(w, groups) for w in widths]
        + [before_block(w, groups) for w in widths]
        + [whole((HALO, w)) for w in widths]
        + [whole((CONV, w)) for w in widths]
        + [token_block(scal.shape[1], groups), whole(rate.shape)]
        + [token_block(w, groups) for w in widths]
        + [
            turn(1, heads * GROUP, WIDE),
            token_block(heads * GROUP, groups),
            turn(1, heads * DK, WIDE),
            whole((heads * DK, DV)),
            whole((heads * DK, DV)),
            token_block(heads * DV, groups),
        ],
        out_specs=[token_block(w, groups) for w in widths]
        + [whole((CONV * 8, w)) for w in widths]
        + [token_block(columns, groups), whole((8, heads))]
        + [pl.BlockSpec(memory_space=pltpu.VMEM)]
        + [whole((8, sum(widths)))] * 3
        + [pl.BlockSpec(memory_space=pl.ANY)],
        out_shape=[jax.ShapeDtypeStruct((tokens, w), bf16) for w in widths]
        + [jax.ShapeDtypeStruct((CONV * 8, w), f32) for w in widths]
        + [
            jax.ShapeDtypeStruct((tokens, columns), bf16),
            jax.ShapeDtypeStruct((8, heads), f32),
            *[jax.ShapeDtypeStruct((8, sum(widths)), f32)] * 4,
            jax.ShapeDtypeStruct((tokens, sum(widths)), bf16),
        ],
        scratch_shapes=[pltpu.VMEM((heads * DK, DV), f32)]
        + [pltpu.VMEM((HALO + GROUP, w), f32) for w in widths]
        + [pltpu.VMEM((16 + GROUP, w), f32) for w in widths]
        + [
            pltpu.VMEM((2, GROUP, sum(widths)), bf16),
            pltpu.SemaphoreType.DMA((2,)),
            pltpu.SemaphoreType.DMA((groups,)),
            *[pltpu.VMEM((8, sum(widths)), f32)] * 4,
            pltpu.SemaphoreType.DMA((3,)),
            pltpu.SemaphoreType.DMA((3,)),
        ],
        compiler_params=pltpu.CompilerParams(
            vmem_limit_bytes=VMEM, collective_id=1, has_side_effects=True
        ),
        cost_estimate=pl.CostEstimate(flops=10**6, bytes_accessed=10**4, transcendentals=0),
        name="delta_backward",
    )(keep, *pres, *pres, *rims, *convs, scal, rate, *made, entry, exit_grad, grad)


def gated_forward_kernel(heads, linear_ref, local_ref, gate_ref, entry_ref, gain_ref, gated_out):
    for h in range(heads):
        wide = pl.ds(h * DV, DV)
        out = local_ref[:, wide] + contract(
            linear_ref[:, pl.ds(h * DK, DK)], entry_ref[pl.ds(h * DK, DK), :]
        )
        scale = lax.rsqrt(jnp.mean(out * out, axis=1, keepdims=True) + epsilon_gate)
        gate = gate_ref[:, wide]
        gated_out[:, wide] = (out * scale * gain_ref[...] * jax.nn.silu(gate)).astype(bf16)


def row_block(rows, width):
    return pl.BlockSpec((rows, width), lambda g: (g, 0))


def gated_forward(linear, local, gate, entry, gain):
    tokens, heads = (local.shape[0], local.shape[1] // DV)
    rows = 2 * GROUP
    return pl.pallas_call(
        functools.partial(gated_forward_kernel, heads),
        grid=(tokens // rows,),
        in_specs=[
            row_block(rows, heads * DK),
            row_block(rows, heads * DV),
            row_block(rows, heads * DV),
            whole((heads * DK, DV)),
            whole((1, DV)),
        ],
        out_specs=row_block(rows, heads * DV),
        out_shape=jax.ShapeDtypeStruct((tokens, heads * DV), bf16),
        compiler_params=pltpu.CompilerParams(vmem_limit_bytes=SMALL),
        cost_estimate=pl.CostEstimate(flops=10**9, bytes_accessed=10**7, transcendentals=0),
        name="gated_forward",
    )(linear, local, gate, entry, gain[None, :])


def gated_backward_kernel(
    heads,
    linear_ref,
    local_ref,
    gate_ref,
    entry_ref,
    gain_ref,
    grad_ref,
    valid_ref,
    delta_out,
    gate_out,
    gain_out,
    entry_out,
):
    @pl.when(pl.program_id(0) == 0)
    def _():
        gain_out[...] = jnp.zeros_like(gain_out)
        entry_out[...] = jnp.zeros_like(entry_out)

    rows = local_ref.shape[0]
    for h in range(heads):
        wide = pl.ds(h * DV, DV)
        linear = linear_ref[:, pl.ds(h * DK, DK)]
        out = local_ref[:, wide] + contract(linear, entry_ref[pl.ds(h * DK, DK), :])
        scale = lax.rsqrt(jnp.mean(out * out, axis=1, keepdims=True) + epsilon_gate)
        unit = out * scale
        gate = gate_ref[:, wide]
        sigmoid = jax.nn.sigmoid(gate)
        grad = grad_ref[:, wide]
        silu = gate * sigmoid
        product = grad * unit
        gain_out[...] += jnp.sum((product * silu).reshape(rows // 8, 8, DV), axis=0)
        gate_out[:, wide] = (
            product * gain_ref[...] * (sigmoid * (1.0 + gate * (1.0 - sigmoid)))
        ).astype(bf16)
        d_unit = grad * gain_ref[...] * silu
        inner = jnp.mean(d_unit * unit, axis=1, keepdims=True)
        delta = (scale * (d_unit - unit * inner) * valid_ref[...]).astype(bf16)
        delta_out[:, wide] = delta
        entry_out[pl.ds(h * DK, DK), :] += contract(linear, delta, 0, 0)


def gated_backward(linear, local, gate, entry, gain, grad, valid):
    tokens, heads = (local.shape[0], local.shape[1] // DV)
    rows = 2 * GROUP
    return pl.pallas_call(
        functools.partial(gated_backward_kernel, heads),
        grid=(tokens // rows,),
        in_specs=[
            row_block(rows, heads * DK),
            row_block(rows, heads * DV),
            row_block(rows, heads * DV),
            whole((heads * DK, DV)),
            whole((1, DV)),
            row_block(rows, heads * DV),
            row_block(rows, 1),
        ],
        out_specs=[
            row_block(rows, heads * DV),
            row_block(rows, heads * DV),
            whole((8, DV)),
            whole((heads * DK, DV)),
        ],
        out_shape=[
            jax.ShapeDtypeStruct((tokens, heads * DV), bf16),
            jax.ShapeDtypeStruct((tokens, heads * DV), bf16),
            jax.ShapeDtypeStruct((8, DV), f32),
            jax.ShapeDtypeStruct((heads * DK, DV), f32),
        ],
        compiler_params=pltpu.CompilerParams(vmem_limit_bytes=SMALL),
        cost_estimate=pl.CostEstimate(flops=10**6, bytes_accessed=10**4, transcendentals=0),
        name="gated_backward",
    )(linear, local, gate, entry, gain[None, :], grad, valid[:, None])


def column_place(tile, tiles, place):
    block, inner = (tile // (tiles // 4), tile % (tiles // 4))
    core = jnp.where(block < 2, 1 - place % 2, place % 2)
    chip = jnp.where(block % 2 == 0, 1 - place // 2, place // 2)
    return (chip * 2 + core) * (tiles // 4) + inner


def plain_dense_kernel(place_ref, left_ref, right_ref, out_ref):
    left = left_ref[:, : right_ref.shape[0]]
    out_ref[...] = contract(left, right_ref[...]).astype(bf16)


def plain_dense(left, right, place, tile=256):
    rows, cols = (left.shape[0], right.shape[1])
    tiles = cols // tile
    return pl.pallas_call(
        plain_dense_kernel,
        grid_spec=pltpu.PrefetchScalarGridSpec(
            num_scalar_prefetch=1,
            grid=(tiles,),
            in_specs=[
                pl.BlockSpec(left.shape, lambda i, place: (0, 0)),
                pl.BlockSpec(
                    (right.shape[0], tile), lambda i, place: (0, column_place(i, tiles, place[0]))
                ),
            ],
            out_specs=pl.BlockSpec((rows, tile), lambda i, place: (0, i)),
        ),
        out_shape=jax.ShapeDtypeStruct((rows, cols), bf16),
        compiler_params=pltpu.CompilerParams(vmem_limit_bytes=SMALL),
        cost_estimate=pl.CostEstimate(
            flops=2 * rows * cols * left.shape[1], bytes_accessed=10**7, transcendentals=0
        ),
        name="plain_dense",
    )(place, left, right)


def norm_dense_kernel(sides, place_ref, *refs):
    count = len(sides)
    lefts, rights = (refs[:count], refs[count : 2 * count])
    rows_ref, scale_ref, gain_ref, out_ref, gain_out, dots_out = refs[2 * count :]
    total = 0.0
    for left, right, side in zip(lefts, rights, sides):
        total = total + contract(left[:, : right.shape[side]], right[...], 1, side)
    out_ref[...] = total.astype(bf16)
    weighted = total * (rows_ref[...].astype(f32) * scale_ref[...])
    gain_out[...] = jnp.sum(weighted, axis=0, keepdims=True)
    dots = jnp.sum(weighted * gain_ref[...], axis=1, keepdims=True)

    @pl.when(pl.program_id(0) == 0)
    def _():
        dots_out[...] = dots

    @pl.when(pl.program_id(0) > 0)
    def _():
        dots_out[...] += dots


def norm_dense(pairs, rows, scale, gain, place, tile=256):
    tokens, cols = rows.shape
    tiles = cols // tile
    lefts, rights = ([left for left, _ in pairs], [right for _, right in pairs])
    placed = lambda i, place: (0, column_place(i, tiles, place[0]))
    upright = lambda i, place: (column_place(i, tiles, place[0]), 0)
    sides = [1 if right.shape[0] == cols else 0 for right in rights]
    return pl.pallas_call(
        functools.partial(norm_dense_kernel, sides),
        grid_spec=pltpu.PrefetchScalarGridSpec(
            num_scalar_prefetch=1,
            grid=(tiles,),
            in_specs=[pl.BlockSpec(left.shape, lambda i, place: (0, 0)) for left in lefts]
            + [
                pl.BlockSpec((tile, right.shape[1]), upright)
                if side
                else pl.BlockSpec((right.shape[0], tile), placed)
                for right, side in zip(rights, sides)
            ]
            + [
                pl.BlockSpec((tokens, tile), placed),
                pl.BlockSpec((tokens, 1), lambda i, place: (0, 0)),
                pl.BlockSpec((1, tile), placed),
            ],
            out_specs=[
                pl.BlockSpec((tokens, tile), lambda i, place: (0, i)),
                pl.BlockSpec((1, tile), placed),
                pl.BlockSpec((tokens, 1), lambda i, place: (0, 0)),
            ],
        ),
        out_shape=[
            jax.ShapeDtypeStruct((tokens, cols), bf16),
            jax.ShapeDtypeStruct((1, cols), f32),
            jax.ShapeDtypeStruct((tokens, 1), f32),
        ],
        compiler_params=pltpu.CompilerParams(vmem_limit_bytes=VMEM),
        cost_estimate=pl.CostEstimate(
            flops=2 * tokens * cols * sum(left.shape[1] for left in lefts),
            bytes_accessed=2 * 10**7,
            transcendentals=0,
        ),
        name="norm_dense",
    )(place, *lefts, *rights, rows, scale, gain[None, :])


def shifted(block, axis, distance):
    devices = range(lax.axis_size(axis))
    route = [(i - distance, i) for i in devices if i - distance in devices]
    return lax.ppermute(block, axis, route)


def exchanged(block, axis, bit):
    route = [(i, i ^ bit) for i in range(lax.axis_size(axis))]
    return lax.ppermute(block, axis, route)


def half(block, axis, at, count):
    width = block.shape[axis] // count
    return lax.dynamic_slice_in_dim(block, at * width, width, axis)


def weight_grad_kernel(turned, place_ref, rows_ref, got_rows_ref, cols_ref, got_cols_ref, out_ref):
    if turned:
        total = contract(cols_ref[...], rows_ref[...], 0, 0)
        total = total + contract(got_cols_ref[...], got_rows_ref[...], 0, 0)
        total = total[: out_ref.shape[0]]
    else:
        total = contract(rows_ref[...], cols_ref[...], 0, 0)
        total = total + contract(got_rows_ref[...], got_cols_ref[...], 0, 0)
    out_ref[...] = total.astype(bf16)


def pair_grad(rows, got_rows, cols, got_cols, turned, kept=None, spot=0):
    odd = lax.axis_index("seq").astype(jnp.int32) % 2
    devices = lax.axis_size("seq")
    tokens, padded = cols.shape
    count = padded if kept is None else kept
    width = rows.shape[1] // devices
    if width % 128:
        part = jnp.concatenate([own_half(rows, odd, width), got_rows], axis=0)
        got_cols = lax.slice_in_dim(got_cols, spot * padded, (spot + 1) * padded, axis=1)
        cols = jnp.concatenate([cols, got_cols], axis=0)[:, :count]
        if turned:
            part = part.reshape(2 * tokens, devices // 2, width)
            total = jnp.einsum("tn,tcw->cnw", cols, part, preferred_element_type=f32)
            return total.reshape(devices // 2 * count, width).astype(bf16)
        return dense(part.T, cols).astype(bf16)
    block = (count, width) if turned else (width, count)
    still = pl.BlockSpec((tokens, padded), lambda i, place: (0, 0))
    return pl.pallas_call(
        functools.partial(weight_grad_kernel, turned),
        grid_spec=pltpu.PrefetchScalarGridSpec(
            num_scalar_prefetch=1,
            grid=(devices // 2,),
            in_specs=[
                pl.BlockSpec((tokens, width), lambda i, place: (0, 2 * i + place[0])),
                pl.BlockSpec((tokens, width), lambda i, place: (0, i)),
                still,
                pl.BlockSpec((tokens, padded), lambda i, place: (0, spot)),
            ],
            out_specs=pl.BlockSpec(block, lambda i, place: (i, 0)),
        ),
        out_shape=jax.ShapeDtypeStruct((devices // 2 * block[0], block[1]), bf16),
        compiler_params=pltpu.CompilerParams(vmem_limit_bytes=SMALL),
        cost_estimate=pl.CostEstimate(flops=10**6, bytes_accessed=10**4, transcendentals=0),
        name="weight_grad",
    )(odd[None], rows, got_rows, cols, got_cols)


def triple_grad_kernel(
    place_ref, rows_ref, got_rows_ref, first_ref, second_ref, third_ref, got_ref, out_ref
):
    rows, got_rows = (rows_ref[...], got_rows_ref[...])
    start = 0
    for ref in (first_ref, second_ref, third_ref):
        spot = pl.ds(start, ref.shape[1])
        total = contract(rows, ref[...], 0, 0) + contract(got_rows, got_ref[:, spot], 0, 0)
        out_ref[:, spot] = total.astype(bf16)
        start += ref.shape[1]


def triple_grad(rows, got_rows, parts, got_all):
    odd = lax.axis_index("seq").astype(jnp.int32) % 2
    devices = lax.axis_size("seq")
    tokens, total = got_all.shape
    width = rows.shape[1] // devices
    if width % 128:
        part = jnp.concatenate([own_half(rows, odd, width), got_rows], axis=0)
        cols = jnp.concatenate([jnp.concatenate(parts, axis=1), got_all], axis=0)
        return dense(part.T, cols).astype(bf16)
    still = lambda cols: pl.BlockSpec((tokens, cols), lambda i, place: (0, 0))
    return pl.pallas_call(
        triple_grad_kernel,
        grid_spec=pltpu.PrefetchScalarGridSpec(
            num_scalar_prefetch=1,
            grid=(devices // 2,),
            in_specs=[
                pl.BlockSpec((tokens, width), lambda i, place: (0, 2 * i + place[0])),
                pl.BlockSpec((tokens, width), lambda i, place: (0, i)),
                *[still(part.shape[1]) for part in parts],
                still(total),
            ],
            out_specs=pl.BlockSpec((width, total), lambda i, place: (i, 0)),
        ),
        out_shape=jax.ShapeDtypeStruct((devices // 2 * width, total), bf16),
        compiler_params=pltpu.CompilerParams(vmem_limit_bytes=SMALL),
        cost_estimate=pl.CostEstimate(flops=10**6, bytes_accessed=10**4, transcendentals=0),
        name="triple_grad",
    )(odd[None], rows, got_rows, *parts, got_all)


def line_kernel(
    planes,
    kept_ref,
    across_ref,
    out_ref,
    across_out,
    up_send,
    up_got,
    down_send,
    down_got,
    send_sem,
    recv_sem,
    across_sem,
):
    seq, head = (lax.axis_index("seq"), lax.axis_index("head"))
    plane = seq // 2
    mesh = pl.DeviceIdType.MESH
    lower, upper = (plane > 0, plane < planes - 1)
    beside = head + 2 - 4 * (head // 2)
    barrier = pltpu.get_barrier_semaphore()
    pl.semaphore_signal(barrier, inc=1, device_id=(seq, beside), device_id_type=mesh)

    @pl.when(lower)
    def _():
        pl.semaphore_signal(barrier, inc=1, device_id=(seq - 2, head), device_id_type=mesh)

    @pl.when(upper)
    def _():
        pl.semaphore_signal(barrier, inc=1, device_id=(seq + 2, head), device_id_type=mesh)

    @pl.when(lower & upper)
    def _():
        pl.semaphore_wait(barrier, 3)

    @pl.when((plane == 0) | (plane == planes - 1))
    def _():
        pl.semaphore_wait(barrier, 2)

    crossing = pltpu.make_async_remote_copy(
        src_ref=across_ref,
        dst_ref=across_out,
        send_sem=across_sem.at[0],
        recv_sem=across_sem.at[1],
        device_id=(seq, beside),
        device_id_type=mesh,
    )
    crossing.start()
    ways = ((up_send, up_got, 2, 0), (down_send, down_got, -2, 1))

    def transfer(way, step, source=None):
        send, got, hop, side = ways[way]
        return pltpu.make_async_remote_copy(
            src_ref=send.at[step - 1] if source is None else source,
            dst_ref=got.at[step - 1],
            send_sem=send_sem.at[side, step - 1],
            recv_sem=recv_sem.at[side, step - 1],
            device_id=(seq + hop, head),
            device_id_type=mesh,
        )

    rows = out_ref.shape[0]
    slab = 2 * HALO

    def each(body):
        def run(i, carry):
            body(pl.ds(pl.multiple_of(i * slab, slab), slab))
            return carry

        lax.fori_loop(0, rows // slab, run, 0)

    for step in range(1, planes):
        for way in range(2):
            send, got, hop, side = ways[way]
            rank = plane if way == 0 else planes - 1 - plane
            at = plane + planes - step if way == 0 else plane - planes + step

            @pl.when((rank < step) & (rank == 0))
            def _(at=at, way=way, step=step):
                transfer(way, step, kept_ref.at[at]).start()

            if step > 1:

                @pl.when((rank < step) & (rank > 0) & (rank < planes - 1))
                def _(send=send, got=got, at=at, way=way, step=step):
                    transfer(way, step - 1).wait_recv()

                    def body(span):
                        total = kept_ref[at, span, :].astype(f32)
                        total = total + got[step - 2, span, :].astype(f32)
                        send[step - 1, span, :] = total.astype(bf16)

                    each(body)
                    transfer(way, step).start()

    def own(span):
        out_ref[span, :] = kept_ref[plane, span, :].astype(f32)

    each(own)
    for way in range(2):
        got = ways[way][1]

        @pl.when(lower if way == 0 else upper)
        def _(got=got, way=way):
            transfer(way, planes - 1).wait_recv()

            def body(span):
                out_ref[span, :] += got[planes - 2, span, :].astype(f32)

            each(body)

    for step in range(1, planes):
        for way in range(2):
            rank = plane if way == 0 else planes - 1 - plane

            @pl.when((rank < step) & (rank < planes - 1))
            def _(way=way, step=step):
                transfer(way, step).wait_send()

    crossing.wait()


def line_summed(kept, across):
    planes = lax.axis_size("seq") // 2
    rows, cols = (kept.shape[0] // planes, kept.shape[1])
    if planes > 4 or rows % (2 * HALO):
        return seq_scattered(kept), exchanged(across, "head", 2)
    slots = pltpu.VMEM((planes - 1, rows, cols), bf16)
    return pl.pallas_call(
        functools.partial(line_kernel, planes),
        in_specs=[pl.BlockSpec(memory_space=pltpu.VMEM)] * 2,
        out_specs=[pl.BlockSpec(memory_space=pltpu.VMEM)] * 2,
        out_shape=[
            jax.ShapeDtypeStruct((rows, cols), f32),
            jax.ShapeDtypeStruct(across.shape, bf16),
        ],
        scratch_shapes=[slots] * 4
        + [pltpu.SemaphoreType.DMA((2, planes - 1))] * 2
        + [pltpu.SemaphoreType.DMA((2,))],
        compiler_params=pltpu.CompilerParams(
            vmem_limit_bytes=VMEM, collective_id=2, has_side_effects=True
        ),
        cost_estimate=pl.CostEstimate(flops=9 * 10**10, bytes_accessed=10**7, transcendentals=0),
        name="line_sum",
    )(kept.reshape(planes, rows, cols), across)


def partner_rows(block):
    width = block.shape[1] * 4 // lax.axis_size("seq")
    odd = lax.axis_index("seq") % 2
    if block.shape[1] == 2 * width:
        part = half(block, 1, 1 - odd, 2)
    else:
        part = own_half(block, 1 - odd, width)
    return exchanged(part, "seq", 1)


def gather_kernel(norm, place_ref, *refs):
    blocks = [ref[...] for ref in refs[:4]]
    width = blocks[0].shape[1]
    place = place_ref[0]
    out_ref = refs[5] if norm else refs[4]
    spots = [pl.ds(pl.multiple_of((place ^ at) * width, 128), width) for at in range(4)]
    for block, spot in zip(blocks, spots):
        out_ref[:, spot] = block
    if norm:
        gain_ref, normed_out, scale_out = (refs[4], refs[6], refs[7])
        wides = [block.astype(f32) for block in blocks]
        total = sum(jnp.sum(wide * wide, axis=1, keepdims=True) for wide in wides)
        scale = lax.rsqrt(total / (4 * width) + epsilon_norm)
        scale_out[...] = scale
        for wide, spot in zip(wides, spots):
            normed_out[:, spot] = (wide * scale * gain_ref[:, spot]).astype(bf16)


def head_gathered(block, gain=None):
    place = lax.axis_index("head").astype(jnp.int32)
    tokens, width = block.shape
    across = exchanged(block, "head", 2)
    beside = exchanged(block, "head", 1)
    corner = exchanged(across, "head", 1)
    rows = 4 * GROUP
    norm = gain is not None
    spec = lambda cols: pl.BlockSpec((rows, cols), lambda i, place: (i, 0))
    whole_shape = jax.ShapeDtypeStruct((tokens, 4 * width), bf16)
    out_specs, out_shape = (spec(4 * width), whole_shape)
    if norm:
        out_specs = [out_specs, spec(4 * width), spec(1)]
        out_shape = [whole_shape, whole_shape, jax.ShapeDtypeStruct((tokens, 1), f32)]
    gain_spec = pl.BlockSpec((1, 4 * width), lambda i, place: (0, 0))
    return pl.pallas_call(
        functools.partial(gather_kernel, norm),
        grid_spec=pltpu.PrefetchScalarGridSpec(
            num_scalar_prefetch=1,
            grid=(tokens // rows,),
            in_specs=[spec(width)] * 4 + ([gain_spec] if norm else []),
            out_specs=out_specs,
        ),
        out_shape=out_shape,
        compiler_params=pltpu.CompilerParams(vmem_limit_bytes=SMALL),
        cost_estimate=pl.CostEstimate(flops=10**6, bytes_accessed=6 * 10**6, transcendentals=0),
        name="gather",
    )(place[None], block, beside, across, corner, *([gain[None, :]] if norm else []))


def rows_dense_kernel(left_ref, right_ref, out_ref):
    out_ref[...] = contract(left_ref[...], right_ref[...], 1, 1)


def rows_dense(left, right):
    tokens, rows = (left.shape[0], 4 * GROUP)
    return pl.pallas_call(
        rows_dense_kernel,
        grid=(tokens // rows,),
        in_specs=[row_block(rows, left.shape[1]), whole(right.shape)],
        out_specs=row_block(rows, right.shape[0]),
        out_shape=jax.ShapeDtypeStruct((tokens, right.shape[0]), f32),
        compiler_params=pltpu.CompilerParams(vmem_limit_bytes=SMALL),
        cost_estimate=pl.CostEstimate(
            flops=2 * left.size * right.shape[0], bytes_accessed=10**7, transcendentals=0
        ),
        name="rows_dense",
    )(left, right)


def ffn_kernel(normed_ref, gate_ref, up_ref, grad_ref, inner_out, d_gate_out, d_up_out):
    normed = normed_ref[...]
    gate = contract(normed, gate_ref[...], 1, 1)
    up = contract(normed, up_ref[...], 1, 1)
    sigmoid = jax.nn.sigmoid(gate)
    silu = gate * sigmoid
    grad = grad_ref[...]
    padding = inner_out.shape[1] - gate.shape[1]
    for ref, values in (
        (inner_out, silu * up),
        (d_gate_out, grad * up * (sigmoid * (1.0 + gate * (1.0 - sigmoid)))),
        (d_up_out, grad * silu),
    ):
        values = values.astype(bf16)
        if padding:
            values = jnp.pad(values, ((0, 0), (0, padding)))
        ref[...] = values


def ffn(normed, w_gate, w_up, grad):
    tokens, count = grad.shape
    rows, padded = (4 * GROUP, -(-count // 128) * 128)
    return pl.pallas_call(
        ffn_kernel,
        grid=(tokens // rows,),
        in_specs=[row_block(rows, normed.shape[1])]
        + [whole(w_gate.shape)] * 2
        + [row_block(rows, count)],
        out_specs=[row_block(rows, padded)] * 3,
        out_shape=[jax.ShapeDtypeStruct((tokens, padded), bf16)] * 3,
        compiler_params=pltpu.CompilerParams(vmem_limit_bytes=VMEM),
        cost_estimate=pl.CostEstimate(
            flops=4 * normed.size * count, bytes_accessed=2 * 10**7, transcendentals=0
        ),
        name="ffn",
    )(normed, w_gate, w_up, grad)


def tied(*values):
    return lax.optimization_barrier(values)


def head_scattered(partial):
    width = partial.shape[1] // 2
    mine = partial[:, width:].astype(f32) + exchanged(partial[:, :width], "head", 1).astype(f32)
    width = width // 2
    return mine[:, width:] + exchanged(mine[:, :width].astype(bf16), "head", 2).astype(f32)


def head_summed(values):
    bit = 1
    while bit < lax.axis_size("head"):
        values = values + exchanged(values, "head", bit)
        bit = bit * 2
    return values


def own_half(rows, odd, width):
    tokens, total = rows.shape
    parts = rows.reshape(tokens, total // (2 * width), 2, width)
    return lax.dynamic_index_in_dim(parts, odd, 2, False).reshape(tokens, total // 2)


def seq_scattered(mine):
    devices = lax.axis_size("seq")
    groups = [list(range(first, devices, 2)) for first in range(2)]
    return lax.psum_scatter(
        mine.astype(bf16), "seq", scatter_dimension=0, axis_index_groups=groups, tiled=True
    ).astype(f32)


def composed(later, before):
    moved = jnp.einsum(
        "hij,hjk->hik", later[:, :, :DK].astype(bf16), before, preferred_element_type=f32
    )
    linear = moved.shape[2] - DV
    offset = later[:, :, DK:] + moved[:, :, linear:]
    return jnp.concatenate([moved[:, :, :linear], offset], axis=2)


def prefix(pair, got, direction):
    odd = lax.axis_index("seq") % 2
    front = odd == 1 if direction == 1 else odd == 0
    wide = got.astype(f32)
    low = pair.astype(bf16)
    closed = composed(jnp.where(front, pair, wide), jnp.where(front, got, low))
    distance = 2
    before = shifted(closed.astype(bf16), "seq", direction * distance)
    opened = before.astype(f32)
    while True:
        closed = composed(closed, before)
        distance = distance * 2
        last = distance * 2 >= lax.axis_size("seq")
        sent = closed[:, :, DK:] if last else closed
        before = shifted(sent.astype(bf16), "seq", direction * distance)
        opened = composed(opened, before)
        if last:
            break
    opened = opened[:, :, -DV:]
    moved = composed(wide, opened.astype(bf16))[:, :, -DV:]
    return jnp.where(front, moved, opened)


def layout(lengths, positions):
    padded = (lengths + (GROUP - 1)) // GROUP * GROUP
    seq_ends = jnp.cumsum(padded)
    begins = seq_ends - padded
    offset = positions[:, None] - begins[None, :]
    inside = (offset >= 0) & (positions[:, None] < seq_ends[None, :])
    valid_mask = jnp.any(inside & (offset < lengths[None, :]), axis=1).astype(jnp.float32)
    starts = jnp.any(offset == 0, axis=1).astype(jnp.float32)
    return (valid_mask, starts)


def dense(left, right):
    return jnp.dot(left, right, preferred_element_type=jnp.float32)


def shards(
    hidden_in,
    lengths,
    attn_gain,
    w_query,
    w_key,
    w_value,
    w_gate,
    w_alpha,
    w_beta,
    conv_query,
    conv_key,
    conv_value,
    decay_log,
    decay_bias,
    out_gain,
    w_out,
    ffn_gain,
    w_ffn_gate,
    w_ffn_up,
    w_ffn_down,
    grad_out,
):
    token_rows = hidden_in.shape[0]
    head_count = w_alpha.shape[1]
    col_width = grad_out.shape[1]
    devices = lax.axis_size("seq")
    positions = lax.axis_index("seq") * token_rows + jnp.arange(token_rows, dtype=jnp.int32)
    valid_mask, starts = layout(lengths, positions)
    keep_flags = 1.0 - starts[::GROUP]
    head_place = lax.axis_index("head")
    place = head_place[None].astype(jnp.int32)
    head_first = head_place * head_count
    col_first = head_place * col_width
    cols = lambda rows: lax.dynamic_slice_in_dim(rows, col_first, col_width, rows.ndim - 1)
    local_log = lax.dynamic_slice_in_dim(decay_log, head_first, head_count)
    local_bias = lax.dynamic_slice_in_dim(decay_bias, head_first, head_count)

    inputs32 = hidden_in.astype(f32)
    attn_scale = lax.rsqrt(jnp.mean(inputs32 * inputs32, axis=-1, keepdims=True) + epsilon_norm)
    normed = (inputs32 * attn_scale * attn_gain).astype(bf16)
    pres = [dense(normed, weight).astype(bf16) for weight in (w_query, w_key, w_value)]
    widths = [pre.shape[1] for pre in pres]
    edges = [0, widths[0], widths[0] + widths[1], sum(widths)]
    split = lambda rows: [rows[:, a:b] for a, b in zip(edges[:-1], edges[1:])]
    tail_first = token_rows - (CONV - 1)
    rims = shifted(jnp.concatenate([pre[tail_first:] for pre in pres], 1), "seq", 1)
    rims, grad_cols, normed_cols = tied(rims, grad_out, cols(normed))
    got_grad_rows = head_gathered(partner_rows(grad_cols))
    got_normed = head_gathered(partner_rows(normed_cols))
    rims = split(jnp.pad(rims, ((HALO - (CONV - 1), 0), (0, 0))))
    w_scal = jnp.concatenate([w_alpha, w_beta], axis=1)
    scal = jnp.concatenate([dense(normed, w_scal), valid_mask[:, None]], axis=1)
    rate = jnp.stack([jnp.exp(local_log), local_bias])
    convs = [conv_query, conv_key, conv_value]
    *made, linear, local, device_pair = delta_forward(
        pres, rims, convs, scal, rate, keep_flags
    )
    grad_rows = head_gathered(grad_out)
    device_pair, grad_rows = tied(device_pair, grad_rows)
    device_pair = device_pair.reshape(head_count, DK, WIDE)
    got_pair = exchanged(device_pair.astype(bf16), "seq", 1)
    entry = prefix(device_pair, got_pair, 1).astype(bf16).reshape(head_count * DK, DV)
    gate_pre = dense(normed, w_gate)
    d_inner = rows_dense(grad_rows, w_ffn_down)
    entry, d_inner, gate_pre, got_grad_rows, got_normed = tied(
        entry, d_inner, gate_pre, got_grad_rows, got_normed
    )
    gated = gated_forward(linear, local, gate_pre, entry, out_gain)
    mixed = head_scattered(plain_dense(gated, w_out, place))
    middle = cols(hidden_in).astype(f32) + mixed
    sent, normed_ffn, ffn_scale = head_gathered(middle.astype(bf16), ffn_gain)
    got_gated = exchanged(gated, "seq", 1)
    d_inner, got_gated = tied(d_inner, got_gated)
    inner_act, d_ffn_gate, d_ffn_up = ffn(normed_ffn, w_ffn_gate.T, w_ffn_up.T, d_inner)
    units = w_ffn_gate.shape[1]
    got_ffn_cols = partner_rows(cols(normed_ffn))
    inner_sent, d_ffn_gate, got_ffn_cols = tied(inner_act, d_ffn_gate, got_ffn_cols)
    got_inner = exchanged(inner_sent, "seq", 1)
    d_normed_ffn, grad_ffn_gain, ffn_dots = norm_dense(
        [(d_ffn_gate, w_ffn_gate.T), (d_ffn_up, w_ffn_up.T)], sent, ffn_scale, ffn_gain, place
    )
    ffn_dots = head_summed(ffn_dots[:, 0])[:, None] / sent.shape[1]
    d_sent_cols = ffn_scale * (
        cols(ffn_gain) * head_scattered(d_normed_ffn)
        - cols(sent).astype(f32) * ffn_scale * ffn_dots
    )
    d_middle = grad_out.astype(f32) + d_sent_cols
    got_normed_ffn = head_gathered(got_ffn_cols)
    middle_cols, got_normed_ffn = tied(d_middle.astype(bf16), got_normed_ffn)
    d_mixed = head_gathered(middle_cols)
    d_gated = dense(d_mixed, w_out.T)
    got_mixed_cols = partner_rows(middle_cols)
    d_gate_sent, got_inner, got_mixed_cols = tied(d_ffn_gate, got_inner, got_mixed_cols)
    got_d_gate = exchanged(d_gate_sent, "seq", 1)
    kept_down = pair_grad(grad_rows, got_grad_rows, inner_act, got_inner, True, units)
    grad_w_ffn_down = seq_scattered(kept_down)
    d_gated, kept_down = tied(d_gated, kept_down)
    d_delta, d_gate_pre, gain_part, entry_grad = gated_backward(
        linear, local, gate_pre, entry, out_gain, d_gated, valid_mask
    )
    back_pair = jnp.concatenate(
        [
            jnp.swapaxes(device_pair[:, :, :DK], 1, 2),
            entry_grad.reshape(head_count, DK, DV),
        ],
        axis=2,
    )
    back_pair, got_d_gate = tied(back_pair, got_d_gate)
    got_back = exchanged(back_pair.astype(bf16), "seq", 1)
    d_up_sent, got_mixed_cols, inner_late, got_back = tied(
        d_ffn_up, got_mixed_cols, inner_act, got_back
    )
    got_d_up = exchanged(d_up_sent, "seq", 1)
    kept_gate = pair_grad(normed_ffn, got_normed_ffn, d_ffn_gate, got_d_gate, True, units)
    got_d_mixed = head_gathered(got_mixed_cols)
    kept_out = pair_grad(d_mixed, got_d_mixed, gated, got_gated, True)
    ffn_out = head_scattered(plain_dense(inner_late, w_ffn_down, place))
    hidden_out = (middle + ffn_out).astype(bf16)
    exit_grad = prefix(back_pair, got_back, -1).reshape(head_count * DK, DV)
    exit_grad, kept_gate, kept_out, grad_w_ffn_down, hidden_out, got_d_up = tied(
        exit_grad, kept_gate, kept_out, grad_w_ffn_down, hidden_out, got_d_up
    )
    grad_w_ffn_gate = seq_scattered(kept_gate)
    grad_w_out = seq_scattered(kept_out)
    results = delta_backward(
        pres, rims, convs, scal, rate, keep_flags, made, entry, exit_grad, d_delta
    )
    d_pres, conv_parts = (results[:3], results[3:6])
    d_scal, d_rate, tails, own_back, other_back, got_tails, got_all = results[6:]
    d_scal, gate_sent, d_up_late = tied(d_scal, d_gate_pre, d_ffn_up)
    gate_middle = gate_sent.shape[1] // 2
    got_gate_low = exchanged(gate_sent[:, :gate_middle], "seq", 1)
    got_gate_high = exchanged(gate_sent[:, gate_middle:], "seq", 1)
    kept_up = pair_grad(normed_ffn, got_normed_ffn, d_up_late, got_d_up, True, units)
    grad_w_ffn_up = seq_scattered(kept_up)
    got_all = lax.dynamic_update_slice(
        got_all, (got_tails + other_back).astype(bf16), (token_rows - 8, 0)
    )
    d_query_pre, d_key_pre, d_value_pre = [
        lax.dynamic_update_slice(d_pre, tail.astype(bf16), (token_rows - 8, 0))
        for d_pre, tail in zip(d_pres, split(tails + own_back))
    ]
    kept_last = triple_grad(
        normed, got_normed, [d_query_pre, d_key_pre, d_value_pre], got_all
    )
    d_scal, kept_last, grad_w_ffn_gate, kept_up, got_gate_low = tied(
        d_scal, kept_last, grad_w_ffn_gate, kept_up, got_gate_low
    )
    gain_count = out_gain.shape[0]
    full_log, full_bias = [
        lax.dynamic_update_slice_in_dim(
            jnp.zeros(decay_log.shape, f32), d_rate[i], head_first, 0
        )
        for i in range(2)
    ]
    d_normed, grad_attn_gain, attn_dots = norm_dense(
        [
            (d_query_pre, w_query),
            (d_key_pre, w_key),
            (d_value_pre, w_value),
            (d_gate_pre, w_gate),
            (d_scal, w_scal),
        ],
        hidden_in,
        attn_scale,
        attn_gain,
        place,
    )
    d_normed, got_gate_high = tied(d_normed, got_gate_high)
    got_d_gate_pre = jnp.concatenate([got_gate_low, got_gate_high], axis=1)
    kept_w_gate = pair_grad(normed, got_normed, d_gate_pre, got_d_gate_pre, False)
    grad_w_gate = seq_scattered(kept_w_gate)
    attn_dots, kept_w_gate = tied(attn_dots, kept_w_gate)
    wide = d_normed.shape[1] // 2
    mine = d_normed[:, wide:].astype(f32) + exchanged(d_normed[:, :wide], "head", 1).astype(f32)
    across = mine[:, : wide // 2].astype(bf16)
    model = attn_gain.shape[0]
    packed_sums = head_summed(
        jnp.concatenate(
            [
                attn_dots[:, 0],
                grad_attn_gain[0],
                grad_ffn_gain[0],
                jnp.sum(gain_part, 0),
                full_log,
                full_bias,
            ]
        )
    )
    packed_sums, across = tied(packed_sums, across)
    attn_dots = packed_sums[:token_rows, None] / hidden_in.shape[1]
    small = dense(d_scal.T, normed)
    small = [jnp.swapaxes(small.reshape(2 * head_count, devices, -1), 0, 1).reshape(devices, -1)]
    for part in conv_parts:
        part = jnp.sum(part.reshape(CONV, 8, -1), axis=1).reshape(CONV, devices, -1)
        small.append(jnp.swapaxes(part, 0, 1).reshape(devices, -1))
    sums = packed_sums[token_rows + 2 * model :]
    for first in (token_rows, token_rows + model):
        small.append(packed_sums[first : first + model].reshape(devices, -1))
    small.append(jnp.broadcast_to(sums, (devices, sums.shape[0])))
    small = jnp.concatenate(small, axis=1)
    small = jnp.pad(small, ((0, 0), (0, -small.shape[1] % 2048)))
    small_width = small.shape[1]
    odd = lax.axis_index("seq") % 2
    small = small.reshape(devices // 2, 2, small_width // 128, 128)
    got = exchanged(lax.dynamic_index_in_dim(small, 1 - odd, 1, False), "seq", 1)
    small = lax.dynamic_index_in_dim(small, odd, 1, False) + got
    small = small.reshape(devices * small_width // 256, 128)
    small_sum = lax.psum_scatter(
        small,
        "seq",
        scatter_dimension=0,
        axis_index_groups=[list(range(first, devices, 2)) for first in range(2)],
        tiled=True,
    )
    kept_last, across, small, grad_w_out, kept_w_gate = tied(
        kept_last, across, small, grad_w_out, kept_w_gate
    )
    last_grads, across = line_summed(kept_last, across)
    grad_w_query, grad_w_key, grad_w_value = split(last_grads)
    small = small_sum.reshape(small_width)
    small_pieces = []
    for rows, width in [(head_count, model // devices)] * 2 + [
        (CONV, width // devices) for width in widths
    ]:
        piece = small[: rows * width].reshape(rows, width)
        small_pieces.append(piece.T if len(small_pieces) < 2 else piece)
        small = small[rows * width :]
    grad_attn_rows, grad_ffn_rows = (
        small[: model // devices],
        small[model // devices : 2 * (model // devices)],
    )
    sums = small[2 * (model // devices) :]
    grad_in = d_middle + attn_scale * (
        cols(attn_gain) * (mine[:, wide // 2 :] + across.astype(f32))
        - cols(hidden_in).astype(f32) * attn_scale * attn_dots
    )
    log_first = gain_count
    bias_first = log_first + decay_log.shape[0]
    return (
        hidden_out,
        grad_in,
        grad_attn_rows,
        grad_w_query,
        grad_w_key,
        grad_w_value,
        grad_w_gate,
        *small_pieces,
        sums[log_first:bias_first],
        sums[bias_first : bias_first + decay_bias.shape[0]],
        sums[:gain_count],
        grad_w_out,
        grad_ffn_rows,
        grad_w_ffn_gate.T,
        grad_w_ffn_up.T,
        grad_w_ffn_down,
    )


def solution(mesh):
    return jax.shard_map(
        shards,
        mesh=mesh,
        in_specs=(
            P("seq", None),
            P(),
            P(),
            P(None, "head"),
            P(None, "head"),
            P(None, "head"),
            P(None, "head"),
            P(None, "head"),
            P(None, "head"),
            P(None, "head"),
            P(None, "head"),
            P(None, "head"),
            P(),
            P(),
            P(),
            P("head", None),
            P(),
            P(None, "head"),
            P(None, "head"),
            P("head", None),
            P("seq", "head"),
        ),
        out_specs=(
            P("seq", "head"),
            P("seq", "head"),
            P("seq"),
            P("seq", "head"),
            P("seq", "head"),
            P("seq", "head"),
            P("seq", "head"),
            P("seq", "head"),
            P("seq", "head"),
            P(None, ("head", "seq")),
            P(None, ("head", "seq")),
            P(None, ("head", "seq")),
            P(),
            P(),
            P(),
            P("head", "seq"),
            P("seq"),
            P("seq", "head"),
            P("seq", "head"),
            P("head", "seq"),
        ),
        check_vma=False,
    )
```
